128 devices in a mesh: ctx: 32 (over y, x, core), shard: 4 (over z).
Axes of the slice: x: 4, y: 4, z: 4, core: 2. Of those that a mesh axis runs over, the one named last changes fastest.
Arguments:
- hidden: bfloat16 [16384, 768], P(('shard', 'ctx')), may hold values from -6 to 6
- ln1_gain: bfloat16 [768], P('shard'), may hold values from 0.5 to 1.5
- ln1_bias: bfloat16 [768], P('shard'), may hold values from -1 to 1
- ln2_gain: bfloat16 [768], P('shard'), may hold values from 0.5 to 1.5
- ln2_bias: bfloat16 [768], P('shard'), may hold values from -1 to 1
- w_qkv: bfloat16 [768, 2304], P('shard'), may hold values from -0.21875 to 0.21875
- b_qkv: bfloat16 [2304], P('shard'), may hold values from -1 to 1
- w_out: bfloat16 [768, 768], P('shard'), may hold values from -1.75 to 1.75
- b_out: bfloat16 [768], P('shard'), may hold values from -1 to 1
- w_up: bfloat16 [768, 3072], P('shard'), may hold values from -0.21875 to 0.21875
- b_up: bfloat16 [3072], P('shard'), may hold values from -1 to 1
- w_down: bfloat16 [3072, 768], P('shard'), may hold values from -0.109375 to 0.109375
- b_down: bfloat16 [768], P('shard'), may hold values from -1 to 1
- block_order: int32 [4, 64], P('shard'), may hold values from 0 to 63, as said below
- positions: int32 [4, 4096], P('shard'), may hold values from 0 to 3071, as said below
- cotangent: bfloat16 [16384, 768], P(('shard', 'ctx')), may hold values from -6 to 6
Outputs:
- output: bfloat16 [16384, 768], P(('shard', 'ctx'))
- grad_input: float32 [16384, 768], P(('shard', 'ctx'))
- grad_ln1_gain: float32 [768], P('shard')
- grad_ln1_bias: float32 [768], P('shard')
- grad_ln2_gain: float32 [768], P('shard')
- grad_ln2_bias: float32 [768], P('shard')
- grad_w_qkv: float32 [768, 2304], P('shard')
- grad_b_qkv: float32 [2304], P('shard')
- grad_w_out: float32 [768, 768], P('shard')
- grad_b_out: float32 [768], P('shard')
- grad_w_up: float32 [768, 3072], P('shard')
- grad_b_up: float32 [3072], P('shard')
- grad_w_down: float32 [3072, 768], P('shard')
- grad_b_down: float32 [768], P('shard')
The draws below stay inside these ranges and needn't reach their ends.
Inputs may be any that keep to these rules, and one draw needn't show every extreme that they name: Each row of block_order holds every number of 0 .. 63 once, and block_order[s, 2 c] + block_order[s, 2 c + 1] = 63 for every c. positions[s, t] is 0 at the first token of a document and rises by one from token to token within it; documents cover each sequence end to end.
All inputs are finite; a program needn't handle non-finite values.
Results may differ from the reference program's by a relative error of at most 0.03.
Values may be sent and summed in bfloat16 or wider, within the bound.
A program may use at most 192 MiB of HBM per device.

```python
import math
import jax
import jax.numpy as jnp
from jax import lax

D = 768
HD = 64
FF = 3072
ROT = 16
BLK = 64
NBLK = 64
LEN = 4096
SEQS = 4
TOKENS = 16384


def draw_block_order(key, part):
    key = jax.random.fold_in(key, 11)
    keys = jax.random.split(key, SEQS)

    def one_row(row_key):
        lower = jax.random.permutation(row_key, NBLK // 2).astype(jnp.int32)
        return jnp.stack([lower, NBLK - 1 - lower], axis=1).reshape(NBLK)
    return jax.vmap(one_row)(keys)


def draw_positions(key, part):
    key = jax.random.fold_in(key, 23)
    keys = jax.random.split(key, SEQS)

    def one_row(row_key):
        first = LEN - LEN // 4
        index = jnp.arange(LEN, dtype=jnp.int32)
        flags = jax.random.randint(row_key, (LEN,), 0, 32) == 0
        starts = jnp.where(flags & (index > first) | (index == first) | (index == 0), index, 0).astype(jnp.int32)
        return (index - lax.cummax(starts, axis=0)).astype(jnp.int32)
    return jax.vmap(one_row)(keys)


def block_levels(stream_key, extent, cuts, least, high):
    factor_of, own = 1.0, jax.random.fold_in(stream_key, 6)
    for dim, shards_of in cuts:
        heights = jnp.exp(jax.random.uniform(jax.random.fold_in(own, dim), (shards_of,), jnp.float32, least / len(cuts), high / len(cuts)))
        factor_of = factor_of * jnp.repeat(heights, extent[dim] // shards_of).reshape([-1 if axis == dim else 1 for axis in range(len(extent))])
    return factor_of


def gaussian(key, dims, scale, reach, cuts=(), kind=jnp.bfloat16):
    values = scale * jax.random.normal(key, dims, jnp.float32)
    if cuts:
        values = values * block_levels(key, dims, cuts, -0.22, 0.18)
    return jnp.clip(values, -reach, reach).astype(kind)


def setup_inputs(seed: int = 0) -> dict:
    key_of = jax.random.split(jax.random.key(seed), 17)
    hidden = gaussian(key_of[0], (TOKENS, D), 1.0, 6.0, ((0, 128),))
    ln1_gain = jnp.clip(1.0 + 0.1 * jax.random.normal(key_of[1], (D,), jnp.float32), 0.5, 1.5).astype(jnp.bfloat16)
    ln1_bias = gaussian(key_of[2], (D,), 0.2, 1.0, ((0, 4),))
    ln2_gain = jnp.clip(1.0 + 0.1 * jax.random.normal(key_of[3], (D,), jnp.float32), 0.5, 1.5).astype(jnp.bfloat16)
    ln2_bias = gaussian(key_of[4], (D,), 0.2, 1.0, ((0, 4),))
    w_qkv = gaussian(key_of[5], (D, 3 * D), D ** -0.5, 0.21875, ((0, 4),))
    b_qkv = gaussian(key_of[6], (3 * D,), 0.2, 1.0, ((0, 4),))
    w_out = gaussian(key_of[7], (D, D), (D // 64) ** -0.5, 1.75, ((0, 4),))
    b_out = gaussian(key_of[8], (D,), 0.2, 1.0, ((0, 4),))
    w_up = gaussian(key_of[9], (D, FF), D ** -0.5, 0.21875, ((0, 4),))
    b_up = gaussian(key_of[10], (FF,), 0.2, 1.0, ((0, 4),))
    w_down = gaussian(key_of[11], (FF, D), FF ** -0.5, 0.109375, ((0, 4),))
    b_down = gaussian(key_of[12], (D,), 0.2, 1.0, ((0, 4),))
    block_order = draw_block_order(jax.random.fold_in(key_of[16], 71), 0)
    positions = draw_positions(jax.random.fold_in(key_of[16], 71), 0)
    cotangent = gaussian(key_of[15], (TOKENS, D), 1.0, 6.0, ((0, 128),))
    return dict(hidden=hidden, ln1_gain=ln1_gain, ln1_bias=ln1_bias, ln2_gain=ln2_gain, ln2_bias=ln2_bias, w_qkv=w_qkv, b_qkv=b_qkv, w_out=w_out, b_out=b_out, w_up=w_up, b_up=b_up, w_down=w_down, b_down=b_down, block_order=block_order, positions=positions, cotangent=cotangent)


@jax.custom_vjp
def low(v):
    return lax.optimization_barrier(v.astype(jnp.bfloat16)).astype(jnp.float32)

@jax.custom_vjp
def low_back(v):
    return v

def low_keep(v):
    return (low(v), None)

def low_pass(kept, grad):
    return (grad,)

def back_keep(v):
    return (v, None)

def back_low(kept, grad):
    return (low(grad),)
low.defvjp(low_keep, low_pass)
low_back.defvjp(back_keep, back_low)

def layer_norm(values, gain, bias):
    center = values - lax.optimization_barrier(jnp.mean(values, axis=-1, keepdims=True))
    variance = lax.optimization_barrier(jnp.mean(center * center, axis=-1, keepdims=True))
    return center * lax.rsqrt(variance + 1e-05) * gain + bias

def rotate(values, cosine, sine):
    count = values.shape[0]
    heads = values.reshape(count, -1, HD)
    half = ROT // 2
    first = heads[..., :half]
    second = heads[..., half:ROT]
    cos_b = cosine[:, None, :]
    sin_b = sine[:, None, :]
    turned = jnp.concatenate([first * cos_b - second * sin_b, second * cos_b + first * sin_b, heads[..., ROT:]], axis=-1)
    return turned.reshape(count, -1)

def tables(places):
    freqs = jnp.power(10000.0, -jnp.arange(0, ROT, 2, dtype=jnp.float32) / ROT)
    angle = places.astype(jnp.float32)[:, None] * freqs[None, :]
    return (jnp.cos(angle), jnp.sin(angle))

def highest(left, right):
    return jnp.dot(left, right, precision=lax.Precision.HIGHEST)

def attention(query, key_rows, value_rows, index, start):
    length = query.shape[0]
    block = min(512, length)
    count = length // block
    scale = 1.0 / math.sqrt(HD)
    key_heads = key_rows.reshape(length, -1, HD)
    value_heads = value_rows.reshape(length, -1, HD)

    def one_block(inputs):
        query_block, index_block, start_block = inputs
        query_heads = query_block.reshape(block, -1, HD)
        scores = jnp.einsum('qhd,khd->hqk', query_heads, key_heads, precision=lax.Precision.HIGHEST) * scale
        scores = low_back(scores)
        allowed = (index[None, :] <= index_block[:, None]) & (start[None, :] == start_block[:, None])
        scores = jnp.where(allowed[None], scores, -1e+30)
        largest = lax.optimization_barrier(jnp.max(scores, axis=-1, keepdims=True))
        weights = jnp.exp(scores - largest)
        probs = low(weights / lax.optimization_barrier(jnp.sum(weights, axis=-1, keepdims=True)))
        mixed = jnp.einsum('hqk,khd->qhd', probs, value_heads, precision=lax.Precision.HIGHEST)
        return mixed.reshape(block, -1)
    result = lax.map(jax.checkpoint(one_block), (query.reshape(count, block, -1), index.reshape(count, block), start.reshape(count, block)))
    return result.reshape(length, -1)

def forward(flat_in, params, index, start, cosine, sine):
    gain_one, bias_one, gain_two, bias_two, weight_qkv, bias_qkv, weight_out, bias_out, weight_up, bias_up, weight_down, bias_down = params
    width = flat_in.shape[1]
    normed_one = low(layer_norm(flat_in, gain_one, bias_one))
    normed_two = low(layer_norm(flat_in, gain_two, bias_two))
    joined = low_back(highest(normed_one, weight_qkv) + bias_qkv)
    query = low(rotate(joined[:, :width], cosine, sine))
    key_rows = low(rotate(joined[:, width:2 * width], cosine, sine))
    value_rows = low(joined[:, 2 * width:])
    mixed = low_back(low(attention(query, key_rows, value_rows, index, start)))
    branch_attn = highest(mixed, weight_out) + bias_out
    hidden_up = low_back(highest(normed_two, weight_up) + bias_up)
    active = low(jax.nn.gelu(hidden_up, approximate=False))
    branch_mlp = highest(active, weight_down) + bias_down
    return flat_in + branch_attn + branch_mlp

def reference(hidden, ln1_gain, ln1_bias, ln2_gain, ln2_bias, w_qkv, b_qkv, w_out, b_out, w_up, b_up, w_down, b_down, block_order, positions, cotangent):
    params = tuple((item.astype(jnp.float32) for item in (ln1_gain, ln1_bias, ln2_gain, ln2_bias, w_qkv, b_qkv, w_out, b_out, w_up, b_up, w_down, b_down)))
    inputs_all = hidden.astype(jnp.float32).reshape(SEQS, LEN, D)
    cot_all = cotangent.astype(jnp.float32).reshape(SEQS, LEN, D)
    offsets = jnp.arange(BLK, dtype=jnp.int32)

    def step(totals, inputs):
        flat_in, cot, order, places = inputs
        index = (order[:, None] * BLK + offsets[None, :]).reshape(LEN).astype(jnp.int32)
        start = (index - places[index]).astype(jnp.int32)
        cosine, sine = tables(places[index])
        result, backward = jax.vjp(lambda values, weights: forward(values, weights, index, start, cosine, sine), flat_in, params)
        grad_in, grad_params = backward(cot)
        totals = jax.tree.map(lambda left, right: left + right, totals, grad_params)
        return (totals, (result.astype(jnp.bfloat16), grad_in))
    zeros = tuple((jnp.zeros_like(item) for item in params))
    grads, (results, grad_inputs) = lax.scan(step, zeros, (inputs_all, cot_all, block_order, positions))
    return (results.reshape(TOKENS, D), grad_inputs.reshape(TOKENS, D), grads[0], grads[1], grads[2], grads[3], grads[4], grads[5], grads[6], grads[7], grads[8], grads[9], grads[10], grads[11])
```

```python
import functools
import math

import jax
import jax.numpy as jnp
import numpy as np
from jax import lax
from jax.experimental import pallas as pl
from jax.experimental.pallas import tpu as pltpu
from jax.sharding import PartitionSpec as P

HD = 64
ROT = 16
D = 768
NH = 3
HC = NH * HD
CHUNK = 512
MESH = pl.DeviceIdType.MESH
BF = jnp.bfloat16
F32 = jnp.float32
LIMIT = 56 * 1024 * 1024


def vmem(count):
    return [pl.BlockSpec(memory_space=pltpu.VMEM)] * count


def spots():
    c = lax.axis_index("ctx")
    return c, lax.div(c, 8), lax.rem(lax.div(c, 2), 4), lax.rem(c, 2)


def place(y, x, k):
    return y * 8 + x * 2 + k


def send(src, dst, send_sem, recv_sem, where):
    copy = pltpu.make_async_remote_copy(
        src_ref=src,
        dst_ref=dst,
        send_sem=send_sem,
        recv_sem=recv_sem,
        device_id=where,
        device_id_type=MESH,
    )
    copy.start()
    return copy


def greet(peers):
    barrier = pltpu.get_barrier_semaphore()
    for peer in peers:
        pl.semaphore_signal(barrier, inc=1, device_id=peer, device_id_type=MESH)
    pl.semaphore_wait(barrier, len(peers))


def dma(*dims):
    return pltpu.SemaphoreType.DMA(dims)


def params(ident):
    return pltpu.CompilerParams(
        collective_id=ident, has_side_effects=True, vmem_limit_bytes=LIMIT
    )


def spread_kernel(
    hid, cot, w_qkv, wu, g1, b1, g2, b2, bo, bd, bq, meta,
    h_all, c_all, wq_all, wu_all, s_all, m_all,
    wq, small, so, ro, sp, rp, sf, rf, ss, rs,
):
    z = lax.axis_index("shard")
    c, y, x, k = spots()
    sibling = {"ctx": c + 1 - 2 * k}
    peers = [{"shard": lax.rem(z + d, 4)} for d in range(4)]
    greet(peers[1:] + [sibling])
    rows = wu.shape[0]
    half = rows // 2
    width = wu_all.shape[2]
    for p in range(4):
        wq[p] = jnp.concatenate(
            [w_qkv[:, D * t + HC * p : D * t + HC * p + HC] for t in range(3)], axis=1
        )
    small[...] = jnp.zeros_like(small)
    for i, ref in enumerate((g1, b1, g2, b2, bo, bd)):
        small[i : i + 1] = ref[...].astype(F32)
    small[6:9] = bq[...].astype(F32)

    mine = pl.ds(pl.multiple_of(k * half, 16), half)
    weights, others = {}, []
    for d in (1, 3, 2):
        p = lax.rem(z + d, 4)
        cols = pl.ds(pl.multiple_of(p * width, 128), width)
        weights[d] = [
            send(wq.at[p, mine], wq_all.at[z, mine], sp.at[0, d - 1], rp.at[0, d - 1], peers[d]),
            send(wu.at[mine, cols], wu_all.at[z, mine], sp.at[1, d - 1], rp.at[1, d - 1], peers[d]),
        ]
    cut = hid.shape[0] // 2
    parts = [pl.ds(0, cut), pl.ds(cut, cut)]
    ring = {}
    for i, (src, dst) in enumerate(((hid, h_all), (cot, c_all))):
        for n in range(2):
            ring[i, 1, n] = send(
                src.at[parts[n]], dst.at[z, parts[n]], so.at[i, 0, n], ro.at[i, 0, n], peers[1]
            )
            m = 1 - n
            ring[i, 3, m] = send(
                src.at[parts[m]], dst.at[z, parts[m]], so.at[i, 1, m], ro.at[i, 1, m], peers[3]
            )
    for d in (1, 2, 3):
        for i, (src, dst) in enumerate(((small, s_all), (meta, m_all))):
            others.append(send(src, dst.at[z], ss.at[i, d - 1], rs.at[i, d - 1], peers[d]))
    h_all[z] = hid[...]
    c_all[z] = cot[...]
    s_all[z] = small[...]
    m_all[z] = meta[...]
    wq_all[z] = wq[z]
    wu_all[z] = wu[:, pl.ds(pl.multiple_of(z * width, 128), width)]
    before, after = lax.rem(z + 3, 4), lax.rem(z + 1, 4)
    for d in (1, 3, 2):
        source = lax.rem(z + 4 - d, 4)
        for i, full in enumerate((wq_all, wu_all)):
            weights[d][i].wait_recv()
            part = full.at[source, mine]
            others.append(send(part, part, sf.at[i, d - 1], rf.at[i, d - 1], sibling))
    for i, full in enumerate((h_all, c_all)):
        ring[i, 1, 0].wait_recv()
        part = full.at[before, parts[0]]
        others.append(send(part, part, ss.at[2 + i, 0], rs.at[2 + i, 0], peers[1]))
        ring[i, 3, 1].wait_recv()
        part = full.at[after, parts[1]]
        others.append(send(part, part, ss.at[2 + i, 1], rs.at[2 + i, 1], peers[3]))
    for i in range(2):
        ring[i, 1, 1].wait_recv()
        ring[i, 3, 0].wait_recv()
    for copy in others:
        copy.wait()
    for d in (1, 3, 2):
        for copy in weights[d]:
            copy.wait_send()
    for copy in ring.values():
        copy.wait_send()


def spread(hid, cot, w_qkv, wu, vectors, meta):
    rows = hid.shape[0]
    width = wu.shape[1] // 4
    return pl.pallas_call(
        spread_kernel,
        out_shape=(
            jax.ShapeDtypeStruct((4, rows, D), BF),
            jax.ShapeDtypeStruct((4, rows, D), BF),
            jax.ShapeDtypeStruct((4, wu.shape[0], 3 * HC), BF),
            jax.ShapeDtypeStruct((4, wu.shape[0], width), BF),
            jax.ShapeDtypeStruct((4, 16, HC), F32),
            jax.ShapeDtypeStruct((4,) + meta.shape, jnp.int32),
        ),
        in_specs=vmem(12),
        out_specs=tuple(vmem(6)),
        scratch_shapes=[
            pltpu.VMEM((4, wu.shape[0], 3 * HC), BF),
            pltpu.VMEM((16, HC), F32),
            dma(2, 2, 2), dma(2, 2, 2), dma(2, 3), dma(2, 3), dma(2, 3), dma(2, 3),
            dma(4, 3), dma(4, 3),
        ],
        compiler_params=params(0),
    )(hid, cot, w_qkv, wu, *vectors, meta)


def dot(left, right):
    return jnp.dot(left, right, preferred_element_type=F32)


def dot_nt(left, right):
    return lax.dot_general(left, right, (((1,), (1,)), ((), ())), preferred_element_type=F32)


def dot_tn(left, right):
    return lax.dot_general(left, right, (((0,), (0,)), ((), ())), preferred_element_type=F32)


def normalize(flat):
    center = flat - jnp.mean(flat, axis=-1, keepdims=True)
    r = lax.rsqrt(jnp.mean(center * center, axis=-1, keepdims=True) + 1e-05)
    return center * r, r


def vector(s_all, i):
    return jnp.concatenate([s_all[p, i : i + 1] for p in range(4)], axis=1)


def turned(v, cosine, sine):
    first, second = v[0:8], v[8:16]
    return jnp.concatenate(
        [first * cosine - second * sine, second * cosine + first * sine, v[16:]], axis=0
    )


def project_kernel(h_all, c_all, wq, s_all, cs, w_out, qkvd, normed):
    z = lax.axis_index("shard")
    count = h_all.shape[1]
    xhat, _ = normalize(h_all[...].reshape(4 * count, D).astype(F32))
    n1 = (xhat * vector(s_all, 0) + vector(s_all, 1)).astype(BF)
    normed[...] = n1
    bias = []
    for t in range(3):
        piece = jnp.zeros((1, HC), F32)
        for p in range(4):
            n = 4 * t + p
            piece = piece + jnp.where(z == p, s_all[n // 3, 6 + n % 3 : 7 + n % 3], 0.0)
        bias.append(piece)
    joined = dot(n1, wq[...].reshape(D, 3 * HC)) + jnp.concatenate(bias, axis=1)
    d_mixed = dot_nt(w_out[...], c_all[...].reshape(4 * count, D)).astype(BF)
    for s in range(4):
        jt = joined[count * s : count * s + count].T
        cosine, sine = cs[s, 0:8], cs[s, 8:16]
        for h in range(NH):
            at = HD * h
            qkvd[s, at : at + HD] = turned(jt[HC + at : HC + at + HD], cosine, sine).astype(BF)
            qkvd[s, 2 * HC + at : 2 * HC + at + HD] = turned(jt[at : at + HD], cosine, sine).astype(BF)
        qkvd[s, HC : 2 * HC] = jt[2 * HC :].astype(BF)
        qkvd[s, 3 * HC :] = d_mixed[:, count * s : count * s + count]


def project(h_all, c_all, wq, s_all, cs, w_out):
    count = h_all.shape[1]
    return pl.pallas_call(
        project_kernel,
        out_shape=(
            jax.ShapeDtypeStruct((4, 4 * HC, count), BF),
            jax.ShapeDtypeStruct((4 * count, D), BF),
        ),
        in_specs=vmem(6),
        out_specs=tuple(vmem(2)),
        compiler_params=pltpu.CompilerParams(vmem_limit_bytes=LIMIT),
    )(h_all, c_all, wq, s_all, cs, w_out)


def feed_kernel(h_all, c_all, wu, w_down, s_all, b_up, zpart, g_up, g_down, small):
    count = h_all.shape[1]
    xhat, _ = normalize(h_all[...].reshape(4 * count, D).astype(F32))
    n2 = (xhat * vector(s_all, 2) + vector(s_all, 3)).astype(BF)
    up = wu[...].reshape(D, wu.shape[2])
    cot = c_all[...].reshape(4 * count, D)
    hidden = dot(n2, up) + b_up[...]
    rise = 0.5 * (1.0 + lax.erf(hidden * (1.0 / math.sqrt(2.0))))
    slope = rise + hidden * jnp.exp(-0.5 * hidden * hidden) * (1.0 / math.sqrt(2.0 * math.pi))
    active = (hidden * rise).astype(BF)
    d_up_f = (dot_nt(cot, w_down[...]) * slope).astype(BF)
    g_down[...] = dot_tn(active, cot).astype(BF)
    g_up[...] = dot_tn(n2, d_up_f).astype(BF).reshape(g_up.shape)
    branch = dot(active, w_down[...]).astype(BF)
    d_two = dot_nt(d_up_f, up)
    for s in range(4):
        zpart[s, 0] = branch[count * s : count * s + count]
        zpart[s, 1] = d_two[count * s : count * s + count].astype(BF)
    small[...] = jnp.zeros_like(small)
    small[2:3] = jnp.sum(d_two * xhat, axis=0, keepdims=True)
    small[3:4] = jnp.sum(d_two, axis=0, keepdims=True)
    small[4:5] = jnp.sum(cot.astype(F32), axis=0, keepdims=True)
    small[5:6] = jnp.sum(d_up_f.astype(F32), axis=0, keepdims=True)


def feed(h_all, c_all, wu, w_down, s_all, b_up):
    count = h_all.shape[1]
    return pl.pallas_call(
        feed_kernel,
        out_shape=(
            jax.ShapeDtypeStruct((4, 2, count, D), BF),
            jax.ShapeDtypeStruct(wu.shape, BF),
            jax.ShapeDtypeStruct(w_down.shape, BF),
            jax.ShapeDtypeStruct((8, D), F32),
        ),
        in_specs=vmem(6),
        out_specs=tuple(vmem(4)),
        compiler_params=pltpu.CompilerParams(vmem_limit_bytes=LIMIT),
    )(h_all, c_all, wu, w_down, s_all, b_up)


def gather_kernel(
    qkvd, g_up, kv_all, qd_all, u_all, sa, ra, sq, rq, sb, rb, sd, rd, sc, rc, sz, rz
):
    z = lax.axis_index("shard")
    c, y, x, k = spots()
    half = kv_all.shape[1]
    base = x * 8 + k * 4
    sibling = {"ctx": c + 1 - 2 * k}
    y_peer = [{"ctx": place(lax.rem(y + d, 4), x, k)} for d in range(4)]
    x_peer = [{"ctx": place(y, lax.rem(x + d, 4), k)} for d in (0, 1, 3)]
    z_peer = [{"shard": lax.rem(z + d, 4)} for d in range(4)]
    greet(y_peer[1:] + x_peer[1:] + z_peer[1:] + [sibling])
    first, tail = {}, []
    for d in (1, 3, 2):
        yp = lax.rem(y + d, 4)
        first[d] = send(
            qkvd.at[yp, pl.ds(0, half)], kv_all.at[base + y], sa.at[d - 1], ra.at[d - 1], y_peer[d]
        )
    for d in (1, 3, 2):
        zp = lax.rem(z + d, 4)
        tail.append(send(g_up.at[zp], u_all.at[z], sz.at[d - 1], rz.at[d - 1], z_peer[d]))
    kv_all[base + y] = qkvd[y, 0:half]
    u_all[z] = g_up[z]
    across = {}
    for d in (0, 1, 3, 2):
        ys = lax.rem(y + 4 - d, 4)
        if d:
            first[d].wait_recv()
        block = kv_all.at[base + ys]
        for e in (1, 2):
            across[d, e] = send(block, block, sb.at[d, e], rb.at[d, e], x_peer[e])
        across[d, 0] = send(block, block, sb.at[d, 0], rb.at[d, 0], sibling)
    for d in (1, 3, 2):
        yp = lax.rem(y + d, 4)
        tail.append(
            send(qkvd.at[yp, pl.ds(half, half)], qd_all.at[y], sq.at[d - 1], rq.at[d - 1], y_peer[d])
        )
    qd_all[y] = qkvd[y, half:]
    relay = {}
    for d in (0, 1, 3, 2):
        ys = lax.rem(y + 4 - d, 4)
        for e in (1, 2):
            across[d, e].wait_recv()
            block = kv_all.at[lax.rem(x + 4 - (1, 3)[e - 1], 4) * 8 + k * 4 + ys]
            if e == 1 + d // 2:
                relay[d] = send(block, block, sd.at[d], rd.at[d], x_peer[e])
            tail.append(send(block, block, sc.at[d, e], rc.at[d, e], sibling))
    for d in (0, 1, 3, 2):
        ys = lax.rem(y + 4 - d, 4)
        relay[d].wait_recv()
        block = kv_all.at[lax.rem(x + 2, 4) * 8 + k * 4 + ys]
        tail.append(send(block, block, sc.at[d, 0], rc.at[d, 0], sibling))
    for copy in tail:
        copy.wait()
    for d in range(4):
        across[d, 0].wait_recv()
        relay[d].wait_send()
        for e in range(3):
            across[d, e].wait_send()
        if d:
            first[d].wait_send()


def gather(qkvd, g_up):
    _, rows, cols = qkvd.shape
    return pl.pallas_call(
        gather_kernel,
        out_shape=(
            jax.ShapeDtypeStruct((32, rows // 2, cols), BF),
            jax.ShapeDtypeStruct((4, rows // 2, cols), BF),
            jax.ShapeDtypeStruct(g_up.shape, BF),
        ),
        in_specs=vmem(2),
        out_specs=tuple(vmem(3)),
        scratch_shapes=[
            dma(3), dma(3), dma(3), dma(3), dma(4, 3), dma(4, 3), dma(4), dma(4),
            dma(4, 3), dma(4, 3), dma(3), dma(3),
        ],
        compiler_params=params(1),
    )(qkvd, g_up)


def attention_kernel(
    nums, kv_all, qd_all, t_q, s_q, d_kv, o_q, kt, vt, dkt, dvt, qdt, oqt, s_buf, p_buf
):
    lane = lax.broadcasted_iota(jnp.int32, (2 * HC, 128), 1)
    left = lane < 64

    def pair(j):
        b0, b1 = 2 * j, 2 * j + 1
        return nums[b0], nums[b1], nums[32 + b0], nums[32 + b1]

    def sort(j, carry):
        slot0, slot1, f0, f1 = pair(j)
        one = pltpu.roll(kv_all[slot0].astype(F32), 64 * f0, 1)
        two = pltpu.roll(kv_all[slot1].astype(F32), 64 * (1 - f1), 1)
        low = jnp.where(left, one, two).astype(BF)
        high = jnp.where(left, two, one).astype(BF)
        at_low = pl.ds(pl.multiple_of(j * 128, 128), 128)
        at_high = pl.ds(pl.multiple_of((31 - j) * 128, 128), 128)
        kt[:, at_low] = low[:HC]
        vt[:, at_low] = low[HC:]
        kt[:, at_high] = high[:HC]
        vt[:, at_high] = high[HC:]
        return carry

    lax.fori_loop(0, 16, sort, 0)
    dkt[...] = jnp.zeros_like(dkt)
    dvt[...] = jnp.zeros_like(dvt)
    for g in range(2):
        one = pltpu.roll(qd_all[2 * g].astype(F32), 64 * nums[64 + 2 * g], 1)
        two = pltpu.roll(qd_all[2 * g + 1].astype(F32), 64 * nums[65 + 2 * g], 1)
        cols = slice(128 * g, 128 * g + 128)
        qdt[0, :, cols] = jnp.where(left, one, pltpu.roll(two, 64, 1))
        qdt[1, :, cols] = jnp.where(left, pltpu.roll(one, 64, 1), two)

    def one_head(tile, h):
        lo, hi = nums[68 + 2 * tile], nums[69 + 2 * tile]
        rows = slice(HD * h, HD * h + HD)
        q_t = qdt[tile, rows, :] * 0.125
        d_t = qdt[tile, HC + HD * h : HC + HD * h + HD, :]
        q_n = q_t.T.astype(BF)
        d_n = d_t.T.astype(BF)
        q_t = q_t.astype(BF)
        d_t = d_t.astype(BF)
        first = s_q[tile]
        last = t_q[tile]

        def scores(i, top):
            at = pl.ds(pl.multiple_of(i * CHUNK, CHUNK), CHUNK)
            s = dot(q_n, kt[rows, at])
            key = lax.broadcasted_iota(jnp.int32, s.shape, 1) + i * CHUNK
            s = jnp.where((key >= first) & (key <= last), s, -1e30)
            s_buf[:, at] = s
            for n in range(CHUNK // 128):
                top = jnp.maximum(top, s[:, 128 * n : 128 * n + 128])
            return top

        top = lax.fori_loop(lo, hi, scores, jnp.full((256, 128), -1e30, F32))
        top = jnp.max(top, axis=1, keepdims=True)

        def weights(i, carry):
            total, inner = carry
            at = pl.ds(pl.multiple_of(i * CHUNK, CHUNK), CHUNK)
            e = jnp.exp(s_buf[:, at] - top)
            s_buf[:, at] = e
            dp = dot(d_n, vt[rows, at])
            p_buf[:, at] = dp
            ep = e * dp
            for n in range(CHUNK // 128):
                total = total + e[:, 128 * n : 128 * n + 128]
                inner = inner + ep[:, 128 * n : 128 * n + 128]
            return total, inner

        zero = jnp.zeros((256, 128), F32)
        total, inner = lax.fori_loop(lo, hi, weights, (zero, zero))
        over = 1.0 / jnp.sum(total, axis=1, keepdims=True)
        inner = jnp.sum(inner, axis=1, keepdims=True) * over

        def products(i, carry):
            out, dq = carry
            at = pl.ds(pl.multiple_of(i * CHUNK, CHUNK), CHUNK)
            p = s_buf[:, at] * over
            pb = p.astype(BF)
            ds = (p * (p_buf[:, at] - inner)).astype(BF)
            out = out + dot_nt(pb, vt[rows, at])
            dq = dq + dot_nt(ds, kt[rows, at])
            dvt[rows, at] += dot(d_t, pb)
            dkt[rows, at] += dot(q_t, ds)
            return out, dq

        small = jnp.zeros((256, HD), F32)
        out, dq = lax.fori_loop(lo, hi, products, (small, small))
        oqt[tile, rows, :] = out.T
        oqt[tile, HC + HD * h : HC + HD * h + HD, :] = (dq * 0.125).T

    for tile in range(2):
        for h in range(NH):
            one_head(tile, h)

    for g in range(2):
        cols = slice(128 * g, 128 * g + 128)
        low, high = oqt[0, :, cols], oqt[1, :, cols]
        one = jnp.where(left, low, pltpu.roll(high, 64, 1))
        two = jnp.where(left, pltpu.roll(low, 64, 1), high)
        o_q[2 * g] = pltpu.roll(one, 64 * nums[64 + 2 * g], 1).astype(BF)
        o_q[2 * g + 1] = pltpu.roll(two, 64 * nums[65 + 2 * g], 1).astype(BF)

    half_left = left[:HC]

    def unsort(j, carry):
        slot0, slot1, f0, f1 = pair(j)
        at_low = pl.ds(pl.multiple_of(j * 128, 128), 128)
        at_high = pl.ds(pl.multiple_of((31 - j) * 128, 128), 128)
        for n, full in enumerate((dkt, dvt)):
            low, high = full[:, at_low], full[:, at_high]
            one = jnp.where(half_left, low, high)
            two = jnp.where(half_left, high, low)
            to = slice(n * HC, n * HC + HC)
            d_kv[slot0, to] = pltpu.roll(one, 64 * f0, 1).astype(BF)
            d_kv[slot1, to] = pltpu.roll(two, 64 * (1 - f1), 1).astype(BF)
        return carry

    lax.fori_loop(0, 16, unsort, 0)


def attention(nums, kv_all, qd_all, t_q, s_q):
    length = 32 * kv_all.shape[2]
    return pl.pallas_call(
        attention_kernel,
        out_shape=(
            jax.ShapeDtypeStruct(kv_all.shape, BF),
            jax.ShapeDtypeStruct(qd_all.shape, BF),
        ),
        in_specs=[pl.BlockSpec(memory_space=pltpu.SMEM)] + vmem(4),
        out_specs=tuple(vmem(2)),
        scratch_shapes=[
            pltpu.VMEM((HC, length), BF),
            pltpu.VMEM((HC, length), BF),
            pltpu.VMEM((HC, length), F32),
            pltpu.VMEM((HC, length), F32),
            pltpu.VMEM((2, 2 * HC, 256), F32),
            pltpu.VMEM((2, 2 * HC, 256), F32),
            pltpu.VMEM((256, length), F32),
            pltpu.VMEM((256, length), F32),
        ],
        compiler_params=pltpu.CompilerParams(vmem_limit_bytes=LIMIT),
    )(nums, kv_all, qd_all, t_q, s_q)


def back_kernel(
    d_kv, o_q, zpart, out, z_all, got, part, far, ready, sc, rc, sx, rx, sy, ry, sq, rq, sz, rz
):
    z = lax.axis_index("shard")
    c, y, x, k = spots()
    z_peer = [{"shard": lax.rem(z + d, 4)} for d in range(4)]
    half = d_kv.shape[1]
    sibling = {"ctx": c + 1 - 2 * k}
    y_peer = [{"ctx": place(lax.rem(y + d, 4), x, k)} for d in range(4)]
    x_peer = [{"ctx": place(y, lax.rem(x + d, 4), k)} for d in range(4)]
    greet(y_peer[1:] + x_peer[1:] + z_peer[1:] + [sibling])
    near = {}
    for e in (1, 3, 2, 0):
        xp = lax.rem(x + e, 4)
        near[e] = send(
            d_kv.at[pl.ds(xp * 8 + (1 - k) * 4, 4)], got.at[xp], sc.at[e], rc.at[e], sibling
        )
    tail = []
    for d in (1, 3, 2):
        yp = lax.rem(y + d, 4)
        tail.append(
            send(o_q.at[yp], out.at[y, pl.ds(half, half)], sq.at[d - 1], rq.at[d - 1], y_peer[d])
        )
    for d in (1, 3, 2):
        zp = lax.rem(z + d, 4)
        tail.append(send(zpart.at[zp], z_all.at[z], sz.at[d - 1], rz.at[d - 1], z_peer[d]))
    out[y, half:] = o_q[y]
    z_all[z] = zpart[z]
    across = {}
    for e in (1, 3, 2, 0):
        xp = lax.rem(x + e, 4)
        near[e].wait_recv()
        for n in range(4):
            both = d_kv[xp * 8 + k * 4 + n].astype(F32) + got[xp, n].astype(F32)
            part[xp, n] = both.astype(BF)
        if e:
            across[e] = send(part.at[xp], far.at[e - 1], sx.at[e - 1], rx.at[e - 1], x_peer[e])
    for e in (1, 3, 2):
        across[e].wait_recv()
    for d in (1, 3, 2, 0):
        yp = lax.rem(y + d, 4)
        total = part[x, yp].astype(F32)
        for e in range(3):
            total = total + far[e, yp].astype(F32)
        if d:
            ready[yp] = total.astype(BF)
            tail.append(
                send(ready.at[yp], out.at[y, pl.ds(0, half)], sy.at[d - 1], ry.at[d - 1], y_peer[d])
            )
        else:
            out[y, 0:half] = total.astype(BF)
    for copy in tail:
        copy.wait()
    for e in range(4):
        near[e].wait_send()
        if e:
            across[e].wait_send()


def back(d_kv, o_q, zpart):
    _, half, cols = d_kv.shape
    return pl.pallas_call(
        back_kernel,
        out_shape=(
            jax.ShapeDtypeStruct((4, 2 * half, cols), BF),
            jax.ShapeDtypeStruct(zpart.shape, BF),
        ),
        in_specs=vmem(3),
        out_specs=tuple(vmem(2)),
        scratch_shapes=[
            pltpu.VMEM((4, 4, half, cols), BF),
            pltpu.VMEM((4, 4, half, cols), BF),
            pltpu.VMEM((3, 4, half, cols), BF),
            pltpu.VMEM((4, half, cols), BF),
            dma(4), dma(4), dma(3), dma(3), dma(3), dma(3), dma(3), dma(3), dma(3), dma(3),
        ],
        compiler_params=params(2),
    )(d_kv, o_q, zpart)


def sum_kernel(
    pack, zpart, small, full, z_all, small_all,
    got, one, far_a, two, far_b, three, last, s1, s2, s3, s4,
    sz, rz, sc, rc, sa, ra, sb, rb, st, rt, gb, hb, ga, ha, gc, hc, sm, rm,
):
    z = lax.axis_index("shard")
    c, y, x, k = spots()
    sibling = {"ctx": c + 1 - 2 * k}
    z_peer = [{"shard": lax.rem(z + d, 4)} for d in range(4)]
    a = x + k * (y - x)
    b = y + k * (x - y)
    a_peer, b_peer = [], []
    for d in range(4):
        ax, by = lax.rem(a + d, 4), lax.rem(b + d, 4)
        a_peer.append({"ctx": place(b + k * (ax - b), ax + k * (b - ax), k)})
        b_peer.append({"ctx": place(by + k * (a - by), a + k * (by - a), k)})
    greet(a_peer[1:] + b_peer[1:] + z_peer[1:] + [sibling])
    near = {}
    for d in (1, 3, 2, 0):
        ap = lax.rem(b + d, 4)
        near[d] = send(pack.at[1 - k, ap], got.at[ap], sc.at[d], rc.at[d], sibling)
    tail = [send(small, s1, sm.at[0], rm.at[0], sibling)]
    for d in (1, 3, 2):
        zp = lax.rem(z + d, 4)
        tail.append(send(zpart.at[zp], z_all.at[z], sz.at[d - 1], rz.at[d - 1], z_peer[d]))
    z_all[z] = zpart[z]
    across = {}
    for d in (1, 3, 2, 0):
        ap = lax.rem(a + d, 4)
        near[d].wait_recv()
        for n in range(4):
            both = pack[k, ap, n].astype(F32) + got[ap, n].astype(F32)
            one[ap, n] = both.astype(BF)
        if d:
            across[d] = send(one.at[ap], far_a.at[d - 1], sa.at[d - 1], ra.at[d - 1], a_peer[d])
    tail[0].wait()
    s2[0] = small[...] + s1[...]
    small_a = [send(s2.at[0], s2.at[d], sm.at[d], rm.at[d], a_peer[d]) for d in (1, 2, 3)]
    for d in (1, 3, 2):
        across[d].wait_recv()
    beyond = {}
    for d in (1, 3, 2, 0):
        bp = lax.rem(b + d, 4)
        total = one[a, bp].astype(F32)
        for n in range(3):
            total = total + far_a[n, bp].astype(F32)
        two[bp] = total.astype(BF)
        if d:
            beyond[d] = send(two.at[bp], far_b.at[d - 1], sb.at[d - 1], rb.at[d - 1], b_peer[d])
    for copy in small_a:
        copy.wait()
    s3[0] = (s2[0] + s2[1]) + (s2[2] + s2[3])
    small_b = [send(s3.at[0], s3.at[d], sm.at[3 + d], rm.at[3 + d], b_peer[d]) for d in (1, 2, 3)]
    for d in (1, 3, 2):
        beyond[d].wait_recv()
    total = two[b].astype(F32)
    for n in range(3):
        total = total + far_b[n].astype(F32)
    three[...] = total.astype(BF)
    turned = []
    for d in (1, 3, 2):
        zp = lax.rem(z + d, 4)
        turned.append(
            send(
                three.at[pl.ds(2 * zp, 2)], last.at[pl.ds(2 * z, 2)],
                st.at[d - 1], rt.at[d - 1], z_peer[d],
            )
        )
    last[pl.ds(2 * z, 2)] = three[pl.ds(2 * z, 2)]
    last[8:] = three[8:]
    for copy in small_b:
        copy.wait()
    s4[...] = (s3[0] + s3[1]) + (s3[2] + s3[3])
    for d in (1, 3, 2):
        tail.append(send(s4, small_all.at[z], sm.at[6 + d], rm.at[6 + d], z_peer[d]))
    small_all[z] = s4[...]
    for copy in turned:
        copy.wait()
    full[k, a, b] = last[...]
    out_b = {}
    for d in (1, 3, 2):
        out_b[d] = send(last, full.at[k, a, b], gb.at[d - 1], hb.at[d - 1], b_peer[d])
    for d in (1, 3, 2):
        out_b[d].wait()
    out_a = {}
    for d in (1, 3, 2):
        out_a[d] = send(full.at[k, a], full.at[k, a], ga.at[d - 1], ha.at[d - 1], a_peer[d])
    tail.append(send(full.at[k, a], full.at[k, a], gc.at[0], hc.at[0], sibling))
    for d in (1, 3, 2):
        out_a[d].wait_recv()
        ap = lax.rem(a + 4 - d, 4)
        tail.append(send(full.at[k, ap], full.at[k, ap], gc.at[d], hc.at[d], sibling))
    for copy in tail[1:]:
        copy.wait()
    for d in (1, 2, 3):
        out_a[d].wait_send()
        across[d].wait_send()
        beyond[d].wait_send()
    for d in range(4):
        near[d].wait_send()


def sums(pack, zpart, small):
    tiles = pack.shape[3:]
    return pl.pallas_call(
        sum_kernel,
        out_shape=(
            jax.ShapeDtypeStruct(pack.shape, BF),
            jax.ShapeDtypeStruct(zpart.shape, BF),
            jax.ShapeDtypeStruct((4,) + small.shape, F32),
        ),
        in_specs=vmem(3),
        out_specs=tuple(vmem(3)),
        scratch_shapes=[
            pltpu.VMEM((4, 4) + tiles, BF),
            pltpu.VMEM((4, 4) + tiles, BF),
            pltpu.VMEM((3, 4) + tiles, BF),
            pltpu.VMEM((4,) + tiles, BF),
            pltpu.VMEM((3,) + tiles, BF),
            pltpu.VMEM(tiles, BF),
            pltpu.VMEM(tiles, BF),
            pltpu.VMEM(small.shape, F32),
            pltpu.VMEM((4,) + small.shape, F32),
            pltpu.VMEM((4,) + small.shape, F32),
            pltpu.VMEM(small.shape, F32),
            dma(3), dma(3), dma(4), dma(4), dma(3), dma(3), dma(3), dma(3), dma(3), dma(3),
            dma(3), dma(3), dma(3), dma(3), dma(4), dma(4), dma(10), dma(10),
        ],
        compiler_params=params(3),
    )(pack, zpart, small)


def after_kernel(ret, h_all, c_all, normed, wq, w_out, cs, given, zpart, pack, small, dj, mt):
    count = h_all.shape[1]
    for s in range(4):
        cosine, sine = cs[s, 0:8], -cs[s, 8:16]
        r = ret[s].astype(F32)
        rows = [turned(r[3 * HC + HD * h : 3 * HC + HD * h + HD], cosine, sine) for h in range(NH)]
        rows += [turned(r[HD * h : HD * h + HD], cosine, sine) for h in range(NH)]
        rows.append(r[HC : 2 * HC])
        dj[count * s : count * s + count] = jnp.concatenate(rows, axis=0).T.astype(BF)
        mt[:, count * s : count * s + count] = ret[s, 2 * HC : 3 * HC]
    cot = c_all[...].reshape(4 * count, D)
    xhat, _ = normalize(h_all[...].reshape(4 * count, D).astype(F32))
    d_one = dot_nt(dj[...], wq[...].reshape(D, 3 * HC))
    branch = dot(mt[...].astype(F32).T.astype(BF), w_out[...])
    for s in range(4):
        zpart[s, 0] = branch[count * s : count * s + count].astype(BF)
        zpart[s, 1] = d_one[count * s : count * s + count].astype(BF)
    small[...] = given[...]
    small[0:1] = jnp.sum(d_one * xhat, axis=0, keepdims=True)
    small[1:2] = jnp.sum(d_one, axis=0, keepdims=True)
    small[6:7, 0 : 3 * HC] = jnp.sum(dj[...].astype(F32), axis=0, keepdims=True)
    pack[24:32] = jnp.zeros((8,) + pack.shape[1:], BF)
    g = dot_tn(normed[...], dj[...])
    for p in range(4):
        mine = g[HC * p : HC * p + HC]
        for j in range(4):
            tiles = mine[:, 128 * j : 128 * j + 128].astype(BF).reshape(6, 2, 16, 128)
            pack[6 * j : 6 * j + 6, 2 * p : 2 * p + 2] = tiles
        rest = jnp.concatenate([mine[: HC // 2, 512:], mine[HC // 2 :, 512:]], axis=1)
        pack[24:27, 2 * p : 2 * p + 2] = rest.astype(BF).reshape(3, 2, 16, 128)
    g = dot(mt[...], cot)
    for j in range(6):
        tiles = g[:, 128 * j : 128 * j + 128].astype(BF).reshape(4, 3, 16, 128)
        pack[4 * j : 4 * j + 4, 8:11] = tiles


def after(ret, h_all, c_all, normed, wq, w_out, cs, given):
    count = h_all.shape[1]
    return pl.pallas_call(
        after_kernel,
        out_shape=(
            jax.ShapeDtypeStruct((4, 2, count, D), BF),
            jax.ShapeDtypeStruct((32, 11, 16, 128), BF),
            jax.ShapeDtypeStruct((8, D), F32),
        ),
        in_specs=vmem(8),
        out_specs=tuple(vmem(3)),
        scratch_shapes=[pltpu.VMEM((4 * count, 3 * HC), BF), pltpu.VMEM((HC, 4 * count), BF)],
        compiler_params=pltpu.CompilerParams(vmem_limit_bytes=LIMIT),
    )(ret, h_all, c_all, normed, wq, w_out, cs, given)


def finish_kernel(hid, cot, z_one, z_two, s_all, full, small_all, out, grad, g_qkv, g_out, vecs):
    z = lax.axis_index("shard")
    branch, d_one, d_two = 0.0, 0.0, 0.0
    for p in range(4):
        branch = branch + (z_one[p, 0].astype(F32) + z_two[p, 0].astype(F32))
        d_one = d_one + z_one[p, 1].astype(F32)
        d_two = d_two + z_two[p, 1].astype(F32)
    flat = hid[...].astype(F32)
    xhat, r = normalize(flat)
    out[...] = (flat + branch + vector(s_all, 4) + vector(s_all, 5)).astype(BF)
    g = d_one * vector(s_all, 0) + d_two * vector(s_all, 2)
    inner = jnp.mean(g * xhat, axis=-1, keepdims=True)
    grad[...] = cot[...].astype(F32) + r * (g - jnp.mean(g, axis=-1, keepdims=True) - xhat * inner)
    planes = []
    for p in range(4):
        cols = [full[6 * j : 6 * j + 6, 2 * p : 2 * p + 2].reshape(HC, 128) for j in range(4)]
        rest = full[24:27, 2 * p : 2 * p + 2].reshape(HC // 2, 128).astype(F32)
        rest = jnp.concatenate([rest[:, :64], rest[:, 64:]], axis=0)
        planes.append(jnp.concatenate([col.astype(F32) for col in cols] + [rest], axis=1))
    for t in range(3):
        g_qkv[:, D * t : D * t + D] = jnp.concatenate(
            [plane[:, HC * t : HC * t + HC] for plane in planes], axis=1
        )
    for j in range(6):
        tiles = full[4 * j : 4 * j + 4, 8:11].reshape(HC, 128)
        g_out[:, 128 * j : 128 * j + 128] = tiles.astype(F32)
    total = (small_all[0] + small_all[1]) + (small_all[2] + small_all[3])
    own = small_all[z]
    rows = jnp.concatenate([total[0:4], own[4:5]], axis=0)
    piece = jnp.zeros((5, HC), F32)
    for p in range(4):
        piece = piece + jnp.where(z == p, rows[:, HC * p : HC * p + HC], 0.0)
    vecs[...] = jnp.zeros_like(vecs)
    vecs[0:5] = piece
    for i in range(3):
        piece = jnp.zeros((1, HC), F32)
        for p in range(4):
            n = 3 * p + i
            at = HC * (n // 4)
            piece = piece + jnp.where(z == p, small_all[n % 4, 6:7, at : at + HC], 0.0)
        vecs[8 + i : 9 + i] = piece
    for i in range(4):
        vecs[11 + i : 12 + i] = own[5:6, HC * i : HC * i + HC]


def finish(hid, cot, z_one, z_two, s_all, full, small_all):
    return pl.pallas_call(
        finish_kernel,
        out_shape=(
            jax.ShapeDtypeStruct(hid.shape, BF),
            jax.ShapeDtypeStruct(hid.shape, F32),
            jax.ShapeDtypeStruct((HC, 3 * D), F32),
            jax.ShapeDtypeStruct((HC, D), F32),
            jax.ShapeDtypeStruct((16, HC), F32),
        ),
        in_specs=vmem(7),
        out_specs=tuple(vmem(5)),
        compiler_params=pltpu.CompilerParams(vmem_limit_bytes=LIMIT),
    )(hid, cot, z_one, z_two, s_all, full, small_all)


def local(
    hidden, ln1_gain, ln1_bias, ln2_gain, ln2_bias, w_qkv, b_qkv, w_out, b_out, w_up, b_up,
    w_down, b_down, block_order, positions, cotangent,
):
    rows = hidden.shape[0]
    c, y, x, k = spots()
    vectors = [v.reshape(1, HC) for v in (ln1_gain, ln1_bias, ln2_gain, ln2_bias, b_out, b_down)]
    vectors.append(b_qkv.reshape(3, HC))
    meta = jnp.concatenate(
        [positions.reshape(32, 128), jnp.pad(block_order, ((0, 7), (0, 64)))], axis=0
    )
    h_all, c_all, wq, wu, s_all, m_all = spread(hidden, cotangent, w_qkv, w_up, vectors, meta)

    places = m_all[:, :32].reshape(4, 64, 64)
    order = m_all[:, 32, :64]
    blocks = jnp.arange(64, dtype=jnp.int32)

    def pick(table, which):
        hit = which[..., None] == blocks
        return jnp.sum(jnp.where(hit[..., None], table, 0), axis=-2)

    mine = lax.dynamic_slice(order, (0, 2 * c), (4, 2))
    pos = pick(places[:, None], mine).reshape(4, 1, rows)
    freqs = jnp.power(10000.0, -jnp.arange(0, ROT, 2, dtype=F32) / ROT)
    angle = pos.astype(F32) * freqs[:, None]
    cs = jnp.concatenate([jnp.cos(angle), jnp.sin(angle)], axis=1)

    order_y = lax.dynamic_index_in_dim(order, y, axis=0, keepdims=False)
    places_y = lax.dynamic_index_in_dim(places, y, axis=0, keepdims=False)
    first = order_y.reshape(32, 2)[:, 0]
    flip = (first >= 32).astype(jnp.int32)
    low = jnp.minimum(first, 63 - first)
    slots = jnp.asarray([((i // 2) % 4) * 8 + (i % 2) * 4 + i // 8 for i in range(32)], jnp.int32)
    hit = low[None, :] == jnp.arange(32, dtype=jnp.int32)[:, None]
    slot_of = jnp.sum(jnp.where(hit, slots[None], 0), axis=1)
    flip_of = jnp.sum(jnp.where(hit, flip[None], 0), axis=1)
    low_q = lax.dynamic_index_in_dim(low.reshape(4, 8), x * 2 + k, axis=1, keepdims=False)
    flip_q = lax.dynamic_index_in_dim(flip.reshape(4, 8), x * 2 + k, axis=1, keepdims=False)
    block_q = jnp.stack([low_q, 63 - low_q])
    t_q = block_q[..., None] * 64 + blocks
    s_q = t_q - pick(places_y, block_q)
    reach = jnp.stack(
        [jnp.min(s_q, axis=(1, 2)) // CHUNK, jnp.max(t_q, axis=(1, 2)) // CHUNK + 1], axis=1
    )
    nums = jnp.concatenate([slot_of, flip_of, flip_q, reach.reshape(4)]).astype(jnp.int32)

    zpart_two, g_up, g_down, small = feed(
        h_all, c_all, wu, w_down, s_all, b_up.astype(F32).reshape(1, -1)
    )
    qkvd, normed = project(h_all, c_all, wq, s_all, cs, w_out)
    kv_all, qd_all, u_all = gather(qkvd, g_up)
    u_sum, down_sum = lax.psum((u_all, g_down), "ctx")
    d_kv, o_q = attention(nums, kv_all, qd_all, t_q.reshape(2, 256, 1), s_q.reshape(2, 256, 1))
    returned, z_two = back(d_kv, o_q, zpart_two)
    zpart_one, pack, small = after(returned, h_all, c_all, normed, wq, w_out, cs, small)
    full, z_one, small_all = sums(pack.reshape(2, 4, 4, 11, 16, 128), zpart_one, small)
    output, grad_input, grad_w_qkv, grad_w_out, vecs = finish(
        hidden, cotangent, z_one, z_two, s_all, full.reshape(32, 11, 16, 128), small_all
    )
    grad_w_up = u_sum.swapaxes(0, 1).reshape(w_up.shape).astype(F32)
    grad_w_down = down_sum.astype(F32)
    return (
        output, grad_input, vecs[0], vecs[1], vecs[2], vecs[3],
        grad_w_qkv, vecs[8:11].reshape(-1), grad_w_out, vecs[4], grad_w_up,
        vecs[11:15].reshape(-1), grad_w_down, vecs[4],
    )


def solution(mesh):
    tokens, vector, matrix = P(("shard", "ctx"), None), P("shard"), P("shard", None)
    return jax.shard_map(
        local,
        mesh=mesh,
        in_specs=(
            tokens, vector, vector, vector, vector, matrix, vector, matrix, vector, matrix, vector,
            matrix, vector, matrix, matrix, tokens,
        ),
        out_specs=(
            tokens, tokens, vector, vector, vector, vector, matrix, vector, matrix, vector, matrix,
            vector, matrix, vector,
        ),
        check_vma=False,
    )
```

```python
import functools
import math

import jax
import jax.numpy as jnp
import numpy as np
from jax import lax
from jax.experimental import pallas as pl
from jax.experimental.pallas import tpu as pltpu
from jax.sharding import PartitionSpec as P

HD = 64
ROT = 16
D = 768
NH = 3
HC = NH * HD
CHUNK = 2048
MESH = pl.DeviceIdType.MESH
BF = jnp.bfloat16
F32 = jnp.float32
LIMIT = 56 * 1024 * 1024


def vmem(count):
    return [pl.BlockSpec(memory_space=pltpu.VMEM)] * count


def spots():
    c = lax.axis_index("ctx")
    return c, lax.div(c, 8), lax.rem(lax.div(c, 2), 4), lax.rem(c, 2)


def place(y, x, k):
    return y * 8 + x * 2 + k


def send(src, dst, send_sem, recv_sem, where):
    copy = pltpu.make_async_remote_copy(
        src_ref=src,
        dst_ref=dst,
        send_sem=send_sem,
        recv_sem=recv_sem,
        device_id=where,
        device_id_type=MESH,
    )
    copy.start()
    return copy


def greet(peers):
    barrier = pltpu.get_barrier_semaphore()
    for peer in peers:
        pl.semaphore_signal(barrier, inc=1, device_id=peer, device_id_type=MESH)
    pl.semaphore_wait(barrier, len(peers))


def dma(*dims):
    return pltpu.SemaphoreType.DMA(dims)


def params(ident):
    return pltpu.CompilerParams(
        collective_id=ident, has_side_effects=True, vmem_limit_bytes=LIMIT
    )


def spread_kernel(
    hid, cot, w_qkv, wu, g1, b1, g2, b2, bo, bd, bq, pos, place_of,
    h_all, c_all, wq_all, wu_all, s_all, p_all, o_all,
    wq, small, so, ro, sp, rp, sf, rf, ss, rs,
):
    z = lax.axis_index("shard")
    c, y, x, k = spots()
    sibling = {"ctx": c + 1 - 2 * k}
    peers = [{"shard": lax.rem(z + d, 4)} for d in range(4)]
    greet(peers[1:] + [sibling])
    rows = wu.shape[0]
    half = rows // 2
    width = wu_all.shape[2]
    for p in range(4):
        wq[p] = jnp.concatenate(
            [w_qkv[:, D * t + HC * p : D * t + HC * p + HC] for t in range(3)], axis=1
        )
    small[...] = jnp.zeros_like(small)
    for i, ref in enumerate((g1, b1, g2, b2, bo, bd)):
        small[i : i + 1] = ref[...].astype(F32).reshape(1, HC)
    bias = bq[...].astype(F32).reshape(1, 3 * HC)
    for i in range(3):
        small[6 + i : 7 + i] = bias[:, HC * i : HC * i + HC]

    mine = pl.ds(pl.multiple_of(k * half, 16), half)
    weights, others = {}, []
    for d in (1, 3, 2):
        p = lax.rem(z + d, 4)
        cols = pl.ds(pl.multiple_of(p * width, 128), width)
        weights[d] = [
            send(wq.at[p, mine], wq_all.at[z, mine], sp.at[0, d - 1], rp.at[0, d - 1], peers[d]),
            send(wu.at[mine, cols], wu_all.at[z, mine], sp.at[1, d - 1], rp.at[1, d - 1], peers[d]),
        ]
    cut = hid.shape[0] // 2
    parts = [pl.ds(0, cut), pl.ds(cut, cut)]
    ring = {}
    for i, (src, dst) in enumerate(((hid, h_all), (cot, c_all))):
        for n in range(2):
            ring[i, 1, n] = send(
                src.at[parts[n]], dst.at[z, parts[n]], so.at[i, 0, n], ro.at[i, 0, n], peers[1]
            )
            m = 1 - n
            ring[i, 3, m] = send(
                src.at[parts[m]], dst.at[z, parts[m]], so.at[i, 1, m], ro.at[i, 1, m], peers[3]
            )
    for d in (1, 2, 3):
        for i, (src, dst) in enumerate(((small, s_all), (pos, p_all), (place_of, o_all))):
            others.append(send(src, dst.at[z], ss.at[i, d - 1], rs.at[i, d - 1], peers[d]))
    h_all[z] = hid[...]
    c_all[z] = cot[...]
    s_all[z] = small[...]
    p_all[z] = pos[...]
    o_all[z] = place_of[...]
    wq_all[z] = wq[z]
    wu_all[z] = wu[:, pl.ds(pl.multiple_of(z * width, 128), width)]
    before, after = lax.rem(z + 3, 4), lax.rem(z + 1, 4)
    for d in (1, 3, 2):
        source = lax.rem(z + 4 - d, 4)
        for i, full in enumerate((wq_all, wu_all)):
            weights[d][i].wait_recv()
            part = full.at[source, mine]
            others.append(send(part, part, sf.at[i, d - 1], rf.at[i, d - 1], sibling))
    for i, full in enumerate((h_all, c_all)):
        ring[i, 1, 0].wait_recv()
        part = full.at[before, parts[0]]
        others.append(send(part, part, ss.at[3 + i, 0], rs.at[3 + i, 0], peers[1]))
        ring[i, 3, 1].wait_recv()
        part = full.at[after, parts[1]]
        others.append(send(part, part, ss.at[3 + i, 1], rs.at[3 + i, 1], peers[3]))
    for i in range(2):
        ring[i, 1, 1].wait_recv()
        ring[i, 3, 0].wait_recv()
    for copy in others:
        copy.wait()
    for d in (1, 3, 2):
        for copy in weights[d]:
            copy.wait_send()
    for copy in ring.values():
        copy.wait_send()


def spread(hid, cot, w_qkv, wu, vectors, pos, place_of):
    rows = hid.shape[0]
    width = wu.shape[1] // 4
    return pl.pallas_call(
        spread_kernel,
        out_shape=(
            jax.ShapeDtypeStruct((4, rows, D), BF),
            jax.ShapeDtypeStruct((4, rows, D), BF),
            jax.ShapeDtypeStruct((4, wu.shape[0], 3 * HC), BF),
            jax.ShapeDtypeStruct((4, wu.shape[0], width), BF),
            jax.ShapeDtypeStruct((4, 16, HC), F32),
            jax.ShapeDtypeStruct((4,) + pos.shape, jnp.int32),
            jax.ShapeDtypeStruct((4,) + place_of.shape, jnp.int32),
        ),
        in_specs=vmem(13),
        out_specs=tuple(vmem(7)),
        scratch_shapes=[
            pltpu.VMEM((4, wu.shape[0], 3 * HC), BF),
            pltpu.VMEM((16, HC), F32),
            dma(2, 2, 2), dma(2, 2, 2), dma(2, 3), dma(2, 3), dma(2, 3), dma(2, 3),
            dma(5, 3), dma(5, 3),
        ],
        compiler_params=params(0),
    )(hid, cot, w_qkv, wu, *vectors, pos, place_of)


def dot(left, right):
    return jnp.dot(left, right, preferred_element_type=F32)


def dot_nt(left, right):
    return lax.dot_general(left, right, (((1,), (1,)), ((), ())), preferred_element_type=F32)


def dot_tn(left, right):
    return lax.dot_general(left, right, (((0,), (0,)), ((), ())), preferred_element_type=F32)


def normalize(flat):
    center = flat - jnp.mean(flat, axis=-1, keepdims=True)
    r = lax.rsqrt(jnp.mean(center * center, axis=-1, keepdims=True) + 1e-05)
    return center * r, r


def vector(s_all, i):
    return jnp.concatenate([s_all[p, i : i + 1] for p in range(4)], axis=1)


def swap(v, flag):
    return jnp.where(flag > 0, pltpu.roll(v, 64, 1), v)


def turned(v, cosine, sine):
    first, second = v[0:8], v[8:16]
    return jnp.concatenate(
        [first * cosine - second * sine, second * cosine + first * sine, v[16:]], axis=0
    )


def project_kernel(flips, h_all, c_all, wq, s_all, cs, w_out, qkvd, normed):
    z = lax.axis_index("shard")
    count = h_all.shape[1]
    xhat, _ = normalize(h_all[...].reshape(4 * count, D).astype(F32))
    n1 = (xhat * vector(s_all, 0) + vector(s_all, 1)).astype(BF)
    normed[...] = n1
    bias = []
    for t in range(3):
        piece = jnp.zeros((1, HC), F32)
        for p in range(4):
            n = 4 * t + p
            piece = piece + jnp.where(z == p, s_all[n // 3, 6 + n % 3 : 7 + n % 3], 0.0)
        bias.append(piece)
    joined = dot(n1, wq[...].reshape(D, 3 * HC)) + jnp.concatenate(bias, axis=1)
    d_mixed = dot_nt(w_out[...], c_all[...].reshape(4 * count, D))
    for s in range(4):
        jt = joined[count * s : count * s + count].T
        cosine, sine = cs[s, 0:8], cs[s, 8:16]
        for h in range(NH):
            at = HD * h
            rows = [
                turned(jt[HC + at : HC + at + HD], cosine, sine),
                jt[2 * HC + at : 2 * HC + at + HD],
                turned(jt[at : at + HD], cosine, sine),
                d_mixed[at : at + HD, count * s : count * s + count],
            ]
            qkvd[s, h] = swap(jnp.concatenate(rows, axis=0), flips[s]).astype(BF)


def project(flips, h_all, c_all, wq, s_all, cs, w_out):
    count = h_all.shape[1]
    return pl.pallas_call(
        project_kernel,
        out_shape=(
            jax.ShapeDtypeStruct((4, NH, 4 * HD, count), BF),
            jax.ShapeDtypeStruct((4 * count, D), BF),
        ),
        in_specs=[pl.BlockSpec(memory_space=pltpu.SMEM)] + vmem(6),
        out_specs=tuple(vmem(2)),
        compiler_params=pltpu.CompilerParams(vmem_limit_bytes=LIMIT),
    )(flips, h_all, c_all, wq, s_all, cs, w_out)


def feed_kernel(h_all, c_all, wu, w_down, s_all, b_up, zpart, g_up, g_down, small):
    count = h_all.shape[1]
    xhat, _ = normalize(h_all[...].reshape(4 * count, D).astype(F32))
    n2 = (xhat * vector(s_all, 2) + vector(s_all, 3)).astype(BF)
    up = wu[...].reshape(D, wu.shape[2])
    cot = c_all[...].reshape(4 * count, D)
    hidden = dot(n2, up) + b_up[...]
    rise = 0.5 * (1.0 + lax.erf(hidden * (1.0 / math.sqrt(2.0))))
    slope = rise + hidden * jnp.exp(-0.5 * hidden * hidden) * (1.0 / math.sqrt(2.0 * math.pi))
    active = (hidden * rise).astype(BF)
    d_up_f = (dot_nt(cot, w_down[...]) * slope).astype(BF)
    g_down[...] = dot_tn(active, cot).astype(BF)
    g_up[...] = dot_tn(n2, d_up_f).astype(BF).reshape(g_up.shape)
    branch = dot(active, w_down[...]).astype(BF)
    d_two = dot_nt(d_up_f, up)
    for s in range(4):
        zpart[s, 0] = branch[count * s : count * s + count]
        zpart[s, 1] = d_two[count * s : count * s + count].astype(BF)
    small[...] = jnp.zeros_like(small)
    small[2:3] = jnp.sum(d_two * xhat, axis=0, keepdims=True)
    small[3:4] = jnp.sum(d_two, axis=0, keepdims=True)
    small[4:5] = jnp.sum(cot.astype(F32), axis=0, keepdims=True)
    small[5:6] = jnp.sum(d_up_f.astype(F32), axis=0, keepdims=True)


def feed(h_all, c_all, wu, w_down, s_all, b_up):
    count = h_all.shape[1]
    return pl.pallas_call(
        feed_kernel,
        out_shape=(
            jax.ShapeDtypeStruct((4, 2, count, D), BF),
            jax.ShapeDtypeStruct(wu.shape, BF),
            jax.ShapeDtypeStruct(w_down.shape, BF),
            jax.ShapeDtypeStruct((8, D), F32),
        ),
        in_specs=vmem(6),
        out_specs=tuple(vmem(4)),
        compiler_params=pltpu.CompilerParams(vmem_limit_bytes=LIMIT),
    )(h_all, c_all, wu, w_down, s_all, b_up)


def attend_kernel(
    qkvd, t_k, t_q, s_q, zpart, out, z_all,
    kv0, kv1, kv2, qd, kt, dkv, qdt, oqt, s_buf, p_buf, dpart, oq, got, part, far, ready,
    s_y, r_y, s_q1, r_q1, s_x, r_x, s_r, r_r, s_f, r_f, s_n, r_n, s_a, r_a, s_b, r_b, s_o, r_o, s_z, r_z,
):
    z = lax.axis_index("shard")
    c, y, x, k = spots()
    kvs = (kv0, kv1, kv2)
    base = x * 8 + k * 4
    sibling = {"ctx": c + 1 - 2 * k}
    y_peer = [{"ctx": place(lax.rem(y + d, 4), x, k)} for d in range(4)]
    x_peer = [{"ctx": place(y, lax.rem(x + d, 4), k)} for d in range(4)]
    z_peer = [{"shard": lax.rem(z + d, 4)} for d in range(4)]
    greet(y_peer[1:] + x_peer[1:] + z_peer[1:] + [sibling])
    tail, first, across, relay, here = [], {}, {}, {}, {0: [], 1: [], 2: []}
    order = (0, 1, 3, 2)
    for h in range(NH):
        for d in order[1:]:
            yp = lax.rem(y + d, 4)
            first[h, d] = send(
                qkvd.at[yp, h, pl.ds(0, 128)], kvs[h].at[base + y],
                s_y.at[h, d - 1], r_y.at[h, d - 1], y_peer[d],
            )
            if h == 0:
                here[0].append(
                    send(
                        qkvd.at[yp, :, pl.ds(128, 128)], qd.at[y],
                        s_q1.at[d - 1], r_q1.at[d - 1], y_peer[d],
                    )
                )
        kvs[h][base + y] = qkvd[y, h, 0:128]
    qd[y] = qkvd[y, :, 128:]
    z_all[z] = zpart[z]

    def blocks_out(h):
        for d in order:
            if d:
                first[h, d].wait_recv()
            block = kvs[h].at[base + lax.rem(y + 4 - d, 4)]
            for e in (1, 3):
                across[h, d, e] = send(
                    block, block, s_x.at[h, d, e - 1], r_x.at[h, d, e - 1], x_peer[e]
                )
            here[h].append(send(block, block, s_f.at[h, d, 1], r_f.at[h, d, 1], sibling))

    def blocks_on(h):
        for d in order:
            ys = lax.rem(y + 4 - d, 4)
            for e in (1, 3):
                across[h, d, e].wait_recv()
                block = kvs[h].at[lax.rem(x + 4 - e, 4) * 8 + k * 4 + ys]
                if e == (1, 1, 3, 3)[d]:
                    relay[h, d] = send(block, block, s_r.at[h, d], r_r.at[h, d], x_peer[e])
                here[h].append(send(block, block, s_f.at[h, d, e - 1], r_f.at[h, d, e - 1], sibling))

    def blocks_last(h):
        for d in order:
            relay[h, d].wait_recv()
            block = kvs[h].at[lax.rem(x + 2, 4) * 8 + k * 4 + lax.rem(y + 4 - d, 4)]
            here[h].append(send(block, block, s_f.at[h, d, 3], r_f.at[h, d, 3], sibling))

    def blocks_here(h):
        for copy in here[h]:
            copy.wait()

    lane = lax.broadcasted_iota(jnp.int32, (128, 128), 1)
    left = lane < 64

    def sort(h):
        def step(j, carry):
            one = kvs[h][2 * j].astype(F32)
            two = pltpu.roll(kvs[h][2 * j + 1].astype(F32), 64, 1)
            kt[:, pl.ds(pl.multiple_of(j * 128, 128), 128)] = jnp.where(left, one, two).astype(BF)
            kt[:, pl.ds(pl.multiple_of((16 + j) * 128, 128), 128)] = jnp.where(left, two, one).astype(BF)
            return carry

        lax.fori_loop(0, 16, step, 0)
        dkv[...] = jnp.zeros_like(dkv)
        for g in range(2):
            one = qd[2 * g, h].astype(F32)
            two = pltpu.roll(qd[2 * g + 1, h].astype(F32), 64, 1)
            cols = slice(128 * g, 128 * g + 128)
            qdt[0, :, cols] = jnp.where(left, one, two)
            qdt[1, :, cols] = jnp.where(left, two, one)

    def unsort(h):
        def step(j, carry):
            low = dkv[:, pl.ds(pl.multiple_of(j * 128, 128), 128)]
            high = dkv[:, pl.ds(pl.multiple_of((16 + j) * 128, 128), 128)]
            dpart[h, 2 * j] = jnp.where(left, low, high).astype(BF)
            dpart[h, 2 * j + 1] = pltpu.roll(jnp.where(left, high, low), 64, 1).astype(BF)
            return carry

        lax.fori_loop(0, 16, step, 0)
        for g in range(2):
            cols = slice(128 * g, 128 * g + 128)
            low, high = oqt[0, :, cols], oqt[1, :, cols]
            oq[h, 2 * g] = jnp.where(left, low, high).astype(BF)
            oq[h, 2 * g + 1] = pltpu.roll(jnp.where(left, high, low), 64, 1).astype(BF)

    keys, values = slice(0, HD), slice(HD, 2 * HD)

    def one_tile(tile, between):
        q_t = qdt[tile, keys, :] * 0.125
        d_t = qdt[tile, values, :]
        q_n, d_n = q_t.T.astype(BF), d_t.T.astype(BF)
        q_t, d_t = q_t.astype(BF), d_t.astype(BF)
        first_key, last_key = s_q[tile], t_q[tile]
        top = jnp.full((256, 128), -1e30, F32)
        total = jnp.zeros((256, 128), F32)
        inner = jnp.zeros((256, 128), F32)
        for i in range(tile + 1):
            at = slice(i * CHUNK, i * CHUNK + CHUNK)
            s = dot(q_n, kt[keys, at])
            key = t_k[:, at]
            s = jnp.where((key >= first_key) & (key <= last_key), s, -1e30)
            s_buf[:, at] = s
            dp = dot(d_n, kt[values, at])
            p_buf[:, at] = dp
            new = top
            for n in range(CHUNK // 128):
                new = jnp.maximum(new, s[:, 128 * n : 128 * n + 128])
            scale = jnp.exp(top - new)
            total, inner, top = total * scale, inner * scale, new
            for n in range(CHUNK // 128):
                e = jnp.exp(s[:, 128 * n : 128 * n + 128] - new)
                total = total + e
                inner = inner + e * dp[:, 128 * n : 128 * n + 128]
        most = jnp.max(top, axis=1, keepdims=True)
        scale = jnp.exp(top - most)
        over = 1.0 / jnp.sum(total * scale, axis=1, keepdims=True)
        inner = jnp.sum(inner * scale, axis=1, keepdims=True) * over
        between()
        out_t = jnp.zeros((HD, 256), F32)
        dq_t = jnp.zeros((HD, 256), F32)
        for i in range(tile + 1):
            at = slice(i * CHUNK, i * CHUNK + CHUNK)
            p = jnp.exp(s_buf[:, at] - most) * over
            pb = p.astype(BF)
            ds = (p * (p_buf[:, at] - inner)).astype(BF)
            out_t = out_t + dot_nt(kt[values, at], pb)
            dq_t = dq_t + dot_nt(kt[keys, at], ds)
            dkv[values, at] += dot(d_t, pb)
            dkv[keys, at] += dot(q_t, ds)
        oqt[tile, keys, :] = out_t
        oqt[tile, values, :] = dq_t * 0.125

    near, beyond = {}, {}

    def grads_out(h):
        for e in (1, 3, 2, 0):
            xp = lax.rem(x + e, 4)
            near[h, e] = send(
                dpart.at[h, pl.ds(xp * 8 + (1 - k) * 4, 4)], got.at[h, xp],
                s_n.at[h, e], r_n.at[h, e], sibling,
            )
        for d in (1, 3, 2):
            yp = lax.rem(y + d, 4)
            tail.append(
                send(
                    oq.at[h, yp], out.at[y, h, pl.ds(128, 128)],
                    s_o.at[h, d - 1], r_o.at[h, d - 1], y_peer[d],
                )
            )
        out[y, h, 128:] = oq[h, y]

    def grads_on(h):
        for e in (1, 3, 2, 0):
            xp = lax.rem(x + e, 4)
            near[h, e].wait_recv()
            own = dpart[h, pl.ds(xp * 8 + k * 4, 4)]
            part[h, xp] = (own.astype(F32) + got[h, xp].astype(F32)).astype(BF)
            if e:
                beyond[h, e] = send(
                    part.at[h, xp], far.at[h, e - 1], s_a.at[h, e - 1], r_a.at[h, e - 1], x_peer[e]
                )

    def grads_last(h):
        for e in (1, 3, 2):
            beyond[h, e].wait_recv()
        for d in (1, 3, 2, 0):
            yp = lax.rem(y + d, 4)
            total = part[h, x, yp].astype(F32)
            for e in range(3):
                total = total + far[h, e, yp].astype(F32)
            if d:
                ready[h, yp] = total.astype(BF)
                tail.append(
                    send(
                        ready.at[h, yp], out.at[y, h, pl.ds(0, 128)],
                        s_b.at[h, d - 1], r_b.at[h, d - 1], y_peer[d],
                    )
                )
            else:
                out[y, h, 0:128] = total.astype(BF)

    def nothing():
        pass

    for h in range(NH):
        blocks_out(h)
    blocks_on(0)
    blocks_last(0)
    for d in (1, 3, 2):
        zp = lax.rem(z + d, 4)
        tail.append(send(zpart.at[zp], z_all.at[z], s_z.at[d - 1], r_z.at[d - 1], z_peer[d]))
    blocks_here(0)

    def later_keys():
        blocks_on(1)
        blocks_on(2)

    def last_keys():
        blocks_last(1)
        blocks_last(2)

    for h in range(NH):
        sort(h)
        one_tile(0, later_keys if h == 0 else functools.partial(grads_on, h - 1))
        one_tile(1, last_keys if h == 0 else functools.partial(grads_last, h - 1))
        unsort(h)
        grads_out(h)
        if h < NH - 1:
            blocks_here(h + 1)
    grads_on(NH - 1)
    grads_last(NH - 1)
    for copy in tail:
        copy.wait()
    for group in (first, across, relay, near, beyond):
        for copy in group.values():
            copy.wait_send()


def attend(qkvd, t_k, t_q, s_q, zpart):
    square = (128, 128)
    return pl.pallas_call(
        attend_kernel,
        out_shape=(
            jax.ShapeDtypeStruct(qkvd.shape, BF),
            jax.ShapeDtypeStruct(zpart.shape, BF),
        ),
        in_specs=vmem(5),
        out_specs=tuple(vmem(2)),
        scratch_shapes=[
            pltpu.VMEM((32,) + square, BF),
            pltpu.VMEM((32,) + square, BF),
            pltpu.VMEM((32,) + square, BF),
            pltpu.VMEM((4, NH) + square, BF),
            pltpu.VMEM((128, 4096), BF),
            pltpu.VMEM((128, 4096), F32),
            pltpu.VMEM((2, 128, 256), F32),
            pltpu.VMEM((2, 128, 256), F32),
            pltpu.VMEM((256, 4096), F32),
            pltpu.VMEM((256, 4096), F32),
            pltpu.VMEM((NH, 32) + square, BF),
            pltpu.VMEM((NH, 4) + square, BF),
            pltpu.VMEM((NH, 4, 4) + square, BF),
            pltpu.VMEM((NH, 4, 4) + square, BF),
            pltpu.VMEM((NH, 3, 4) + square, BF),
            pltpu.VMEM((NH, 4) + square, BF),
            dma(3, 3), dma(3, 3), dma(3), dma(3), dma(3, 4, 3), dma(3, 4, 3), dma(3, 4), dma(3, 4),
            dma(3, 4, 4), dma(3, 4, 4), dma(3, 4), dma(3, 4), dma(3, 3), dma(3, 3), dma(3, 3),
            dma(3, 3), dma(3, 3), dma(3, 3), dma(3), dma(3),
        ],
        compiler_params=params(1),
    )(qkvd, t_k, t_q, s_q, zpart)


def sum_kernel(
    pack, zpart, small, full, z_all, small_all,
    got, one, far_a, two, far_b, three, last, s1, s2, s3, s4,
    sz, rz, sc, rc, sa, ra, sb, rb, st, rt, gb, hb, ga, ha, gc, hc, sm, rm,
):
    z = lax.axis_index("shard")
    c, y, x, k = spots()
    sibling = {"ctx": c + 1 - 2 * k}
    z_peer = [{"shard": lax.rem(z + d, 4)} for d in range(4)]
    a = x + k * (y - x)
    b = y + k * (x - y)
    a_peer, b_peer = [], []
    for d in range(4):
        ax, by = lax.rem(a + d, 4), lax.rem(b + d, 4)
        a_peer.append({"ctx": place(b + k * (ax - b), ax + k * (b - ax), k)})
        b_peer.append({"ctx": place(by + k * (a - by), a + k * (by - a), k)})
    greet(a_peer[1:] + b_peer[1:] + z_peer[1:] + [sibling])
    near = {}
    for d in (1, 3, 2, 0):
        ap = lax.rem(b + d, 4)
        near[d] = send(pack.at[1 - k, ap], got.at[ap], sc.at[d], rc.at[d], sibling)
    tail = [send(small, s1, sm.at[0], rm.at[0], sibling)]
    for d in (1, 3, 2):
        zp = lax.rem(z + d, 4)
        tail.append(send(zpart.at[zp], z_all.at[z], sz.at[d - 1], rz.at[d - 1], z_peer[d]))
    z_all[z] = zpart[z]
    across = {}
    for d in (1, 3, 2, 0):
        ap = lax.rem(a + d, 4)
        near[d].wait_recv()
        for n in range(4):
            both = pack[k, ap, n].astype(F32) + got[ap, n].astype(F32)
            one[ap, n] = both.astype(BF)
        if d:
            across[d] = send(one.at[ap], far_a.at[d - 1], sa.at[d - 1], ra.at[d - 1], a_peer[d])
    tail[0].wait()
    s2[0] = small[...] + s1[...]
    small_a = [send(s2.at[0], s2.at[d], sm.at[d], rm.at[d], a_peer[d]) for d in (1, 2, 3)]
    for d in (1, 3, 2):
        across[d].wait_recv()
    beyond = {}
    for d in (1, 3, 2, 0):
        bp = lax.rem(b + d, 4)
        total = one[a, bp].astype(F32)
        for n in range(3):
            total = total + far_a[n, bp].astype(F32)
        two[bp] = total.astype(BF)
        if d:
            beyond[d] = send(two.at[bp], far_b.at[d - 1], sb.at[d - 1], rb.at[d - 1], b_peer[d])
    for copy in small_a:
        copy.wait()
    s3[0] = (s2[0] + s2[1]) + (s2[2] + s2[3])
    small_b = [send(s3.at[0], s3.at[d], sm.at[3 + d], rm.at[3 + d], b_peer[d]) for d in (1, 2, 3)]
    for d in (1, 3, 2):
        beyond[d].wait_recv()
    total = two[b].astype(F32)
    for n in range(3):
        total = total + far_b[n].astype(F32)
    three[...] = total.astype(BF)
    turned = []
    for d in (1, 3, 2):
        zp = lax.rem(z + d, 4)
        turned.append(
            send(
                three.at[pl.ds(2 * zp, 2)], last.at[pl.ds(2 * z, 2)],
                st.at[d - 1], rt.at[d - 1], z_peer[d],
            )
        )
    last[pl.ds(2 * z, 2)] = three[pl.ds(2 * z, 2)]
    last[8:] = three[8:]
    for copy in small_b:
        copy.wait()
    s4[...] = (s3[0] + s3[1]) + (s3[2] + s3[3])
    for d in (1, 3, 2):
        tail.append(send(s4, small_all.at[z], sm.at[6 + d], rm.at[6 + d], z_peer[d]))
    small_all[z] = s4[...]
    for copy in turned:
        copy.wait()
    full[k, a, b] = last[...]
    out_b = {}
    for d in (1, 3, 2):
        out_b[d] = send(last, full.at[k, a, b], gb.at[d - 1], hb.at[d - 1], b_peer[d])
    for d in (1, 3, 2):
        out_b[d].wait()
    out_a = {}
    for d in (1, 3, 2):
        out_a[d] = send(full.at[k, a], full.at[k, a], ga.at[d - 1], ha.at[d - 1], a_peer[d])
    tail.append(send(full.at[k, a], full.at[k, a], gc.at[0], hc.at[0], sibling))
    for d in (1, 3, 2):
        out_a[d].wait_recv()
        ap = lax.rem(a + 4 - d, 4)
        tail.append(send(full.at[k, ap], full.at[k, ap], gc.at[d], hc.at[d], sibling))
    for copy in tail[1:]:
        copy.wait()
    for d in (1, 2, 3):
        out_a[d].wait_send()
        across[d].wait_send()
        beyond[d].wait_send()
    for d in range(4):
        near[d].wait_send()


def sums(pack, zpart, small):
    tiles = pack.shape[3:]
    return pl.pallas_call(
        sum_kernel,
        out_shape=(
            jax.ShapeDtypeStruct(pack.shape, BF),
            jax.ShapeDtypeStruct(zpart.shape, BF),
            jax.ShapeDtypeStruct((4,) + small.shape, F32),
        ),
        in_specs=vmem(3),
        out_specs=tuple(vmem(3)),
        scratch_shapes=[
            pltpu.VMEM((4, 4) + tiles, BF),
            pltpu.VMEM((4, 4) + tiles, BF),
            pltpu.VMEM((3, 4) + tiles, BF),
            pltpu.VMEM((4,) + tiles, BF),
            pltpu.VMEM((3,) + tiles, BF),
            pltpu.VMEM(tiles, BF),
            pltpu.VMEM(tiles, BF),
            pltpu.VMEM(small.shape, F32),
            pltpu.VMEM((4,) + small.shape, F32),
            pltpu.VMEM((4,) + small.shape, F32),
            pltpu.VMEM(small.shape, F32),
            dma(3), dma(3), dma(4), dma(4), dma(3), dma(3), dma(3), dma(3), dma(3), dma(3),
            dma(3), dma(3), dma(3), dma(3), dma(4), dma(4), dma(10), dma(10),
        ],
        compiler_params=params(3),
    )(pack, zpart, small)


def after_kernel(flips, ret, h_all, c_all, normed, wq, w_out, cs, given, zpart, pack, small, dj, mt):
    count = h_all.shape[1]
    for s in range(4):
        cosine, sine = cs[s, 0:8], -cs[s, 8:16]
        r = [swap(ret[s, h].astype(F32), flips[s]) for h in range(NH)]
        rows = [turned(r[h][3 * HD :], cosine, sine) for h in range(NH)]
        rows += [turned(r[h][0:HD], cosine, sine) for h in range(NH)]
        rows += [r[h][HD : 2 * HD] for h in range(NH)]
        dj[count * s : count * s + count] = jnp.concatenate(rows, axis=0).T.astype(BF)
        for h in range(NH):
            mt[HD * h : HD * h + HD, count * s : count * s + count] = r[h][2 * HD : 3 * HD].astype(BF)
    cot = c_all[...].reshape(4 * count, D)
    xhat, _ = normalize(h_all[...].reshape(4 * count, D).astype(F32))
    d_one = dot_nt(dj[...], wq[...].reshape(D, 3 * HC))
    branch = dot(mt[...].astype(F32).T.astype(BF), w_out[...])
    for s in range(4):
        zpart[s, 0] = branch[count * s : count * s + count].astype(BF)
        zpart[s, 1] = d_one[count * s : count * s + count].astype(BF)
    small[...] = given[...]
    small[0:1] = jnp.sum(d_one * xhat, axis=0, keepdims=True)
    small[1:2] = jnp.sum(d_one, axis=0, keepdims=True)
    small[6:7, 0 : 3 * HC] = jnp.sum(dj[...].astype(F32), axis=0, keepdims=True)
    pack[24:32] = jnp.zeros((8,) + pack.shape[1:], BF)
    g = dot_tn(normed[...], dj[...])
    for p in range(4):
        mine = g[HC * p : HC * p + HC]
        for j in range(4):
            tiles = mine[:, 128 * j : 128 * j + 128].astype(BF).reshape(6, 2, 16, 128)
            pack[6 * j : 6 * j + 6, 2 * p : 2 * p + 2] = tiles
        rest = jnp.concatenate([mine[: HC // 2, 512:], mine[HC // 2 :, 512:]], axis=1)
        pack[24:27, 2 * p : 2 * p + 2] = rest.astype(BF).reshape(3, 2, 16, 128)
    g = dot(mt[...], cot)
    for j in range(6):
        tiles = g[:, 128 * j : 128 * j + 128].astype(BF).reshape(4, 3, 16, 128)
        pack[4 * j : 4 * j + 4, 8:11] = tiles


def after(flips, ret, h_all, c_all, normed, wq, w_out, cs, given):
    count = h_all.shape[1]
    return pl.pallas_call(
        after_kernel,
        out_shape=(
            jax.ShapeDtypeStruct((4, 2, count, D), BF),
            jax.ShapeDtypeStruct((32, 11, 16, 128), BF),
            jax.ShapeDtypeStruct((8, D), F32),
        ),
        in_specs=[pl.BlockSpec(memory_space=pltpu.SMEM)] + vmem(8),
        out_specs=tuple(vmem(3)),
        scratch_shapes=[pltpu.VMEM((4 * count, 3 * HC), BF), pltpu.VMEM((HC, 4 * count), BF)],
        compiler_params=pltpu.CompilerParams(vmem_limit_bytes=LIMIT),
    )(flips, ret, h_all, c_all, normed, wq, w_out, cs, given)


def finish_kernel(
    hid, cot, z_one, z_two, s_all, full, small_all, u0, u1, u2, u3, down,
    out, grad, g_qkv, g_out, g_up, g_down, one_g, one_b, two_g, two_b, g_bqkv, g_bout, g_bup,
):
    z = lax.axis_index("shard")
    branch, d_one, d_two = 0.0, 0.0, 0.0
    for p in range(4):
        branch = branch + (z_one[p, 0].astype(F32) + z_two[p, 0].astype(F32))
        d_one = d_one + z_one[p, 1].astype(F32)
        d_two = d_two + z_two[p, 1].astype(F32)
    flat = hid[...].astype(F32)
    xhat, r = normalize(flat)
    out[...] = (flat + branch + vector(s_all, 4) + vector(s_all, 5)).astype(BF)
    g = d_one * vector(s_all, 0) + d_two * vector(s_all, 2)
    inner = jnp.mean(g * xhat, axis=-1, keepdims=True)
    grad[...] = cot[...].astype(F32) + r * (g - jnp.mean(g, axis=-1, keepdims=True) - xhat * inner)
    planes = []
    for p in range(4):
        cols = [full[6 * j : 6 * j + 6, 2 * p : 2 * p + 2].reshape(HC, 128) for j in range(4)]
        rest = full[24:27, 2 * p : 2 * p + 2].reshape(HC // 2, 128).astype(F32)
        rest = jnp.concatenate([rest[:, :64], rest[:, 64:]], axis=0)
        planes.append(jnp.concatenate([col.astype(F32) for col in cols] + [rest], axis=1))
    for t in range(3):
        g_qkv[:, D * t : D * t + D] = jnp.concatenate(
            [plane[:, HC * t : HC * t + HC] for plane in planes], axis=1
        )
    for j in range(6):
        tiles = full[4 * j : 4 * j + 4, 8:11].reshape(HC, 128)
        g_out[:, 128 * j : 128 * j + 128] = tiles.astype(F32)
    total = (small_all[0] + small_all[1]) + (small_all[2] + small_all[3])
    own = small_all[z]
    rows = jnp.concatenate([total[0:4], own[4:5]], axis=0)
    piece = jnp.zeros((5, HC), F32)
    for p in range(4):
        piece = piece + jnp.where(z == p, rows[:, HC * p : HC * p + HC], 0.0)
    for i, ref in enumerate((one_g, one_b, two_g, two_b, g_bout)):
        ref[...] = piece[i : i + 1].reshape(HC)
    pieces = []
    for i in range(3):
        piece = jnp.zeros((1, HC), F32)
        for p in range(4):
            n = 3 * p + i
            at = HC * (n // 4)
            piece = piece + jnp.where(z == p, small_all[n % 4, 6:7, at : at + HC], 0.0)
        pieces.append(piece)
    g_bqkv[...] = jnp.concatenate(pieces, axis=1).reshape(3 * HC)
    g_bup[...] = own[5:6].reshape(g_bup.shape)
    g_down[...] = down[...].astype(F32)
    width = u0.shape[1]
    for p in range(4):
        for d, ref in enumerate((u0, u1, u2, u3)):

            @pl.when(lax.rem(z + 4 - p, 4) == d)
            def _():
                g_up[:, width * p : width * p + width] = ref[...].astype(F32)


def finish(hid, cot, z_one, z_two, s_all, full, small_all, ups, down):
    return pl.pallas_call(
        finish_kernel,
        out_shape=(
            jax.ShapeDtypeStruct(hid.shape, BF),
            jax.ShapeDtypeStruct(hid.shape, F32),
            jax.ShapeDtypeStruct((HC, 3 * D), F32),
            jax.ShapeDtypeStruct((HC, D), F32),
            jax.ShapeDtypeStruct((HC, 4 * ups[0].shape[1]), F32),
            jax.ShapeDtypeStruct(down.shape, F32),
            jax.ShapeDtypeStruct((HC,), F32),
            jax.ShapeDtypeStruct((HC,), F32),
            jax.ShapeDtypeStruct((HC,), F32),
            jax.ShapeDtypeStruct((HC,), F32),
            jax.ShapeDtypeStruct((3 * HC,), F32),
            jax.ShapeDtypeStruct((HC,), F32),
            jax.ShapeDtypeStruct((down.shape[0],), F32),
        ),
        in_specs=vmem(12),
        out_specs=tuple(vmem(13)),
        compiler_params=pltpu.CompilerParams(vmem_limit_bytes=LIMIT),
    )(hid, cot, z_one, z_two, s_all, full, small_all, *ups, down)


def local(
    hidden, ln1_gain, ln1_bias, ln2_gain, ln2_bias, w_qkv, b_qkv, w_out, b_out, w_up, b_up,
    w_down, b_down, block_order, positions, cotangent,
):
    rows = hidden.shape[0]
    c, y, x, k = spots()
    vectors = (ln1_gain, ln1_bias, ln2_gain, ln2_bias, b_out, b_down, b_qkv)
    h_all, c_all, wq, wu, s_all, p_all, o_all = spread(
        hidden, cotangent, w_qkv, w_up, vectors, positions, block_order
    )

    places = p_all.reshape(4, 64, 64)
    order = o_all.reshape(4, 64)
    blocks = jnp.arange(64, dtype=jnp.int32)

    def pick(table, which):
        hit = which[..., None] == blocks
        return jnp.sum(jnp.where(hit[..., None], table, 0), axis=-2)

    mine = lax.dynamic_slice(order, (0, 2 * c), (4, 2))
    pos = pick(places[:, None], mine).reshape(4, 1, rows)
    freqs = jnp.power(10000.0, -jnp.arange(0, ROT, 2, dtype=F32) / ROT)
    angle = pos.astype(F32) * freqs[:, None]
    cs = jnp.concatenate([jnp.cos(angle), jnp.sin(angle)], axis=1)

    order_y = lax.dynamic_index_in_dim(order, y, axis=0, keepdims=False)
    places_y = lax.dynamic_index_in_dim(places, y, axis=0, keepdims=False)
    first = order_y.reshape(32, 2)[:, 0]
    low = jnp.minimum(first, 63 - first)
    low_k = low.reshape(4, 4, 2).transpose(1, 2, 0).reshape(16, 2)
    block_k = jnp.concatenate([low_k, 63 - low_k[:, ::-1]]).reshape(64, 1)
    t_k = (block_k * 64 + blocks).reshape(1, 4096)
    low_q = lax.dynamic_index_in_dim(low.reshape(4, 8), x * 2 + k, axis=1, keepdims=False)
    flips = (mine[:, 0] >= 32).astype(jnp.int32)
    block_q = jnp.stack([low_q, 63 - low_q.reshape(2, 2)[:, ::-1].reshape(4)])
    t_q = block_q[..., None] * 64 + blocks
    s_q = t_q - pick(places_y, block_q)
    zpart_two, g_up, g_down, small = feed(
        h_all, c_all, wu, w_down, s_all, b_up.astype(F32).reshape(1, -1)
    )
    z = lax.axis_index("shard")
    ups = [lax.dynamic_index_in_dim(g_up, z, keepdims=False)]
    for d in (1, 2, 3):
        goes = lax.dynamic_index_in_dim(g_up, lax.rem(z + d, 4), keepdims=False)
        ups.append(lax.ppermute(goes, "shard", [(i, (i + d) % 4) for i in range(4)]))
    qkvd, normed = project(flips, h_all, c_all, wq, s_all, cs, w_out)
    *ups, down = lax.psum((*ups, g_down), "ctx")
    returned, z_two = attend(qkvd, t_k, t_q.reshape(2, 256, 1), s_q.reshape(2, 256, 1), zpart_two)
    zpart_one, pack, small = after(flips, returned, h_all, c_all, normed, wq, w_out, cs, small)
    full, z_one, small_all = sums(pack.reshape(2, 4, 4, 11, 16, 128), zpart_one, small)
    (
        output, grad_input, grad_qkv, grad_out, grad_up, grad_down, one_g, one_b, two_g, two_b,
        grad_bqkv, grad_bout, grad_bup,
    ) = finish(
        hidden, cotangent, z_one, z_two, s_all, full.reshape(32, 11, 16, 128), small_all, ups, down
    )
    return (
        output, grad_input, one_g, one_b, two_g, two_b, grad_qkv, grad_bqkv, grad_out, grad_bout,
        grad_up, grad_bup, grad_down, grad_bout,
    )


def solution(mesh):
    tokens, vector, matrix = P(("shard", "ctx"), None), P("shard"), P("shard", None)
    return jax.shard_map(
        local,
        mesh=mesh,
        in_specs=(
            tokens, vector, vector, vector, vector, matrix, vector, matrix, vector, matrix, vector,
            matrix, vector, matrix, matrix, tokens,
        ),
        out_specs=(
            tokens, tokens, vector, vector, vector, vector, matrix, vector, matrix, vector, matrix,
            vector, matrix, vector,
        ),
        check_vma=False,
    )
```

```python
import functools
import math

import jax
import jax.numpy as jnp
import numpy as np
from jax import lax
from jax.experimental import pallas as pl
from jax.experimental.pallas import tpu as pltpu
from jax.sharding import PartitionSpec as P

HD = 64
ROT = 16
D = 768
NH = 3
HC = NH * HD
CHUNK = 2048
MESH = pl.DeviceIdType.MESH
BF = jnp.bfloat16
F32 = jnp.float32
LIMIT = 56 * 1024 * 1024


def vmem(count):
    return [pl.BlockSpec(memory_space=pltpu.VMEM)] * count


def spots():
    c = lax.axis_index("ctx")
    return c, lax.div(c, 8), lax.rem(lax.div(c, 2), 4), lax.rem(c, 2)


def place(y, x, k):
    return y * 8 + x * 2 + k


def plane(x, y, k):
    a = x + k * (y - x)
    b = y + k * (x - y)
    a_peer, b_peer = [], []
    for d in range(4):
        ax, by = lax.rem(a + d, 4), lax.rem(b + d, 4)
        a_peer.append({"ctx": place(b + k * (ax - b), ax + k * (b - ax), k)})
        b_peer.append({"ctx": place(by + k * (a - by), a + k * (by - a), k)})
    return a, b, a_peer, b_peer


def send(src, dst, send_sem, recv_sem, where):
    copy = pltpu.make_async_remote_copy(
        src_ref=src,
        dst_ref=dst,
        send_sem=send_sem,
        recv_sem=recv_sem,
        device_id=where,
        device_id_type=MESH,
    )
    copy.start()
    return copy


def greet(peers):
    barrier = pltpu.get_barrier_semaphore()
    for peer in peers:
        pl.semaphore_signal(barrier, inc=1, device_id=peer, device_id_type=MESH)
    pl.semaphore_wait(barrier, len(peers))


def dma(*dims):
    return pltpu.SemaphoreType.DMA(dims)


def params(ident):
    return pltpu.CompilerParams(
        collective_id=ident, has_side_effects=True, vmem_limit_bytes=LIMIT
    )


def spread_kernel(
    hid, cot, w_qkv, wu, g1, b1, g2, b2, bo, bd, bq, pos, place_of,
    h_all, c_all, wq_all, wu_all, s_all, p_all, o_all,
    wq, small, so, ro, sp, rp, sf, rf, ss, rs,
):
    z = lax.axis_index("shard")
    c, y, x, k = spots()
    sibling = {"ctx": c + 1 - 2 * k}
    peers = [{"shard": lax.rem(z + d, 4)} for d in range(4)]
    greet(peers[1:] + [sibling])
    rows = wu.shape[0]
    half = rows // 2
    width = wu_all.shape[2]
    for p in range(4):
        wq[p] = jnp.concatenate(
            [w_qkv[:, D * t + HC * p : D * t + HC * p + HC] for t in range(3)], axis=1
        )
    small[...] = jnp.zeros_like(small)
    for i, ref in enumerate((g1, b1, g2, b2, bo, bd)):
        small[i : i + 1] = ref[...].astype(F32).reshape(1, HC)
    bias = bq[...].astype(F32).reshape(1, 3 * HC)
    for i in range(3):
        small[6 + i : 7 + i] = bias[:, HC * i : HC * i + HC]

    mine = pl.ds(pl.multiple_of(k * half, 16), half)
    weights, others = {}, []
    for d in (1, 3, 2):
        p = lax.rem(z + d, 4)
        cols = pl.ds(pl.multiple_of(p * width, 128), width)
        weights[d] = [
            send(wq.at[p, mine], wq_all.at[z, mine], sp.at[0, d - 1], rp.at[0, d - 1], peers[d]),
            send(wu.at[mine, cols], wu_all.at[z, mine], sp.at[1, d - 1], rp.at[1, d - 1], peers[d]),
        ]
    cut = hid.shape[0] // 2
    parts = [pl.ds(0, cut), pl.ds(cut, cut)]
    ring = {}
    for i, (src, dst) in enumerate(((hid, h_all), (cot, c_all))):
        for n in range(2):
            ring[i, 1, n] = send(
                src.at[parts[n]], dst.at[z, parts[n]], so.at[i, 0, n], ro.at[i, 0, n], peers[1]
            )
            m = 1 - n
            ring[i, 3, m] = send(
                src.at[parts[m]], dst.at[z, parts[m]], so.at[i, 1, m], ro.at[i, 1, m], peers[3]
            )
    for d in (1, 2, 3):
        for i, (src, dst) in enumerate(((small, s_all), (pos, p_all), (place_of, o_all))):
            others.append(send(src, dst.at[z], ss.at[i, d - 1], rs.at[i, d - 1], peers[d]))
    h_all[z] = hid[...]
    c_all[z] = cot[...]
    s_all[z] = small[...]
    p_all[z] = pos[...]
    o_all[z] = place_of[...]
    wq_all[z] = wq[z]
    wu_all[z] = wu[:, pl.ds(pl.multiple_of(z * width, 128), width)]
    before, after = lax.rem(z + 3, 4), lax.rem(z + 1, 4)
    for d in (1, 3, 2):
        source = lax.rem(z + 4 - d, 4)
        for i, full in enumerate((wq_all, wu_all)):
            weights[d][i].wait_recv()
            part = full.at[source, mine]
            others.append(send(part, part, sf.at[i, d - 1], rf.at[i, d - 1], sibling))
    for i, full in enumerate((h_all, c_all)):
        ring[i, 1, 0].wait_recv()
        part = full.at[before, parts[0]]
        others.append(send(part, part, ss.at[3 + i, 0], rs.at[3 + i, 0], peers[1]))
        ring[i, 3, 1].wait_recv()
        part = full.at[after, parts[1]]
        others.append(send(part, part, ss.at[3 + i, 1], rs.at[3 + i, 1], peers[3]))
    for i in range(2):
        ring[i, 1, 1].wait_recv()
        ring[i, 3, 0].wait_recv()
    for copy in others:
        copy.wait()
    for d in (1, 3, 2):
        for copy in weights[d]:
            copy.wait_send()
    for copy in ring.values():
        copy.wait_send()


def spread(hid, cot, w_qkv, wu, vectors, pos, place_of):
    rows = hid.shape[0]
    width = wu.shape[1] // 4
    return pl.pallas_call(
        spread_kernel,
        out_shape=(
            jax.ShapeDtypeStruct((4, rows, D), BF),
            jax.ShapeDtypeStruct((4, rows, D), BF),
            jax.ShapeDtypeStruct((4, wu.shape[0], 3 * HC), BF),
            jax.ShapeDtypeStruct((4, wu.shape[0], width), BF),
            jax.ShapeDtypeStruct((4, 16, HC), F32),
            jax.ShapeDtypeStruct((4,) + pos.shape, jnp.int32),
            jax.ShapeDtypeStruct((4,) + place_of.shape, jnp.int32),
        ),
        in_specs=vmem(13),
        out_specs=tuple(vmem(7)),
        scratch_shapes=[
            pltpu.VMEM((4, wu.shape[0], 3 * HC), BF),
            pltpu.VMEM((16, HC), F32),
            dma(2, 2, 2), dma(2, 2, 2), dma(2, 3), dma(2, 3), dma(2, 3), dma(2, 3),
            dma(5, 3), dma(5, 3),
        ],
        compiler_params=params(0),
    )(hid, cot, w_qkv, wu, *vectors, pos, place_of)


def dot(left, right):
    return jnp.dot(left, right, preferred_element_type=F32)


def dot_nt(left, right):
    return lax.dot_general(left, right, (((1,), (1,)), ((), ())), preferred_element_type=F32)


def dot_tn(left, right):
    return lax.dot_general(left, right, (((0,), (0,)), ((), ())), preferred_element_type=F32)


def normalize(flat):
    center = flat - jnp.mean(flat, axis=-1, keepdims=True)
    r = lax.rsqrt(jnp.mean(center * center, axis=-1, keepdims=True) + 1e-05)
    return center * r, r


def vector(s_all, i):
    return jnp.concatenate([s_all[p, i : i + 1] for p in range(4)], axis=1)


def swap(v, flag):
    return jnp.where(flag > 0, pltpu.roll(v, 64, 1), v)


def turned(v, cosine, sine):
    first, second = v[0:8], v[8:16]
    return jnp.concatenate(
        [first * cosine - second * sine, second * cosine + first * sine, v[16:]], axis=0
    )


def prepare_kernel(
    flips, h_all, c_all, wq, wu, s_all, cs, w_out, w_down, b_up, qkvd, normed, zpart, pack, small
):
    z = lax.axis_index("shard")
    count = h_all.shape[1]
    xhat, _ = normalize(h_all[...].reshape(4 * count, D).astype(F32))
    cot = c_all[...].reshape(4 * count, D)
    n1 = (xhat * vector(s_all, 0) + vector(s_all, 1)).astype(BF)
    normed[...] = n1
    bias = []
    for t in range(3):
        piece = jnp.zeros((1, HC), F32)
        for p in range(4):
            n = 4 * t + p
            piece = piece + jnp.where(z == p, s_all[n // 3, 6 + n % 3 : 7 + n % 3], 0.0)
        bias.append(piece)
    joined = dot(n1, wq[...].reshape(D, 3 * HC)) + jnp.concatenate(bias, axis=1)
    d_mixed = dot_nt(w_out[...], cot)
    for s in range(4):
        jt = joined[count * s : count * s + count].T
        cosine, sine = cs[s, 0:8], cs[s, 8:16]
        for h in range(NH):
            at = HD * h
            rows = [
                turned(jt[HC + at : HC + at + HD], cosine, sine),
                jt[2 * HC + at : 2 * HC + at + HD],
                turned(jt[at : at + HD], cosine, sine),
                d_mixed[at : at + HD, count * s : count * s + count],
            ]
            qkvd[s, h] = swap(jnp.concatenate(rows, axis=0), flips[s]).astype(BF)

    n2 = (xhat * vector(s_all, 2) + vector(s_all, 3)).astype(BF)
    up = wu[...].reshape(D, wu.shape[2])
    hidden = dot(n2, up) + b_up[...].astype(F32).reshape(1, b_up.shape[0])
    rise = 0.5 * (1.0 + lax.erf(hidden * (1.0 / math.sqrt(2.0))))
    slope = rise + hidden * jnp.exp(-0.5 * hidden * hidden) * (1.0 / math.sqrt(2.0 * math.pi))
    active = (hidden * rise).astype(BF)
    d_up = (dot_nt(cot, w_down[...]) * slope).astype(BF)
    g_down = dot_tn(active, cot).astype(BF)
    for half in range(2):
        for i in range(3):
            at = 384 * half + 128 * i
            tiles = g_down[:, at : at + 128].reshape(16, 3, 16, 128)
            pack[:, half, 12 + 3 * i : 15 + 3 * i] = tiles
    g_up = dot_tn(n2, d_up).astype(BF)
    pack[12:16, :, 0:12] = jnp.zeros((4, 2, 12, 16, 128), BF)
    for p in range(4):
        for j in range(6):
            tiles = g_up[HC * p : HC * p + HC, 128 * j : 128 * j + 128].reshape(2, 2, 3, 16, 128)
            pack[2 * j : 2 * j + 2, :, 3 * p : 3 * p + 3] = tiles
    branch = dot(active, w_down[...]).astype(BF)
    d_two = dot_nt(d_up, up)
    for s in range(4):
        zpart[s, 0] = branch[count * s : count * s + count]
        zpart[s, 1] = d_two[count * s : count * s + count].astype(BF)
    small[...] = jnp.zeros_like(small)
    small[2:3] = jnp.sum(d_two * xhat, axis=0, keepdims=True)
    small[3:4] = jnp.sum(d_two, axis=0, keepdims=True)
    small[4:5] = jnp.sum(cot.astype(F32), axis=0, keepdims=True)
    small[5:6] = jnp.sum(d_up.astype(F32), axis=0, keepdims=True)


def prepare(flips, h_all, c_all, wq, wu, s_all, cs, w_out, w_down, b_up):
    count = h_all.shape[1]
    return pl.pallas_call(
        prepare_kernel,
        out_shape=(
            jax.ShapeDtypeStruct((4, NH, 4 * HD, count), BF),
            jax.ShapeDtypeStruct((4 * count, D), BF),
            jax.ShapeDtypeStruct((4, 2, count, D), BF),
            jax.ShapeDtypeStruct((16, 2, 21, 16, 128), BF),
            jax.ShapeDtypeStruct((8, D), F32),
        ),
        in_specs=[pl.BlockSpec(memory_space=pltpu.SMEM)] + vmem(9),
        out_specs=tuple(vmem(5)),
        compiler_params=pltpu.CompilerParams(vmem_limit_bytes=LIMIT),
    )(flips, h_all, c_all, wq, wu, s_all, cs, w_out, w_down, b_up)


def attend_kernel(
    qkvd, t_k, t_q, s_q, zpart, pack, out, z_all, full,
    in_a, in_b, kv_a, kv_b, kt, dkv, qdt, oqt, s_buf, p_buf, dpart, got, part, far, ready,
    w_got, w_one, w_far, w_two, w_beyond, w_three, w_last,
    s_y, r_y, s_x, r_x, s_r, r_r, s_f, r_f, s_n, r_n, s_a, r_a, s_b, r_b, s_z, r_z,
    w_sc, w_rc, w_sa, w_ra, w_sb, w_rb, w_sz, w_rz, w_gb, w_hb, w_ga, w_ha, w_gc, w_hc,
):
    z = lax.axis_index("shard")
    c, y, x, k = spots()
    base = x * 8 + k * 4
    sibling = {"ctx": c + 1 - 2 * k}
    y_peer = [{"ctx": place(lax.rem(y + d, 4), x, k)} for d in range(4)]
    x_peer = [{"ctx": place(y, lax.rem(x + d, 4), k)} for d in range(4)]
    z_peer = [{"shard": lax.rem(z + d, 4)} for d in range(4)]
    a, b, a_peer, b_peer = plane(x, y, k)
    greet(y_peer[1:] + x_peer[1:] + z_peer[1:] + [sibling])
    tail, first, across, relay, here = [], {}, {}, {}, ([], [])
    ins, kvs = (in_a, in_b), (kv_a, kv_b)
    heads = (slice(0, 1), slice(1, NH))
    for g in range(2):
        for d in (1, 3, 2):
            src = qkvd.at[lax.rem(y + d, 4), pl.ds(g, 1 + g)]
            first[g, d] = send(src, ins[g].at[y], s_y.at[g, d - 1], r_y.at[g, d - 1], y_peer[d])
        ins[g][y] = qkvd[y, heads[g]]

    def blocks_out(g):
        for d in (1, 3, 2):
            first[g, d].wait_recv()
        kvs[g][pl.ds(base, 4)] = ins[g][:, :, 0:128]
        block = kvs[g].at[pl.ds(base, 4)]
        for e in (1, 3):
            across[g, e] = send(block, block, s_x.at[g, e], r_x.at[g, e], x_peer[e])
        here[g].append(send(block, block, s_f.at[g, 0], r_f.at[g, 0], sibling))

    def blocks_on(g):
        for e in (1, 3):
            across[g, e].wait_recv()
            slot = lax.rem(x + 4 - e, 4) * 8 + k * 4
            part_of = kvs[g].at[pl.ds(slot + e - 1, 2)]
            relay[g, e] = send(part_of, part_of, s_r.at[g, e], r_r.at[g, e], x_peer[e])
            block = kvs[g].at[pl.ds(slot, 4)]
            here[g].append(send(block, block, s_f.at[g, e], r_f.at[g, e], sibling))

    def blocks_last(g):
        for e in (1, 3):
            relay[g, e].wait_recv()
        block = kvs[g].at[pl.ds(lax.rem(x + 2, 4) * 8 + k * 4, 4)]
        here[g].append(send(block, block, s_f.at[g, 2], r_f.at[g, 2], sibling))

    def blocks_here(g):
        for copy in here[g]:
            copy.wait()

    w_near, w_across, w_over, w_turn, w_out_b, w_out_a = {}, {}, {}, {}, {}, {}

    def w_core():
        for d in (1, 3, 2, 0):
            ap = lax.rem(b + d, 4)
            w_near[d] = send(pack.at[1 - k, ap], w_got.at[ap], w_sc.at[d], w_rc.at[d], sibling)

    def w_sum_core():
        for d in (1, 3, 2, 0):
            ap = lax.rem(a + d, 4)
            w_near[d].wait_recv()
            w_one[ap] = (pack[k, ap].astype(F32) + w_got[ap].astype(F32)).astype(BF)
            if d:
                w_across[d] = send(
                    w_one.at[ap], w_far.at[d - 1], w_sa.at[d - 1], w_ra.at[d - 1], a_peer[d]
                )

    def w_sum_a():
        for d in (1, 3, 2):
            w_across[d].wait_recv()
        for d in (1, 3, 2, 0):
            bp = lax.rem(b + d, 4)
            total = w_one[a, bp].astype(F32)
            for n in range(3):
                total = total + w_far[n, bp].astype(F32)
            w_two[bp] = total.astype(BF)
            if d:
                w_over[d] = send(
                    w_two.at[bp], w_beyond.at[d - 1], w_sb.at[d - 1], w_rb.at[d - 1], b_peer[d]
                )

    def w_sum_b():
        for d in (1, 3, 2):
            w_over[d].wait_recv()
        total = w_two[b].astype(F32)
        for n in range(3):
            total = total + w_beyond[n].astype(F32)
        w_three[...] = total.astype(BF)
        for d in (1, 3, 2):
            zp = lax.rem(z + d, 4)
            w_turn[d] = send(
                w_three.at[pl.ds(3 * zp, 3)], w_last.at[pl.ds(3 * z, 3)],
                w_sz.at[d - 1], w_rz.at[d - 1], z_peer[d],
            )
        w_last[pl.ds(3 * z, 3)] = w_three[pl.ds(3 * z, 3)]
        w_last[12:] = w_three[12:]

    def w_back_b():
        for d in (1, 3, 2):
            w_turn[d].wait()
        full[k, a, b] = w_last[...]
        for d in (1, 3, 2):
            w_out_b[d] = send(
                w_last, full.at[k, a, b], w_gb.at[d - 1], w_hb.at[d - 1], b_peer[d]
            )

    def w_back_a():
        for d in (1, 3, 2):
            w_out_b[d].wait()
        for d in (1, 3, 2):
            w_out_a[d] = send(
                full.at[k, a], full.at[k, a], w_ga.at[d - 1], w_ha.at[d - 1], a_peer[d]
            )
        tail.append(send(full.at[k, a], full.at[k, a], w_gc.at[0], w_hc.at[0], sibling))

    def w_back_core():
        for d in (1, 3, 2):
            w_out_a[d].wait_recv()
            ap = lax.rem(a + 4 - d, 4)
            tail.append(send(full.at[k, ap], full.at[k, ap], w_gc.at[d], w_hc.at[d], sibling))

    lane = lax.broadcasted_iota(jnp.int32, (128, 128), 1)
    left = lane < 64

    def sort(h):
        g, i = (0, 0) if h == 0 else (1, h - 1)

        def step(j, carry):
            one = kvs[g][2 * j, i].astype(F32)
            two = pltpu.roll(kvs[g][2 * j + 1, i].astype(F32), 64, 1)
            kt[:, pl.ds(pl.multiple_of(j * 128, 128), 128)] = jnp.where(left, one, two).astype(BF)
            kt[:, pl.ds(pl.multiple_of((16 + j) * 128, 128), 128)] = jnp.where(left, two, one).astype(BF)
            return carry

        lax.fori_loop(0, 16, step, 0)
        dkv[...] = jnp.zeros_like(dkv)
        for n in range(2):
            one = ins[g][2 * n, i, 128:].astype(F32)
            two = pltpu.roll(ins[g][2 * n + 1, i, 128:].astype(F32), 64, 1)
            cols = slice(128 * n, 128 * n + 128)
            qdt[0, :, cols] = jnp.where(left, one, two)
            qdt[1, :, cols] = jnp.where(left, two, one)

    def unsort(h):
        def step(j, carry):
            low = dkv[:, pl.ds(pl.multiple_of(j * 128, 128), 128)]
            high = dkv[:, pl.ds(pl.multiple_of((16 + j) * 128, 128), 128)]
            dpart[h, 2 * j] = jnp.where(left, low, high).astype(BF)
            dpart[h, 2 * j + 1] = pltpu.roll(jnp.where(left, high, low), 64, 1).astype(BF)
            return carry

        lax.fori_loop(0, 16, step, 0)
        for n in range(2):
            cols = slice(128 * n, 128 * n + 128)
            low, high = oqt[0, :, cols], oqt[1, :, cols]
            ready[h, 2 * n, 128:] = jnp.where(left, low, high).astype(BF)
            ready[h, 2 * n + 1, 128:] = pltpu.roll(jnp.where(left, high, low), 64, 1).astype(BF)

    keys, values = slice(0, HD), slice(HD, 2 * HD)

    def one_tile(tile, between):
        q_t = qdt[tile, keys, :] * 0.125
        d_t = qdt[tile, values, :]
        q_n, d_n = q_t.T.astype(BF), d_t.T.astype(BF)
        q_t, d_t = q_t.astype(BF), d_t.astype(BF)
        first_key, last_key = s_q[tile], t_q[tile]
        top = jnp.full((256, 128), -1e30, F32)
        total = jnp.zeros((256, 128), F32)
        inner = jnp.zeros((256, 128), F32)
        for i in range(tile + 1):
            at = slice(i * CHUNK, i * CHUNK + CHUNK)
            s = dot(q_n, kt[keys, at])
            key = t_k[:, at]
            s = jnp.where((key >= first_key) & (key <= last_key), s, -1e30)
            s_buf[:, at] = s
            dp = dot(d_n, kt[values, at])
            p_buf[:, at] = dp
            new = top
            for n in range(CHUNK // 128):
                new = jnp.maximum(new, s[:, 128 * n : 128 * n + 128])
            scale = jnp.exp(top - new)
            total, inner, top = total * scale, inner * scale, new
            for n in range(CHUNK // 128):
                e = jnp.exp(s[:, 128 * n : 128 * n + 128] - new)
                total = total + e
                inner = inner + e * dp[:, 128 * n : 128 * n + 128]
        most = jnp.max(top, axis=1, keepdims=True)
        scale = jnp.exp(top - most)
        over = 1.0 / jnp.sum(total * scale, axis=1, keepdims=True)
        inner = jnp.sum(inner * scale, axis=1, keepdims=True) * over
        between()
        out_t = jnp.zeros((HD, 256), F32)
        dq_t = jnp.zeros((HD, 256), F32)
        for i in range(tile + 1):
            at = slice(i * CHUNK, i * CHUNK + CHUNK)
            p = jnp.exp(s_buf[:, at] - most) * over
            pb = p.astype(BF)
            ds = (p * (p_buf[:, at] - inner)).astype(BF)
            out_t = out_t + dot_nt(kt[values, at], pb)
            dq_t = dq_t + dot_nt(kt[keys, at], ds)
            dkv[values, at] += dot(d_t, pb)
            dkv[keys, at] += dot(q_t, ds)
        oqt[tile, keys, :] = out_t
        oqt[tile, values, :] = dq_t * 0.125

    near, beyond = {}, {}

    def grads_out(h):
        for e in (1, 3, 2, 0):
            xp = lax.rem(x + e, 4)
            near[h, e] = send(
                dpart.at[h, pl.ds(xp * 8 + (1 - k) * 4, 4)], got.at[h, xp],
                s_n.at[h, e], r_n.at[h, e], sibling,
            )

    def grads_on(h):
        for e in (1, 3, 2, 0):
            xp = lax.rem(x + e, 4)
            near[h, e].wait_recv()
            own = dpart[h, pl.ds(xp * 8 + k * 4, 4)]
            part[h, xp] = (own.astype(F32) + got[h, xp].astype(F32)).astype(BF)
            if e:
                beyond[h, e] = send(
                    part.at[h, xp], far.at[h, e - 1], s_a.at[h, e - 1], r_a.at[h, e - 1], x_peer[e]
                )

    def grads_last(h):
        for e in (1, 3, 2):
            beyond[h, e].wait_recv()
        for d in (1, 3, 2, 0):
            yp = lax.rem(y + d, 4)
            total = part[h, x, yp].astype(F32)
            for e in range(3):
                total = total + far[h, e, yp].astype(F32)
            ready[h, yp, 0:128] = total.astype(BF)
            if d:
                tail.append(
                    send(
                        ready.at[h, yp], out.at[y, h], s_b.at[h, d - 1], r_b.at[h, d - 1], y_peer[d]
                    )
                )
            else:
                out[y, h] = ready[h, y]

    blocks_out(0)
    blocks_on(0)
    blocks_out(1)
    blocks_last(0)
    w_core()
    for d in (1, 3, 2):
        zp = lax.rem(z + d, 4)
        tail.append(send(zpart.at[zp], z_all.at[z], s_z.at[d - 1], r_z.at[d - 1], z_peer[d]))
    z_all[z] = zpart[z]
    blocks_here(0)

    def point_0():
        blocks_on(1)
        w_sum_core()

    def point_3():
        w_sum_b()

    def point_4():
        grads_on(1)
        w_back_a()

    def nothing():
        pass

    points = (
        (point_0, functools.partial(blocks_last, 1)),
        (functools.partial(grads_on, 0), point_3),
        (point_4, nothing),
    )
    for h in range(NH):
        sort(h)
        one_tile(0, points[h][0])
        one_tile(1, points[h][1])
        unsort(h)
        grads_out(h)
        if h == 0:
            blocks_here(1)
            w_sum_a()
        if h == 1:
            grads_last(0)
            w_back_b()
    grads_last(1)
    grads_on(2)
    w_back_core()
    grads_last(2)
    for copy in tail:
        copy.wait()
    for group in (
        first, across, relay, near, beyond, w_near, w_across, w_over, w_out_a
    ):
        for copy in group.values():
            copy.wait_send()


def attend(qkvd, t_k, t_q, s_q, zpart, pack):
    square = (128, 128)
    tiles = pack.shape[3:]
    return pl.pallas_call(
        attend_kernel,
        out_shape=(
            jax.ShapeDtypeStruct(qkvd.shape, BF),
            jax.ShapeDtypeStruct(zpart.shape, BF),
            jax.ShapeDtypeStruct(pack.shape, BF),
        ),
        in_specs=vmem(6),
        out_specs=tuple(vmem(3)),
        scratch_shapes=[
            pltpu.VMEM((4, 1, 256, 128), BF),
            pltpu.VMEM((4, 2, 256, 128), BF),
            pltpu.VMEM((32, 1) + square, BF),
            pltpu.VMEM((32, 2) + square, BF),
            pltpu.VMEM((128, 4096), BF),
            pltpu.VMEM((128, 4096), F32),
            pltpu.VMEM((2, 128, 256), F32),
            pltpu.VMEM((2, 128, 256), F32),
            pltpu.VMEM((256, 4096), F32),
            pltpu.VMEM((256, 4096), F32),
            pltpu.VMEM((NH, 32) + square, BF),
            pltpu.VMEM((NH, 4, 4) + square, BF),
            pltpu.VMEM((NH, 4, 4) + square, BF),
            pltpu.VMEM((NH, 3, 4) + square, BF),
            pltpu.VMEM((NH, 4, 256, 128), BF),
            pltpu.VMEM((4, 4) + tiles, BF),
            pltpu.VMEM((4, 4) + tiles, BF),
            pltpu.VMEM((3, 4) + tiles, BF),
            pltpu.VMEM((4,) + tiles, BF),
            pltpu.VMEM((3,) + tiles, BF),
            pltpu.VMEM(tiles, BF),
            pltpu.VMEM(tiles, BF),
            dma(2, 3), dma(2, 3), dma(2, 4), dma(2, 4), dma(2, 4), dma(2, 4), dma(2, 4), dma(2, 4),
            dma(3, 4), dma(3, 4), dma(3, 3), dma(3, 3), dma(3, 3), dma(3, 3), dma(3), dma(3),
            dma(4), dma(4), dma(3), dma(3), dma(3), dma(3), dma(3), dma(3),
            dma(3), dma(3), dma(3), dma(3), dma(4), dma(4),
        ],
        compiler_params=params(1),
    )(qkvd, t_k, t_q, s_q, zpart, pack)


def sum_kernel(
    pack, zpart, small, full, z_all, small_all,
    got, one, far_a, two, far_b, three, last, s1, s2, s3, s4,
    sz, rz, sc, rc, sa, ra, sb, rb, st, rt, gb, hb, ga, ha, gc, hc, sm, rm,
):
    z = lax.axis_index("shard")
    c, y, x, k = spots()
    sibling = {"ctx": c + 1 - 2 * k}
    z_peer = [{"shard": lax.rem(z + d, 4)} for d in range(4)]
    a, b, a_peer, b_peer = plane(x, y, k)
    greet(a_peer[1:] + b_peer[1:] + z_peer[1:] + [sibling])
    near = {}
    for d in (1, 3, 2, 0):
        ap = lax.rem(b + d, 4)
        near[d] = send(pack.at[1 - k, ap], got.at[ap], sc.at[d], rc.at[d], sibling)
    tail = [send(small, s1, sm.at[0], rm.at[0], sibling)]
    for d in (1, 3, 2):
        zp = lax.rem(z + d, 4)
        tail.append(send(zpart.at[zp], z_all.at[z], sz.at[d - 1], rz.at[d - 1], z_peer[d]))
    z_all[z] = zpart[z]
    across = {}
    for d in (1, 3, 2, 0):
        ap = lax.rem(a + d, 4)
        near[d].wait_recv()
        for n in range(4):
            both = pack[k, ap, n].astype(F32) + got[ap, n].astype(F32)
            one[ap, n] = both.astype(BF)
        if d:
            across[d] = send(one.at[ap], far_a.at[d - 1], sa.at[d - 1], ra.at[d - 1], a_peer[d])
    tail[0].wait()
    s2[0] = small[...] + s1[...]
    small_a = [send(s2.at[0], s2.at[d], sm.at[d], rm.at[d], a_peer[d]) for d in (1, 2, 3)]
    for d in (1, 3, 2):
        across[d].wait_recv()
    beyond = {}
    for d in (1, 3, 2, 0):
        bp = lax.rem(b + d, 4)
        total = one[a, bp].astype(F32)
        for n in range(3):
            total = total + far_a[n, bp].astype(F32)
        two[bp] = total.astype(BF)
        if d:
            beyond[d] = send(two.at[bp], far_b.at[d - 1], sb.at[d - 1], rb.at[d - 1], b_peer[d])
    for copy in small_a:
        copy.wait()
    s3[0] = (s2[0] + s2[1]) + (s2[2] + s2[3])
    small_b = [send(s3.at[0], s3.at[d], sm.at[3 + d], rm.at[3 + d], b_peer[d]) for d in (1, 2, 3)]
    for d in (1, 3, 2):
        beyond[d].wait_recv()
    total = two[b].astype(F32)
    for n in range(3):
        total = total + far_b[n].astype(F32)
    three[...] = total.astype(BF)
    turned = []
    for d in (1, 3, 2):
        zp = lax.rem(z + d, 4)
        turned.append(
            send(
                three.at[pl.ds(2 * zp, 2)], last.at[pl.ds(2 * z, 2)],
                st.at[d - 1], rt.at[d - 1], z_peer[d],
            )
        )
    last[pl.ds(2 * z, 2)] = three[pl.ds(2 * z, 2)]
    last[8:] = three[8:]
    for copy in small_b:
        copy.wait()
    s4[...] = (s3[0] + s3[1]) + (s3[2] + s3[3])
    for d in (1, 3, 2):
        tail.append(send(s4, small_all.at[z], sm.at[6 + d], rm.at[6 + d], z_peer[d]))
    small_all[z] = s4[...]
    for copy in turned:
        copy.wait()
    full[k, a, b] = last[...]
    out_b = {}
    for d in (1, 3, 2):
        out_b[d] = send(last, full.at[k, a, b], gb.at[d - 1], hb.at[d - 1], b_peer[d])
    for d in (1, 3, 2):
        out_b[d].wait()
    out_a = {}
    for d in (1, 3, 2):
        out_a[d] = send(full.at[k, a], full.at[k, a], ga.at[d - 1], ha.at[d - 1], a_peer[d])
    tail.append(send(full.at[k, a], full.at[k, a], gc.at[0], hc.at[0], sibling))
    for d in (1, 3, 2):
        out_a[d].wait_recv()
        ap = lax.rem(a + 4 - d, 4)
        tail.append(send(full.at[k, ap], full.at[k, ap], gc.at[d], hc.at[d], sibling))
    for copy in tail[1:]:
        copy.wait()
    for d in (1, 2, 3):
        out_a[d].wait_send()
        across[d].wait_send()
        beyond[d].wait_send()
    for d in range(4):
        near[d].wait_send()


def sums(pack, zpart, small):
    tiles = pack.shape[3:]
    return pl.pallas_call(
        sum_kernel,
        out_shape=(
            jax.ShapeDtypeStruct(pack.shape, BF),
            jax.ShapeDtypeStruct(zpart.shape, BF),
            jax.ShapeDtypeStruct((4,) + small.shape, F32),
        ),
        in_specs=vmem(3),
        out_specs=tuple(vmem(3)),
        scratch_shapes=[
            pltpu.VMEM((4, 4) + tiles, BF),
            pltpu.VMEM((4, 4) + tiles, BF),
            pltpu.VMEM((3, 4) + tiles, BF),
            pltpu.VMEM((4,) + tiles, BF),
            pltpu.VMEM((3,) + tiles, BF),
            pltpu.VMEM(tiles, BF),
            pltpu.VMEM(tiles, BF),
            pltpu.VMEM(small.shape, F32),
            pltpu.VMEM((4,) + small.shape, F32),
            pltpu.VMEM((4,) + small.shape, F32),
            pltpu.VMEM(small.shape, F32),
            dma(3), dma(3), dma(4), dma(4), dma(3), dma(3), dma(3), dma(3), dma(3), dma(3),
            dma(3), dma(3), dma(3), dma(3), dma(4), dma(4), dma(10), dma(10),
        ],
        compiler_params=params(3),
    )(pack, zpart, small)


def after_kernel(flips, ret, h_all, c_all, normed, wq, w_out, cs, given, zpart, pack, small, dj, mt):
    count = h_all.shape[1]
    for s in range(4):
        cosine, sine = cs[s, 0:8], -cs[s, 8:16]
        r = [swap(ret[s, h].astype(F32), flips[s]) for h in range(NH)]
        rows = [turned(r[h][3 * HD :], cosine, sine) for h in range(NH)]
        rows += [turned(r[h][0:HD], cosine, sine) for h in range(NH)]
        rows += [r[h][HD : 2 * HD] for h in range(NH)]
        dj[count * s : count * s + count] = jnp.concatenate(rows, axis=0).T.astype(BF)
        for h in range(NH):
            mt[HD * h : HD * h + HD, count * s : count * s + count] = r[h][2 * HD : 3 * HD].astype(BF)
    cot = c_all[...].reshape(4 * count, D)
    xhat, _ = normalize(h_all[...].reshape(4 * count, D).astype(F32))
    d_one = dot_nt(dj[...], wq[...].reshape(D, 3 * HC))
    branch = dot(mt[...].astype(F32).T.astype(BF), w_out[...])
    for s in range(4):
        zpart[s, 0] = branch[count * s : count * s + count].astype(BF)
        zpart[s, 1] = d_one[count * s : count * s + count].astype(BF)
    small[...] = given[...]
    small[0:1] = jnp.sum(d_one * xhat, axis=0, keepdims=True)
    small[1:2] = jnp.sum(d_one, axis=0, keepdims=True)
    small[6:7, 0 : 3 * HC] = jnp.sum(dj[...].astype(F32), axis=0, keepdims=True)
    pack[24:32] = jnp.zeros((8,) + pack.shape[1:], BF)
    g = dot_tn(normed[...], dj[...])
    for p in range(4):
        mine = g[HC * p : HC * p + HC]
        for j in range(4):
            tiles = mine[:, 128 * j : 128 * j + 128].astype(BF).reshape(6, 2, 16, 128)
            pack[6 * j : 6 * j + 6, 2 * p : 2 * p + 2] = tiles
        rest = jnp.concatenate([mine[: HC // 2, 512:], mine[HC // 2 :, 512:]], axis=1)
        pack[24:27, 2 * p : 2 * p + 2] = rest.astype(BF).reshape(3, 2, 16, 128)
    g = dot(mt[...], cot)
    for j in range(6):
        tiles = g[:, 128 * j : 128 * j + 128].astype(BF).reshape(4, 3, 16, 128)
        pack[4 * j : 4 * j + 4, 8:11] = tiles


def after(flips, ret, h_all, c_all, normed, wq, w_out, cs, given):
    count = h_all.shape[1]
    return pl.pallas_call(
        after_kernel,
        out_shape=(
            jax.ShapeDtypeStruct((4, 2, count, D), BF),
            jax.ShapeDtypeStruct((32, 11, 16, 128), BF),
            jax.ShapeDtypeStruct((8, D), F32),
        ),
        in_specs=[pl.BlockSpec(memory_space=pltpu.SMEM)] + vmem(8),
        out_specs=tuple(vmem(3)),
        scratch_shapes=[pltpu.VMEM((4 * count, 3 * HC), BF), pltpu.VMEM((HC, 4 * count), BF)],
        compiler_params=pltpu.CompilerParams(vmem_limit_bytes=LIMIT),
    )(flips, ret, h_all, c_all, normed, wq, w_out, cs, given)


def finish_kernel(
    hid, cot, z_one, z_two, s_all, full, small_all, feed,
    out, grad, g_qkv, g_out, g_up, g_down, one_g, one_b, two_g, two_b, g_bqkv, g_bout, g_bup,
):
    z = lax.axis_index("shard")
    branch, d_one, d_two = 0.0, 0.0, 0.0
    for p in range(4):
        branch = branch + (z_one[p, 0].astype(F32) + z_two[p, 0].astype(F32))
        d_one = d_one + z_one[p, 1].astype(F32)
        d_two = d_two + z_two[p, 1].astype(F32)
    flat = hid[...].astype(F32)
    xhat, r = normalize(flat)
    out[...] = (flat + branch + vector(s_all, 4) + vector(s_all, 5)).astype(BF)
    g = d_one * vector(s_all, 0) + d_two * vector(s_all, 2)
    inner = jnp.mean(g * xhat, axis=-1, keepdims=True)
    grad[...] = cot[...].astype(F32) + r * (g - jnp.mean(g, axis=-1, keepdims=True) - xhat * inner)
    planes = []
    for p in range(4):
        cols = [full[6 * j : 6 * j + 6, 2 * p : 2 * p + 2].reshape(HC, 128) for j in range(4)]
        rest = full[24:27, 2 * p : 2 * p + 2].reshape(HC // 2, 128).astype(F32)
        rest = jnp.concatenate([rest[:, :64], rest[:, 64:]], axis=0)
        planes.append(jnp.concatenate([col.astype(F32) for col in cols] + [rest], axis=1))
    for t in range(3):
        g_qkv[:, D * t : D * t + D] = jnp.concatenate(
            [plane[:, HC * t : HC * t + HC] for plane in planes], axis=1
        )
    for j in range(6):
        tiles = full[4 * j : 4 * j + 4, 8:11].reshape(HC, 128)
        g_out[:, 128 * j : 128 * j + 128] = tiles.astype(F32)
    total = (small_all[0] + small_all[1]) + (small_all[2] + small_all[3])
    own = small_all[z]
    rows = jnp.concatenate([total[0:4], own[4:5]], axis=0)
    piece = jnp.zeros((5, HC), F32)
    for p in range(4):
        piece = piece + jnp.where(z == p, rows[:, HC * p : HC * p + HC], 0.0)
    for i, ref in enumerate((one_g, one_b, two_g, two_b, g_bout)):
        ref[...] = piece[i : i + 1].reshape(HC)
    pieces = []
    for i in range(3):
        piece = jnp.zeros((1, HC), F32)
        for p in range(4):
            n = 3 * p + i
            at = HC * (n // 4)
            piece = piece + jnp.where(z == p, small_all[n % 4, 6:7, at : at + HC], 0.0)
        pieces.append(piece)
    g_bqkv[...] = jnp.concatenate(pieces, axis=1).reshape(3 * HC)
    g_bup[...] = own[5:6].reshape(g_bup.shape)
    for half in range(2):
        for i in range(3):
            tiles = feed[:, half, 12 + 3 * i : 15 + 3 * i].reshape(D, 128)
            at = 384 * half + 128 * i
            g_down[:, at : at + 128] = tiles.astype(F32)
    for p in range(4):
        for j in range(6):
            tiles = feed[2 * j : 2 * j + 2, :, 3 * p : 3 * p + 3].reshape(HC, 128)
            g_up[:, D * p + 128 * j : D * p + 128 * j + 128] = tiles.astype(F32)


def finish(hid, cot, z_one, z_two, s_all, full, small_all, feed):
    return pl.pallas_call(
        finish_kernel,
        out_shape=(
            jax.ShapeDtypeStruct(hid.shape, BF),
            jax.ShapeDtypeStruct(hid.shape, F32),
            jax.ShapeDtypeStruct((HC, 3 * D), F32),
            jax.ShapeDtypeStruct((HC, D), F32),
            jax.ShapeDtypeStruct((HC, 4 * D), F32),
            jax.ShapeDtypeStruct((D, D), F32),
            jax.ShapeDtypeStruct((HC,), F32),
            jax.ShapeDtypeStruct((HC,), F32),
            jax.ShapeDtypeStruct((HC,), F32),
            jax.ShapeDtypeStruct((HC,), F32),
            jax.ShapeDtypeStruct((3 * HC,), F32),
            jax.ShapeDtypeStruct((HC,), F32),
            jax.ShapeDtypeStruct((D,), F32),
        ),
        in_specs=vmem(8),
        out_specs=tuple(vmem(13)),
        compiler_params=pltpu.CompilerParams(vmem_limit_bytes=LIMIT),
    )(hid, cot, z_one, z_two, s_all, full, small_all, feed)


def local(
    hidden, ln1_gain, ln1_bias, ln2_gain, ln2_bias, w_qkv, b_qkv, w_out, b_out, w_up, b_up,
    w_down, b_down, block_order, positions, cotangent,
):
    rows = hidden.shape[0]
    c, y, x, k = spots()
    vectors = (ln1_gain, ln1_bias, ln2_gain, ln2_bias, b_out, b_down, b_qkv)
    h_all, c_all, wq, wu, s_all, p_all, o_all = spread(
        hidden, cotangent, w_qkv, w_up, vectors, positions, block_order
    )

    places = p_all.reshape(4, 64, 64)
    order = o_all.reshape(4, 64)
    blocks = jnp.arange(64, dtype=jnp.int32)

    def pick(table, which):
        hit = which[..., None] == blocks
        return jnp.sum(jnp.where(hit[..., None], table, 0), axis=-2)

    mine = lax.dynamic_slice(order, (0, 2 * c), (4, 2))
    pos = pick(places[:, None], mine).reshape(4, 1, rows)
    freqs = jnp.power(10000.0, -jnp.arange(0, ROT, 2, dtype=F32) / ROT)
    angle = pos.astype(F32) * freqs[:, None]
    cs = jnp.concatenate([jnp.cos(angle), jnp.sin(angle)], axis=1)

    order_y = lax.dynamic_index_in_dim(order, y, axis=0, keepdims=False)
    places_y = lax.dynamic_index_in_dim(places, y, axis=0, keepdims=False)
    first = order_y.reshape(32, 2)[:, 0]
    low = jnp.minimum(first, 63 - first)
    low_k = low.reshape(4, 4, 2).transpose(1, 2, 0).reshape(16, 2)
    block_k = jnp.concatenate([low_k, 63 - low_k[:, ::-1]]).reshape(64, 1)
    t_k = (block_k * 64 + blocks).reshape(1, 4096)
    low_q = lax.dynamic_index_in_dim(low.reshape(4, 8), x * 2 + k, axis=1, keepdims=False)
    flips = (mine[:, 0] >= 32).astype(jnp.int32)
    block_q = jnp.stack([low_q, 63 - low_q.reshape(2, 2)[:, ::-1].reshape(4)])
    t_q = block_q[..., None] * 64 + blocks
    s_q = t_q - pick(places_y, block_q)
    qkvd, normed, zpart_two, feed_pack, small = prepare(
        flips, h_all, c_all, wq, wu, s_all, cs, w_out, w_down, b_up
    )
    returned, z_two, feed = attend(
        qkvd, t_k, t_q.reshape(2, 256, 1), s_q.reshape(2, 256, 1), zpart_two,
        feed_pack.reshape(2, 4, 4, 21, 16, 128),
    )
    zpart_one, pack, small = after(flips, returned, h_all, c_all, normed, wq, w_out, cs, small)
    full, z_one, small_all = sums(pack.reshape(2, 4, 4, 11, 16, 128), zpart_one, small)
    (
        output, grad_input, grad_qkv, grad_out, grad_up, grad_down, one_g, one_b, two_g, two_b,
        grad_bqkv, grad_bout, grad_bup,
    ) = finish(
        hidden, cotangent, z_one, z_two, s_all, full.reshape(32, 11, 16, 128), small_all,
        feed.reshape(16, 2, 21, 16, 128),
    )
    return (
        output, grad_input, one_g, one_b, two_g, two_b, grad_qkv, grad_bqkv, grad_out, grad_bout,
        grad_up, grad_bup, grad_down, grad_bout,
    )


def solution(mesh):
    tokens, vector, matrix = P(("shard", "ctx"), None), P("shard"), P("shard", None)
    return jax.shard_map(
        local,
        mesh=mesh,
        in_specs=(
            tokens, vector, vector, vector, vector, matrix, vector, matrix, vector, matrix, vector,
            matrix, vector, matrix, matrix, tokens,
        ),
        out_specs=(
            tokens, tokens, vector, vector, vector, vector, matrix, vector, matrix, vector, matrix,
            vector, matrix, vector,
        ),
        check_vma=False,
    )
```

```python
import functools
import math

import jax
import jax.numpy as jnp
import numpy as np
from jax import lax
from jax.experimental import pallas as pl
from jax.experimental.pallas import tpu as pltpu
from jax.sharding import PartitionSpec as P

HD = 64
ROT = 16
D = 768
NH = 3
HC = NH * HD
CHUNK = 2048
MESH = pl.DeviceIdType.MESH
BF = jnp.bfloat16
F32 = jnp.float32
LIMIT = 56 * 1024 * 1024


def vmem(count):
    return [pl.BlockSpec(memory_space=pltpu.VMEM)] * count


def spots():
    c = lax.axis_index("ctx")
    return c, lax.div(c, 8), lax.rem(lax.div(c, 2), 4), lax.rem(c, 2)


def place(y, x, k):
    return y * 8 + x * 2 + k


def plane(x, y, k):
    a = x + k * (y - x)
    b = y + k * (x - y)
    a_peer, b_peer = [], []
    for d in range(4):
        ax, by = lax.rem(a + d, 4), lax.rem(b + d, 4)
        a_peer.append({"ctx": place(b + k * (ax - b), ax + k * (b - ax), k)})
        b_peer.append({"ctx": place(by + k * (a - by), a + k * (by - a), k)})
    return a, b, a_peer, b_peer


def remote(src, dst, send_sem, recv_sem, where):
    return pltpu.make_async_remote_copy(
        src_ref=src,
        dst_ref=dst,
        send_sem=send_sem,
        recv_sem=recv_sem,
        device_id=where,
        device_id_type=MESH,
    )


def send(src, dst, send_sem, recv_sem, where):
    copy = remote(src, dst, send_sem, recv_sem, where)
    copy.start()
    return copy


def greet(peers):
    barrier = pltpu.get_barrier_semaphore()
    for peer in peers:
        pl.semaphore_signal(barrier, inc=1, device_id=peer, device_id_type=MESH)
    pl.semaphore_wait(barrier, len(peers))


def dma(*dims):
    return pltpu.SemaphoreType.DMA(dims)


def params(ident):
    return pltpu.CompilerParams(
        collective_id=ident, has_side_effects=True, vmem_limit_bytes=LIMIT
    )


def spread_kernel(
    hid, cot, w_qkv, wu, g1, b1, g2, b2, bo, bd, bq, pos, place_of,
    h_all, c_all, wq_all, wu_all, s_all, p_all, o_all,
    wq, small, so, ro, sp, rp, sf, rf, ss, rs,
):
    z = lax.axis_index("shard")
    c, y, x, k = spots()
    sibling = {"ctx": c + 1 - 2 * k}
    peers = [{"shard": lax.rem(z + d, 4)} for d in range(4)]
    greet(peers[1:] + [sibling])
    rows = wu.shape[0]
    half = rows // 2
    width = wu_all.shape[2]
    for p in range(4):
        wq[p] = jnp.concatenate(
            [w_qkv[:, D * t + HC * p : D * t + HC * p + HC] for t in range(3)], axis=1
        )
    small[...] = jnp.zeros_like(small)
    for i, ref in enumerate((g1, b1, g2, b2, bo, bd)):
        small[i : i + 1] = ref[...].astype(F32).reshape(1, HC)
    bias = bq[...].astype(F32).reshape(1, 3 * HC)
    for i in range(3):
        small[6 + i : 7 + i] = bias[:, HC * i : HC * i + HC]

    mine = pl.ds(pl.multiple_of(k * half, 16), half)
    weights, others = {}, []
    for d in (1, 3, 2):
        p = lax.rem(z + d, 4)
        cols = pl.ds(pl.multiple_of(p * width, 128), width)
        weights[d] = [
            send(wq.at[p, mine], wq_all.at[z, mine], sp.at[0, d - 1], rp.at[0, d - 1], peers[d]),
            send(wu.at[mine, cols], wu_all.at[z, mine], sp.at[1, d - 1], rp.at[1, d - 1], peers[d]),
        ]
    cut = hid.shape[0] // 2
    parts = [pl.ds(0, cut), pl.ds(cut, cut)]
    ring = {}
    for i, (src, dst) in enumerate(((hid, h_all), (cot, c_all))):
        for n in range(2):
            ring[i, 1, n] = send(
                src.at[parts[n]], dst.at[z, parts[n]], so.at[i, 0, n], ro.at[i, 0, n], peers[1]
            )
            m = 1 - n
            ring[i, 3, m] = send(
                src.at[parts[m]], dst.at[z, parts[m]], so.at[i, 1, m], ro.at[i, 1, m], peers[3]
            )
    for d in (1, 2, 3):
        for i, (src, dst) in enumerate(((small, s_all), (pos, p_all), (place_of, o_all))):
            others.append(send(src, dst.at[z], ss.at[i, d - 1], rs.at[i, d - 1], peers[d]))
    h_all[z] = hid[...]
    c_all[z] = cot[...]
    s_all[z] = small[...]
    p_all[z] = pos[...]
    o_all[z] = place_of[...]
    wq_all[z] = wq[z]
    wu_all[z] = wu[:, pl.ds(pl.multiple_of(z * width, 128), width)]
    before, after = lax.rem(z + 3, 4), lax.rem(z + 1, 4)
    for d in (1, 3, 2):
        source = lax.rem(z + 4 - d, 4)
        for i, full in enumerate((wq_all, wu_all)):
            weights[d][i].wait_recv()
            part = full.at[source, mine]
            others.append(send(part, part, sf.at[i, d - 1], rf.at[i, d - 1], sibling))
    for i, full in enumerate((h_all, c_all)):
        ring[i, 1, 0].wait_recv()
        part = full.at[before, parts[0]]
        others.append(send(part, part, ss.at[3 + i, 0], rs.at[3 + i, 0], peers[1]))
        ring[i, 3, 1].wait_recv()
        part = full.at[after, parts[1]]
        others.append(send(part, part, ss.at[3 + i, 1], rs.at[3 + i, 1], peers[3]))
    for i in range(2):
        ring[i, 1, 1].wait_recv()
        ring[i, 3, 0].wait_recv()
    for copy in others:
        copy.wait()
    for d in (1, 3, 2):
        for copy in weights[d]:
            copy.wait_send()
    for copy in ring.values():
        copy.wait_send()


def spread(hid, cot, w_qkv, wu, vectors, pos, place_of):
    rows = hid.shape[0]
    width = wu.shape[1] // 4
    return pl.pallas_call(
        spread_kernel,
        out_shape=(
            jax.ShapeDtypeStruct((4, rows, D), BF),
            jax.ShapeDtypeStruct((4, rows, D), BF),
            jax.ShapeDtypeStruct((4, wu.shape[0], 3 * HC), BF),
            jax.ShapeDtypeStruct((4, wu.shape[0], width), BF),
            jax.ShapeDtypeStruct((4, 16, HC), F32),
            jax.ShapeDtypeStruct((4,) + pos.shape, jnp.int32),
            jax.ShapeDtypeStruct((4,) + place_of.shape, jnp.int32),
        ),
        in_specs=vmem(13),
        out_specs=tuple(vmem(7)),
        scratch_shapes=[
            pltpu.VMEM((4, wu.shape[0], 3 * HC), BF),
            pltpu.VMEM((16, HC), F32),
            dma(2, 2, 2), dma(2, 2, 2), dma(2, 3), dma(2, 3), dma(2, 3), dma(2, 3),
            dma(5, 3), dma(5, 3),
        ],
        compiler_params=params(0),
    )(hid, cot, w_qkv, wu, *vectors, pos, place_of)


def dot(left, right):
    return jnp.dot(left, right, preferred_element_type=F32)


def dot_nt(left, right):
    return lax.dot_general(left, right, (((1,), (1,)), ((), ())), preferred_element_type=F32)


def dot_tn(left, right):
    return lax.dot_general(left, right, (((0,), (0,)), ((), ())), preferred_element_type=F32)


def normalize(flat):
    center = flat - jnp.mean(flat, axis=-1, keepdims=True)
    r = lax.rsqrt(jnp.mean(center * center, axis=-1, keepdims=True) + 1e-05)
    return center * r, r


def vector(s_all, i):
    return jnp.concatenate([s_all[p, i : i + 1] for p in range(4)], axis=1)


def swap(v, flag):
    return jnp.where(flag > 0, pltpu.roll(v, 64, 1), v)


def turned(v, cosine, sine):
    first, second = v[0:8], v[8:16]
    return jnp.concatenate(
        [first * cosine - second * sine, second * cosine + first * sine, v[16:]], axis=0
    )


def prepare_kernel(
    flips, h_all, c_all, wq, wu, s_all, cs, w_out, w_down, b_up, qkvd, normed, zpart, pack, small
):
    z = lax.axis_index("shard")
    count = h_all.shape[1]
    xhat, _ = normalize(h_all[...].reshape(4 * count, D).astype(F32))
    cot = c_all[...].reshape(4 * count, D)
    n1 = (xhat * vector(s_all, 0) + vector(s_all, 1)).astype(BF)
    normed[...] = n1
    bias = []
    for t in range(3):
        piece = jnp.zeros((1, HC), F32)
        for p in range(4):
            n = 4 * t + p
            piece = piece + jnp.where(z == p, s_all[n // 3, 6 + n % 3 : 7 + n % 3], 0.0)
        bias.append(piece)
    joined = dot(n1, wq[...].reshape(D, 3 * HC)) + jnp.concatenate(bias, axis=1)
    d_mixed = dot_nt(w_out[...], cot)
    for s in range(4):
        jt = joined[count * s : count * s + count].T
        cosine, sine = cs[s, 0:8], cs[s, 8:16]
        for h in range(NH):
            at = HD * h
            rows = [
                turned(jt[HC + at : HC + at + HD], cosine, sine),
                jt[2 * HC + at : 2 * HC + at + HD],
                turned(jt[at : at + HD], cosine, sine),
                d_mixed[at : at + HD, count * s : count * s + count],
            ]
            qkvd[s, h] = swap(jnp.concatenate(rows, axis=0), flips[s]).astype(BF)

    n2 = (xhat * vector(s_all, 2) + vector(s_all, 3)).astype(BF)
    up = wu[...].reshape(D, wu.shape[2])
    hidden = dot(n2, up) + b_up[...].astype(F32).reshape(1, b_up.shape[0])
    rise = 0.5 * (1.0 + lax.erf(hidden * (1.0 / math.sqrt(2.0))))
    slope = rise + hidden * jnp.exp(-0.5 * hidden * hidden) * (1.0 / math.sqrt(2.0 * math.pi))
    active = (hidden * rise).astype(BF)
    d_up = (dot_nt(cot, w_down[...]) * slope).astype(BF)
    g_down = dot_tn(active, cot).astype(BF)
    for half in range(2):
        for i in range(3):
            at = 384 * half + 128 * i
            tiles = g_down[:, at : at + 128].reshape(16, 3, 16, 128)
            pack[:, half, 12 + 3 * i : 15 + 3 * i] = tiles
    g_up = dot_tn(n2, d_up).astype(BF)
    pack[12:16, :, 0:12] = jnp.zeros((4, 2, 12, 16, 128), BF)
    for p in range(4):
        for j in range(6):
            tiles = g_up[HC * p : HC * p + HC, 128 * j : 128 * j + 128].reshape(2, 2, 3, 16, 128)
            pack[2 * j : 2 * j + 2, :, 3 * p : 3 * p + 3] = tiles
    branch = dot(active, w_down[...]).astype(BF)
    d_two = dot_nt(d_up, up)
    for s in range(4):
        zpart[s, 0] = branch[count * s : count * s + count]
        zpart[s, 1] = d_two[count * s : count * s + count].astype(BF)
    small[...] = jnp.zeros_like(small)
    small[2:3] = jnp.sum(d_two * xhat, axis=0, keepdims=True)
    small[3:4] = jnp.sum(d_two, axis=0, keepdims=True)
    small[4:5] = jnp.sum(cot.astype(F32), axis=0, keepdims=True)
    small[5:6] = jnp.sum(d_up.astype(F32), axis=0, keepdims=True)


def prepare(flips, h_all, c_all, wq, wu, s_all, cs, w_out, w_down, b_up):
    count = h_all.shape[1]
    return pl.pallas_call(
        prepare_kernel,
        out_shape=(
            jax.ShapeDtypeStruct((4, NH, 4 * HD, count), BF),
            jax.ShapeDtypeStruct((4 * count, D), BF),
            jax.ShapeDtypeStruct((4, 2, count, D), BF),
            jax.ShapeDtypeStruct((16, 2, 21, 16, 128), BF),
            jax.ShapeDtypeStruct((8, D), F32),
        ),
        in_specs=[pl.BlockSpec(memory_space=pltpu.SMEM)] + vmem(9),
        out_specs=tuple(vmem(5)),
        compiler_params=pltpu.CompilerParams(vmem_limit_bytes=LIMIT),
    )(flips, h_all, c_all, wq, wu, s_all, cs, w_out, w_down, b_up)


def attend_kernel(
    qkvd, t_k, t_q, s_q, zpart, pack, out, z_all, full,
    kv, qd, kt, dkv, qdt, oqt, s_buf, p_buf, dpart, got, ready,
    w_got, w_one, w_far, w_two, w_beyond, w_three, w_last,
    s_k, r_k, s_d, r_d, s_f, r_f, s_n, r_n, s_o, r_o, s_z, r_z,
    w_sc, w_rc, w_sa, w_ra, w_sb, w_rb, w_sz, w_rz, w_gb, w_hb, w_ga, w_ha, w_gc, w_hc,
):
    z = lax.axis_index("shard")
    c, y, x, k = spots()
    sibling = {"ctx": c + 1 - 2 * k}
    z_peer = [{"shard": lax.rem(z + d, 4)} for d in range(4)]
    a, b, a_peer, b_peer = plane(x, y, k)
    steps = [(dy, dx) for dy in range(4) for dx in range(4) if dy or dx]
    steps.sort(key=lambda s: min(s[0], 4 - s[0]) + min(s[1], 4 - s[1]))
    far_spot, far_peer = {}, {}
    for dy, dx in steps:
        ys, xs = lax.rem(y + dy, 4), lax.rem(x + dx, 4)
        far_spot[dy, dx] = (ys, xs)
        far_peer[dy, dx] = {"ctx": place(ys, xs, k)}
    greet(list(far_peer.values()) + z_peer[1:] + [sibling])
    busy = x < 3
    slot = y * 4 + x
    tail = []

    there = {}
    for dy, dx in steps:
        ys, xs = far_spot[dy, dx]
        n = 4 * dy + dx
        h = lax.rem(xs, 3)
        there[dy, dx] = [
            remote(
                qkvd.at[ys, h, pl.ds(0, 128)], kv.at[k * 16 + slot], s_k.at[n], r_k.at[n],
                far_peer[dy, dx],
            ),
            remote(
                qkvd.at[ys, h, pl.ds(128, 128)], qd.at[slot], s_d.at[n], r_d.at[n],
                far_peer[dy, dx],
            ),
        ]
    for i in range(2):
        for dy, dx in steps:

            @pl.when(far_spot[dy, dx][1] < 3)
            def _():
                there[dy, dx][i].start()

    @pl.when(busy)
    def _():
        kv[k * 16 + slot] = qkvd[y, lax.rem(x, 3), 0:128]
        qd[slot] = qkvd[y, lax.rem(x, 3), 128:]

    w_near, w_across, w_over, w_turn, w_out_b, w_out_a = {}, {}, {}, {}, {}, {}

    def w_core():
        for d in (1, 3, 2, 0):
            ap = lax.rem(b + d, 4)
            w_near[d] = send(pack.at[1 - k, ap], w_got.at[ap], w_sc.at[d], w_rc.at[d], sibling)

    def w_sum_core():
        for d in (1, 3, 2, 0):
            ap = lax.rem(a + d, 4)
            w_near[d].wait_recv()
            w_one[ap] = (pack[k, ap].astype(F32) + w_got[ap].astype(F32)).astype(BF)
            if d:
                w_across[d] = send(
                    w_one.at[ap], w_far.at[d - 1], w_sa.at[d - 1], w_ra.at[d - 1], a_peer[d]
                )

    def w_sum_a():
        for d in (1, 3, 2):
            w_across[d].wait_recv()
        for d in (1, 3, 2, 0):
            bp = lax.rem(b + d, 4)
            total = w_one[a, bp].astype(F32)
            for n in range(3):
                total = total + w_far[n, bp].astype(F32)
            w_two[bp] = total.astype(BF)
            if d:
                w_over[d] = send(
                    w_two.at[bp], w_beyond.at[d - 1], w_sb.at[d - 1], w_rb.at[d - 1], b_peer[d]
                )

    def w_sum_b():
        for d in (1, 3, 2):
            w_over[d].wait_recv()
        total = w_two[b].astype(F32)
        for n in range(3):
            total = total + w_beyond[n].astype(F32)
        w_three[...] = total.astype(BF)
        for d in (1, 3, 2):
            zp = lax.rem(z + d, 4)
            w_turn[d] = send(
                w_three.at[pl.ds(3 * zp, 3)], w_last.at[pl.ds(3 * z, 3)],
                w_sz.at[d - 1], w_rz.at[d - 1], z_peer[d],
            )
        w_last[pl.ds(3 * z, 3)] = w_three[pl.ds(3 * z, 3)]
        w_last[12:] = w_three[12:]

    def w_back_b():
        for d in (1, 3, 2):
            w_turn[d].wait()
        full[k, a, b] = w_last[...]
        for d in (1, 3, 2):
            w_out_b[d] = send(
                w_last, full.at[k, a, b], w_gb.at[d - 1], w_hb.at[d - 1], b_peer[d]
            )

    def w_back_a():
        for d in (1, 3, 2):
            w_out_b[d].wait()
        for d in (1, 3, 2):
            w_out_a[d] = send(
                full.at[k, a], full.at[k, a], w_ga.at[d - 1], w_ha.at[d - 1], a_peer[d]
            )
        tail.append(send(full.at[k, a], full.at[k, a], w_gc.at[0], w_hc.at[0], sibling))

    def w_back_core():
        for d in (1, 3, 2):
            w_out_a[d].wait_recv()
            ap = lax.rem(a + 4 - d, 4)
            tail.append(send(full.at[k, ap], full.at[k, ap], w_gc.at[d], w_hc.at[d], sibling))

    left = lax.broadcasted_iota(jnp.int32, (128, 128), 1) < 64
    mine, others = pl.ds(k * 16, 16), pl.ds((1 - k) * 16, 16)
    forward = remote(kv.at[mine], kv.at[mine], s_f.at[0], r_f.at[0], sibling)

    def sort():
        def step(j, carry):
            one = kv[2 * j].astype(F32)
            two = pltpu.roll(kv[2 * j + 1].astype(F32), 64, 1)
            kt[:, pl.ds(pl.multiple_of(j * 128, 128), 128)] = jnp.where(left, one, two).astype(BF)
            kt[:, pl.ds(pl.multiple_of((16 + j) * 128, 128), 128)] = jnp.where(left, two, one).astype(BF)
            return carry

        lax.fori_loop(0, 16, step, 0)
        dkv[...] = jnp.zeros_like(dkv)

    def queries(n):
        for m in range(2):
            one = qd[4 * n + 2 * m].astype(F32)
            two = pltpu.roll(qd[4 * n + 2 * m + 1].astype(F32), 64, 1)
            cols = slice(128 * m, 128 * m + 128)
            qdt[0, :, cols] = jnp.where(left, one, two)
            qdt[1, :, cols] = jnp.where(left, two, one)

    def answers(n):
        for m in range(2):
            cols = slice(128 * m, 128 * m + 128)
            low, high = oqt[0, :, cols], oqt[1, :, cols]
            ready[1, 4 * n + 2 * m] = jnp.where(left, low, high).astype(BF)
            ready[1, 4 * n + 2 * m + 1] = pltpu.roll(jnp.where(left, high, low), 64, 1).astype(BF)

    def unsort():
        def step(j, carry):
            low = dkv[:, pl.ds(pl.multiple_of(j * 128, 128), 128)]
            high = dkv[:, pl.ds(pl.multiple_of((16 + j) * 128, 128), 128)]
            dpart[2 * j] = jnp.where(left, low, high).astype(BF)
            dpart[2 * j + 1] = pltpu.roll(jnp.where(left, high, low), 64, 1).astype(BF)
            return carry

        lax.fori_loop(0, 16, step, 0)

    keys, values = slice(0, HD), slice(HD, 2 * HD)

    def one_tile(tile, n):
        q_t = qdt[tile, keys, :] * 0.125
        d_t = qdt[tile, values, :]
        q_n, d_n = q_t.T.astype(BF), d_t.T.astype(BF)
        q_t, d_t = q_t.astype(BF), d_t.astype(BF)
        first_key, last_key = s_q[tile, n], t_q[tile, n]
        top = jnp.full((256, 128), -1e30, F32)
        total = jnp.zeros((256, 128), F32)
        inner = jnp.zeros((256, 128), F32)
        for i in range(tile + 1):
            at = slice(i * CHUNK, i * CHUNK + CHUNK)
            s = dot(q_n, kt[keys, at])
            key = t_k[:, at]
            s = jnp.where((key >= first_key) & (key <= last_key), s, -1e30)
            s_buf[:, at] = s
            dp = dot(d_n, kt[values, at])
            p_buf[:, at] = dp
            new = top
            for m in range(CHUNK // 128):
                new = jnp.maximum(new, s[:, 128 * m : 128 * m + 128])
            scale = jnp.exp(top - new)
            total, inner, top = total * scale, inner * scale, new
            for m in range(CHUNK // 128):
                e = jnp.exp(s[:, 128 * m : 128 * m + 128] - new)
                total = total + e
                inner = inner + e * dp[:, 128 * m : 128 * m + 128]
        most = jnp.max(top, axis=1, keepdims=True)
        scale = jnp.exp(top - most)
        over = 1.0 / jnp.sum(total * scale, axis=1, keepdims=True)
        inner = jnp.sum(inner * scale, axis=1, keepdims=True) * over
        out_t = jnp.zeros((HD, 256), F32)
        dq_t = jnp.zeros((HD, 256), F32)
        for i in range(tile + 1):
            at = slice(i * CHUNK, i * CHUNK + CHUNK)
            p = jnp.exp(s_buf[:, at] - most) * over
            pb = p.astype(BF)
            ds = (p * (p_buf[:, at] - inner)).astype(BF)
            out_t = out_t + dot_nt(kt[values, at], pb)
            dq_t = dq_t + dot_nt(kt[keys, at], ds)
            dkv[values, at] += dot(d_t, pb)
            dkv[keys, at] += dot(q_t, ds)
        oqt[tile, keys, :] = out_t
        oqt[tile, values, :] = dq_t * 0.125

    home = {}
    h = lax.rem(x, 3)
    for dy, dx in steps:
        ys, xs = far_spot[dy, dx]
        n = 4 * dy + dx
        home[dy, dx] = [
            remote(
                ready.at[i, 4 * ys + xs], out.at[y, h, pl.ds(128 * i, 128)],
                s_o.at[i, n], r_o.at[i, n], far_peer[dy, dx],
            )
            for i in range(2)
        ]

    w_core()
    for d in (1, 3, 2):
        zp = lax.rem(z + d, 4)
        tail.append(send(zpart.at[zp], z_all.at[z], s_z.at[d - 1], r_z.at[d - 1], z_peer[d]))
    z_all[z] = zpart[z]

    @pl.when(busy)
    def _():
        for dy, dx in steps:
            there[dy, dx][0].wait_recv()
        forward.start()
        for dy, dx in steps:
            there[dy, dx][1].wait_recv()
        forward.wait()
        sort()

    def nothing():
        pass

    points = (
        (w_sum_core, nothing), (nothing, w_sum_a), (w_sum_b, w_back_b), (w_back_a, nothing)
    )
    for n in range(4):

        @pl.when(busy)
        def _():
            queries(n)
            one_tile(0, n)

        points[n][0]()

        @pl.when(busy)
        def _():
            one_tile(1, n)
            answers(n)

        points[n][1]()

    swap_out = remote(dpart.at[others], got, s_n.at[0], r_n.at[0], sibling)

    @pl.when(busy)
    def _():
        unsort()
        swap_out.start()
        for dy, dx in steps:
            home[dy, dx][1].start()
        out[y, h, 128:] = ready[1, slot]
        swap_out.wait()
        for i in range(4):
            own = dpart[pl.ds(k * 16 + 4 * i, 4)].astype(F32)
            ready[0, 4 * i : 4 * i + 4] = (own + got[4 * i : 4 * i + 4].astype(F32)).astype(BF)
        for dy, dx in steps:
            home[dy, dx][0].start()
        out[y, h, 0:128] = ready[0, slot]

    w_back_core()
    for dy, dx in steps:
        @pl.when(lax.rem(x + 4 - dx, 4) < 3)
        def _():
            for i in range(2):
                home[dy, dx][i].wait_recv()

        @pl.when(far_spot[dy, dx][1] < 3)
        def _():
            for i in range(2):
                there[dy, dx][i].wait_send()

    @pl.when(busy)
    def _():
        for dy, dx in steps:
            for i in range(2):
                home[dy, dx][i].wait_send()

    for copy in tail:
        copy.wait()
    for group in (w_near, w_across, w_over, w_out_a):
        for copy in group.values():
            copy.wait_send()


def attend(qkvd, t_k, t_q, s_q, zpart, pack):
    square = (128, 128)
    tiles = pack.shape[3:]
    return pl.pallas_call(
        attend_kernel,
        out_shape=(
            jax.ShapeDtypeStruct(qkvd.shape, BF),
            jax.ShapeDtypeStruct(zpart.shape, BF),
            jax.ShapeDtypeStruct(pack.shape, BF),
        ),
        in_specs=vmem(6),
        out_specs=tuple(vmem(3)),
        scratch_shapes=[
            pltpu.VMEM((32,) + square, BF),
            pltpu.VMEM((16,) + square, BF),
            pltpu.VMEM((128, 4096), BF),
            pltpu.VMEM((128, 4096), F32),
            pltpu.VMEM((2, 128, 256), F32),
            pltpu.VMEM((2, 128, 256), F32),
            pltpu.VMEM((256, 4096), F32),
            pltpu.VMEM((256, 4096), F32),
            pltpu.VMEM((32,) + square, BF),
            pltpu.VMEM((16,) + square, BF),
            pltpu.VMEM((2, 16) + square, BF),
            pltpu.VMEM((4, 4) + tiles, BF),
            pltpu.VMEM((4, 4) + tiles, BF),
            pltpu.VMEM((3, 4) + tiles, BF),
            pltpu.VMEM((4,) + tiles, BF),
            pltpu.VMEM((3,) + tiles, BF),
            pltpu.VMEM(tiles, BF),
            pltpu.VMEM(tiles, BF),
            dma(16), dma(16), dma(16), dma(16), dma(1), dma(1), dma(1), dma(1),
            dma(2, 16), dma(2, 16), dma(3), dma(3),
            dma(4), dma(4), dma(3), dma(3), dma(3), dma(3), dma(3), dma(3),
            dma(3), dma(3), dma(3), dma(3), dma(4), dma(4),
        ],
        compiler_params=params(1),
    )(qkvd, t_k, t_q, s_q, zpart, pack)


def sum_kernel(
    pack, zpart, small, full, z_all, small_all,
    got, one, far_a, two, far_b, three, last, s1, s2, s3, s4,
    sz, rz, sc, rc, sa, ra, sb, rb, st, rt, gb, hb, ga, ha, gc, hc, sm, rm,
):
    z = lax.axis_index("shard")
    c, y, x, k = spots()
    sibling = {"ctx": c + 1 - 2 * k}
    z_peer = [{"shard": lax.rem(z + d, 4)} for d in range(4)]
    a, b, a_peer, b_peer = plane(x, y, k)
    greet(a_peer[1:] + b_peer[1:] + z_peer[1:] + [sibling])
    near = {}
    for d in (1, 3, 2, 0):
        ap = lax.rem(b + d, 4)
        near[d] = send(pack.at[1 - k, ap], got.at[ap], sc.at[d], rc.at[d], sibling)
    tail = [send(small, s1, sm.at[0], rm.at[0], sibling)]
    for d in (1, 3, 2):
        zp = lax.rem(z + d, 4)
        tail.append(send(zpart.at[zp], z_all.at[z], sz.at[d - 1], rz.at[d - 1], z_peer[d]))
    z_all[z] = zpart[z]
    across = {}
    for d in (1, 3, 2, 0):
        ap = lax.rem(a + d, 4)
        near[d].wait_recv()
        for n in range(4):
            both = pack[k, ap, n].astype(F32) + got[ap, n].astype(F32)
            one[ap, n] = both.astype(BF)
        if d:
            across[d] = send(one.at[ap], far_a.at[d - 1], sa.at[d - 1], ra.at[d - 1], a_peer[d])
    tail[0].wait()
    s2[0] = small[...] + s1[...]
    small_a = [send(s2.at[0], s2.at[d], sm.at[d], rm.at[d], a_peer[d]) for d in (1, 2, 3)]
    for d in (1, 3, 2):
        across[d].wait_recv()
    beyond = {}
    for d in (1, 3, 2, 0):
        bp = lax.rem(b + d, 4)
        total = one[a, bp].astype(F32)
        for n in range(3):
            total = total + far_a[n, bp].astype(F32)
        two[bp] = total.astype(BF)
        if d:
            beyond[d] = send(two.at[bp], far_b.at[d - 1], sb.at[d - 1], rb.at[d - 1], b_peer[d])
    for copy in small_a:
        copy.wait()
    s3[0] = (s2[0] + s2[1]) + (s2[2] + s2[3])
    small_b = [send(s3.at[0], s3.at[d], sm.at[3 + d], rm.at[3 + d], b_peer[d]) for d in (1, 2, 3)]
    for d in (1, 3, 2):
        beyond[d].wait_recv()
    total = two[b].astype(F32)
    for n in range(3):
        total = total + far_b[n].astype(F32)
    three[...] = total.astype(BF)
    turned = []
    for d in (1, 3, 2):
        zp = lax.rem(z + d, 4)
        turned.append(
            send(
                three.at[pl.ds(2 * zp, 2)], last.at[pl.ds(2 * z, 2)],
                st.at[d - 1], rt.at[d - 1], z_peer[d],
            )
        )
    last[pl.ds(2 * z, 2)] = three[pl.ds(2 * z, 2)]
    last[8:] = three[8:]
    for copy in small_b:
        copy.wait()
    s4[...] = (s3[0] + s3[1]) + (s3[2] + s3[3])
    for d in (1, 3, 2):
        tail.append(send(s4, small_all.at[z], sm.at[6 + d], rm.at[6 + d], z_peer[d]))
    small_all[z] = s4[...]
    for copy in turned:
        copy.wait()
    full[k, a, b] = last[...]
    out_b = {}
    for d in (1, 3, 2):
        out_b[d] = send(last, full.at[k, a, b], gb.at[d - 1], hb.at[d - 1], b_peer[d])
    for d in (1, 3, 2):
        out_b[d].wait()
    out_a = {}
    for d in (1, 3, 2):
        out_a[d] = send(full.at[k, a], full.at[k, a], ga.at[d - 1], ha.at[d - 1], a_peer[d])
    tail.append(send(full.at[k, a], full.at[k, a], gc.at[0], hc.at[0], sibling))
    for d in (1, 3, 2):
        out_a[d].wait_recv()
        ap = lax.rem(a + 4 - d, 4)
        tail.append(send(full.at[k, ap], full.at[k, ap], gc.at[d], hc.at[d], sibling))
    for copy in tail[1:]:
        copy.wait()
    for d in (1, 2, 3):
        out_a[d].wait_send()
        across[d].wait_send()
        beyond[d].wait_send()
    for d in range(4):
        near[d].wait_send()


def sums(pack, zpart, small):
    tiles = pack.shape[3:]
    return pl.pallas_call(
        sum_kernel,
        out_shape=(
            jax.ShapeDtypeStruct(pack.shape, BF),
            jax.ShapeDtypeStruct(zpart.shape, BF),
            jax.ShapeDtypeStruct((4,) + small.shape, F32),
        ),
        in_specs=vmem(3),
        out_specs=tuple(vmem(3)),
        scratch_shapes=[
            pltpu.VMEM((4, 4) + tiles, BF),
            pltpu.VMEM((4, 4) + tiles, BF),
            pltpu.VMEM((3, 4) + tiles, BF),
            pltpu.VMEM((4,) + tiles, BF),
            pltpu.VMEM((3,) + tiles, BF),
            pltpu.VMEM(tiles, BF),
            pltpu.VMEM(tiles, BF),
            pltpu.VMEM(small.shape, F32),
            pltpu.VMEM((4,) + small.shape, F32),
            pltpu.VMEM((4,) + small.shape, F32),
            pltpu.VMEM(small.shape, F32),
            dma(3), dma(3), dma(4), dma(4), dma(3), dma(3), dma(3), dma(3), dma(3), dma(3),
            dma(3), dma(3), dma(3), dma(3), dma(4), dma(4), dma(10), dma(10),
        ],
        compiler_params=params(3),
    )(pack, zpart, small)


def after_kernel(flips, ret, h_all, c_all, normed, wq, w_out, cs, given, zpart, pack, small, dj, mt):
    count = h_all.shape[1]
    for s in range(4):
        cosine, sine = cs[s, 0:8], -cs[s, 8:16]
        r = [swap(ret[s, h].astype(F32), flips[s]) for h in range(NH)]
        rows = [turned(r[h][3 * HD :], cosine, sine) for h in range(NH)]
        rows += [turned(r[h][0:HD], cosine, sine) for h in range(NH)]
        rows += [r[h][HD : 2 * HD] for h in range(NH)]
        dj[count * s : count * s + count] = jnp.concatenate(rows, axis=0).T.astype(BF)
        for h in range(NH):
            mt[HD * h : HD * h + HD, count * s : count * s + count] = r[h][2 * HD : 3 * HD].astype(BF)
    cot = c_all[...].reshape(4 * count, D)
    xhat, _ = normalize(h_all[...].reshape(4 * count, D).astype(F32))
    d_one = dot_nt(dj[...], wq[...].reshape(D, 3 * HC))
    branch = dot(mt[...].astype(F32).T.astype(BF), w_out[...])
    for s in range(4):
        zpart[s, 0] = branch[count * s : count * s + count].astype(BF)
        zpart[s, 1] = d_one[count * s : count * s + count].astype(BF)
    small[...] = given[...]
    small[0:1] = jnp.sum(d_one * xhat, axis=0, keepdims=True)
    small[1:2] = jnp.sum(d_one, axis=0, keepdims=True)
    small[6:7, 0 : 3 * HC] = jnp.sum(dj[...].astype(F32), axis=0, keepdims=True)
    pack[24:32] = jnp.zeros((8,) + pack.shape[1:], BF)
    g = dot_tn(normed[...], dj[...])
    for p in range(4):
        mine = g[HC * p : HC * p + HC]
        for j in range(4):
            tiles = mine[:, 128 * j : 128 * j + 128].astype(BF).reshape(6, 2, 16, 128)
            pack[6 * j : 6 * j + 6, 2 * p : 2 * p + 2] = tiles
        rest = jnp.concatenate([mine[: HC // 2, 512:], mine[HC // 2 :, 512:]], axis=1)
        pack[24:27, 2 * p : 2 * p + 2] = rest.astype(BF).reshape(3, 2, 16, 128)
    g = dot(mt[...], cot)
    for j in range(6):
        tiles = g[:, 128 * j : 128 * j + 128].astype(BF).reshape(4, 3, 16, 128)
        pack[4 * j : 4 * j + 4, 8:11] = tiles


def after(flips, ret, h_all, c_all, normed, wq, w_out, cs, given):
    count = h_all.shape[1]
    return pl.pallas_call(
        after_kernel,
        out_shape=(
            jax.ShapeDtypeStruct((4, 2, count, D), BF),
            jax.ShapeDtypeStruct((32, 11, 16, 128), BF),
            jax.ShapeDtypeStruct((8, D), F32),
        ),
        in_specs=[pl.BlockSpec(memory_space=pltpu.SMEM)] + vmem(8),
        out_specs=tuple(vmem(3)),
        scratch_shapes=[pltpu.VMEM((4 * count, 3 * HC), BF), pltpu.VMEM((HC, 4 * count), BF)],
        compiler_params=pltpu.CompilerParams(vmem_limit_bytes=LIMIT),
    )(flips, ret, h_all, c_all, normed, wq, w_out, cs, given)


def finish_kernel(
    hid, cot, z_one, z_two, s_all, full, small_all, feed,
    out, grad, g_qkv, g_out, g_up, g_down, one_g, one_b, two_g, two_b, g_bqkv, g_bout, g_bup,
):
    z = lax.axis_index("shard")
    branch, d_one, d_two = 0.0, 0.0, 0.0
    for p in range(4):
        branch = branch + (z_one[p, 0].astype(F32) + z_two[p, 0].astype(F32))
        d_one = d_one + z_one[p, 1].astype(F32)
        d_two = d_two + z_two[p, 1].astype(F32)
    flat = hid[...].astype(F32)
    xhat, r = normalize(flat)
    out[...] = (flat + branch + vector(s_all, 4) + vector(s_all, 5)).astype(BF)
    g = d_one * vector(s_all, 0) + d_two * vector(s_all, 2)
    inner = jnp.mean(g * xhat, axis=-1, keepdims=True)
    grad[...] = cot[...].astype(F32) + r * (g - jnp.mean(g, axis=-1, keepdims=True) - xhat * inner)
    planes = []
    for p in range(4):
        cols = [full[6 * j : 6 * j + 6, 2 * p : 2 * p + 2].reshape(HC, 128) for j in range(4)]
        rest = full[24:27, 2 * p : 2 * p + 2].reshape(HC // 2, 128).astype(F32)
        rest = jnp.concatenate([rest[:, :64], rest[:, 64:]], axis=0)
        planes.append(jnp.concatenate([col.astype(F32) for col in cols] + [rest], axis=1))
    for t in range(3):
        g_qkv[:, D * t : D * t + D] = jnp.concatenate(
            [plane[:, HC * t : HC * t + HC] for plane in planes], axis=1
        )
    for j in range(6):
        tiles = full[4 * j : 4 * j + 4, 8:11].reshape(HC, 128)
        g_out[:, 128 * j : 128 * j + 128] = tiles.astype(F32)
    total = (small_all[0] + small_all[1]) + (small_all[2] + small_all[3])
    own = small_all[z]
    rows = jnp.concatenate([total[0:4], own[4:5]], axis=0)
    piece = jnp.zeros((5, HC), F32)
    for p in range(4):
        piece = piece + jnp.where(z == p, rows[:, HC * p : HC * p + HC], 0.0)
    for i, ref in enumerate((one_g, one_b, two_g, two_b, g_bout)):
        ref[...] = piece[i : i + 1].reshape(HC)
    pieces = []
    for i in range(3):
        piece = jnp.zeros((1, HC), F32)
        for p in range(4):
            n = 3 * p + i
            at = HC * (n // 4)
            piece = piece + jnp.where(z == p, small_all[n % 4, 6:7, at : at + HC], 0.0)
        pieces.append(piece)
    g_bqkv[...] = jnp.concatenate(pieces, axis=1).reshape(3 * HC)
    g_bup[...] = own[5:6].reshape(g_bup.shape)
    for half in range(2):
        for i in range(3):
            tiles = feed[:, half, 12 + 3 * i : 15 + 3 * i].reshape(D, 128)
            at = 384 * half + 128 * i
            g_down[:, at : at + 128] = tiles.astype(F32)
    for p in range(4):
        for j in range(6):
            tiles = feed[2 * j : 2 * j + 2, :, 3 * p : 3 * p + 3].reshape(HC, 128)
            g_up[:, D * p + 128 * j : D * p + 128 * j + 128] = tiles.astype(F32)


def finish(hid, cot, z_one, z_two, s_all, full, small_all, feed):
    return pl.pallas_call(
        finish_kernel,
        out_shape=(
            jax.ShapeDtypeStruct(hid.shape, BF),
            jax.ShapeDtypeStruct(hid.shape, F32),
            jax.ShapeDtypeStruct((HC, 3 * D), F32),
            jax.ShapeDtypeStruct((HC, D), F32),
            jax.ShapeDtypeStruct((HC, 4 * D), F32),
            jax.ShapeDtypeStruct((D, D), F32),
            jax.ShapeDtypeStruct((HC,), F32),
            jax.ShapeDtypeStruct((HC,), F32),
            jax.ShapeDtypeStruct((HC,), F32),
            jax.ShapeDtypeStruct((HC,), F32),
            jax.ShapeDtypeStruct((3 * HC,), F32),
            jax.ShapeDtypeStruct((HC,), F32),
            jax.ShapeDtypeStruct((D,), F32),
        ),
        in_specs=vmem(8),
        out_specs=tuple(vmem(13)),
        compiler_params=pltpu.CompilerParams(vmem_limit_bytes=LIMIT),
    )(hid, cot, z_one, z_two, s_all, full, small_all, feed)


def local(
    hidden, ln1_gain, ln1_bias, ln2_gain, ln2_bias, w_qkv, b_qkv, w_out, b_out, w_up, b_up,
    w_down, b_down, block_order, positions, cotangent,
):
    rows = hidden.shape[0]
    c, y, x, k = spots()
    vectors = (ln1_gain, ln1_bias, ln2_gain, ln2_bias, b_out, b_down, b_qkv)
    h_all, c_all, wq, wu, s_all, p_all, o_all = spread(
        hidden, cotangent, w_qkv, w_up, vectors, positions, block_order
    )

    places = p_all.reshape(4, 64, 64)
    order = o_all.reshape(4, 64)
    blocks = jnp.arange(64, dtype=jnp.int32)

    def pick(table, which):
        hit = which[..., None] == blocks
        return jnp.sum(jnp.where(hit[..., None], table, 0), axis=-2)

    mine = lax.dynamic_slice(order, (0, 2 * c), (4, 2))
    pos = pick(places[:, None], mine).reshape(4, 1, rows)
    freqs = jnp.power(10000.0, -jnp.arange(0, ROT, 2, dtype=F32) / ROT)
    angle = pos.astype(F32) * freqs[:, None]
    cs = jnp.concatenate([jnp.cos(angle), jnp.sin(angle)], axis=1)

    order_y = lax.dynamic_index_in_dim(order, y, axis=0, keepdims=False)
    places_y = lax.dynamic_index_in_dim(places, y, axis=0, keepdims=False)
    first = order_y.reshape(32, 2)[:, 0]
    low = jnp.minimum(first, 63 - first)
    low_k = low.reshape(16, 2).T.reshape(16, 2)
    block_k = jnp.concatenate([low_k, 63 - low_k[:, ::-1]]).reshape(64, 1)
    t_k = (block_k * 64 + blocks).reshape(1, 4096)
    low_q = lax.dynamic_index_in_dim(low.reshape(16, 2), k, axis=1, keepdims=False)
    flips = (mine[:, 0] >= 32).astype(jnp.int32)
    block_q = jnp.stack([low_q, 63 - low_q.reshape(8, 2)[:, ::-1].reshape(16)])
    t_q = block_q[..., None] * 64 + blocks
    s_q = t_q - pick(places_y, block_q)
    qkvd, normed, zpart_two, feed_pack, small = prepare(
        flips, h_all, c_all, wq, wu, s_all, cs, w_out, w_down, b_up
    )
    returned, z_two, feed = attend(
        qkvd, t_k, t_q.reshape(2, 4, 256, 1), s_q.reshape(2, 4, 256, 1), zpart_two,
        feed_pack.reshape(2, 4, 4, 21, 16, 128),
    )
    zpart_one, pack, small = after(flips, returned, h_all, c_all, normed, wq, w_out, cs, small)
    full, z_one, small_all = sums(pack.reshape(2, 4, 4, 11, 16, 128), zpart_one, small)
    (
        output, grad_input, grad_qkv, grad_out, grad_up, grad_down, one_g, one_b, two_g, two_b,
        grad_bqkv, grad_bout, grad_bup,
    ) = finish(
        hidden, cotangent, z_one, z_two, s_all, full.reshape(32, 11, 16, 128), small_all,
        feed.reshape(16, 2, 21, 16, 128),
    )
    return (
        output, grad_input, one_g, one_b, two_g, two_b, grad_qkv, grad_bqkv, grad_out, grad_bout,
        grad_up, grad_bup, grad_down, grad_bout,
    )


def solution(mesh):
    tokens, vector, matrix = P(("shard", "ctx"), None), P("shard"), P("shard", None)
    return jax.shard_map(
        local,
        mesh=mesh,
        in_specs=(
            tokens, vector, vector, vector, vector, matrix, vector, matrix, vector, matrix, vector,
            matrix, vector, matrix, matrix, tokens,
        ),
        out_specs=(
            tokens, tokens, vector, vector, vector, vector, matrix, vector, matrix, vector, matrix,
            vector, matrix, vector,
        ),
        check_vma=False,
    )
```

```python
import functools
import math

import jax
import jax.numpy as jnp
import numpy as np
from jax import lax
from jax.experimental import pallas as pl
from jax.experimental.pallas import tpu as pltpu
from jax.sharding import PartitionSpec as P

HD = 64
ROT = 16
D = 768
NH = 3
HC = NH * HD
CHUNK = 2048
MESH = pl.DeviceIdType.MESH
BF = jnp.bfloat16
F32 = jnp.float32
LIMIT = 56 * 1024 * 1024


def vmem(count):
    return [pl.BlockSpec(memory_space=pltpu.VMEM)] * count


def spots():
    c = lax.axis_index("ctx")
    return c, lax.div(c, 8), lax.rem(lax.div(c, 2), 4), lax.rem(c, 2)


def place(y, x, k):
    return y * 8 + x * 2 + k


def plane(x, y, k):
    a = x + k * (y - x)
    b = y + k * (x - y)
    a_peer, b_peer = [], []
    for d in range(4):
        ax, by = lax.rem(a + d, 4), lax.rem(b + d, 4)
        a_peer.append({"ctx": place(b + k * (ax - b), ax + k * (b - ax), k)})
        b_peer.append({"ctx": place(by + k * (a - by), a + k * (by - a), k)})
    return a, b, a_peer, b_peer


def remote(src, dst, send_sem, recv_sem, where):
    return pltpu.make_async_remote_copy(
        src_ref=src,
        dst_ref=dst,
        send_sem=send_sem,
        recv_sem=recv_sem,
        device_id=where,
        device_id_type=MESH,
    )


def send(src, dst, send_sem, recv_sem, where):
    copy = remote(src, dst, send_sem, recv_sem, where)
    copy.start()
    return copy


def greet(peers):
    barrier = pltpu.get_barrier_semaphore()
    for peer in peers:
        pl.semaphore_signal(barrier, inc=1, device_id=peer, device_id_type=MESH)
    pl.semaphore_wait(barrier, len(peers))


def dma(*dims):
    return pltpu.SemaphoreType.DMA(dims)


def params(ident):
    return pltpu.CompilerParams(
        collective_id=ident, has_side_effects=True, vmem_limit_bytes=LIMIT
    )


def spread_kernel(
    hid, cot, w_qkv, wu, g1, b1, g2, b2, bo, bd, bq, pos, place_of,
    h_all, c_all, wq_all, wu_all, s_all, p_all, o_all,
    wq, small, so, ro, sp, rp, sx, rx, sf, rf, ss, rs,
):
    z = lax.axis_index("shard")
    c, y, x, k = spots()
    sibling = {"ctx": c + 1 - 2 * k}
    peers = [{"shard": lax.rem(z + d, 4)} for d in range(4)]
    greet(
        peers[1:] + [sibling] + [{"ctx": place(y, lax.rem(x + d, 4), k)} for d in (1, 2, 3)]
    )
    rows = wu.shape[0]
    quarter = rows // 4
    width = wu_all.shape[2]
    for p in range(4):
        wq[p] = jnp.concatenate(
            [w_qkv[:, D * t + HC * p : D * t + HC * p + HC] for t in range(3)], axis=1
        )
    small[...] = jnp.zeros_like(small)
    for i, ref in enumerate((g1, b1, g2, b2, bo, bd)):
        small[i : i + 1] = ref[...].astype(F32).reshape(1, HC)
    bias = bq[...].astype(F32).reshape(1, 3 * HC)
    for i in range(3):
        small[6 + i : 7 + i] = bias[:, HC * i : HC * i + HC]

    mine = pl.ds(pl.multiple_of(x * quarter, 16), quarter)
    x_peer = [{"ctx": place(y, lax.rem(x + d, 4), k)} for d in range(4)]
    weights, spread_x, spread_k, others = {}, {}, {}, []
    for d in (1, 3, 2):
        p = lax.rem(z + d, 4)
        source = lax.rem(z + 4 - d, 4)
        cols = pl.ds(pl.multiple_of(p * width, 128), width)
        weights[d] = (
            remote(wu.at[mine, cols], wu_all.at[z, mine], sp.at[0, d - 1], rp.at[0, d - 1], peers[d]),
            remote(wq.at[p, mine], wq_all.at[z, mine], sp.at[1, d - 1], rp.at[1, d - 1], peers[d]),
        )
        for i, full in enumerate((wu_all, wq_all)):
            part = full.at[source, mine]
            for e in (1, 3, 2):
                spread_x[i, d, e] = remote(
                    part, part, sx.at[i, 3 * d + e - 4], rx.at[i, 3 * d + e - 4], x_peer[e]
                )
            spread_k[i, d] = remote(
                full.at[source], full.at[source], sf.at[i, d - 1], rf.at[i, d - 1], sibling
            )
    for i in range(2):

        @pl.when(k == i)
        def _():
            for d in (1, 3, 2):
                weights[d][i].start()

    cut = hid.shape[0] // 2
    parts = [pl.ds(0, cut), pl.ds(cut, cut)]
    ring = {}
    for i, (src, dst) in enumerate(((hid, h_all), (cot, c_all))):
        for n in range(2):
            ring[i, 1, n] = send(
                src.at[parts[n]], dst.at[z, parts[n]], so.at[i, 0, n], ro.at[i, 0, n], peers[1]
            )
            m = 1 - n
            ring[i, 3, m] = send(
                src.at[parts[m]], dst.at[z, parts[m]], so.at[i, 1, m], ro.at[i, 1, m], peers[3]
            )
    for d in (1, 2, 3):
        for i, (src, dst) in enumerate(((small, s_all), (pos, p_all), (place_of, o_all))):
            others.append(send(src, dst.at[z], ss.at[i, d - 1], rs.at[i, d - 1], peers[d]))
    h_all[z] = hid[...]
    c_all[z] = cot[...]
    s_all[z] = small[...]
    p_all[z] = pos[...]
    o_all[z] = place_of[...]
    wq_all[z] = wq[z]
    wu_all[z] = wu[:, pl.ds(pl.multiple_of(z * width, 128), width)]
    before, after = lax.rem(z + 3, 4), lax.rem(z + 1, 4)
    for i in range(2):

        @pl.when(k == i)
        def _():
            for d in (1, 3, 2):
                weights[d][i].wait_recv()
                for e in (1, 3, 2):
                    spread_x[i, d, e].start()

    for i, full in enumerate((h_all, c_all)):
        ring[i, 1, 0].wait_recv()
        part = full.at[before, parts[0]]
        others.append(send(part, part, ss.at[3 + i, 0], rs.at[3 + i, 0], peers[1]))
        ring[i, 3, 1].wait_recv()
        part = full.at[after, parts[1]]
        others.append(send(part, part, ss.at[3 + i, 1], rs.at[3 + i, 1], peers[3]))
    for i in range(2):
        ring[i, 1, 1].wait_recv()
        ring[i, 3, 0].wait_recv()
    for i in range(2):

        @pl.when(k == i)
        def _():
            for d in (1, 3, 2):
                for e in (1, 3, 2):
                    spread_x[i, d, e].wait_recv()
                spread_k[i, d].start()
            for d in (1, 3, 2):
                spread_k[1 - i, d].wait_recv()
                spread_k[i, d].wait_send()
                weights[d][i].wait_send()
                for e in (1, 3, 2):
                    spread_x[i, d, e].wait_send()

    for copy in others:
        copy.wait()
    for copy in ring.values():
        copy.wait_send()


def spread(hid, cot, w_qkv, wu, vectors, pos, place_of):
    rows = hid.shape[0]
    width = wu.shape[1] // 4
    return pl.pallas_call(
        spread_kernel,
        out_shape=(
            jax.ShapeDtypeStruct((4, rows, D), BF),
            jax.ShapeDtypeStruct((4, rows, D), BF),
            jax.ShapeDtypeStruct((4, wu.shape[0], 3 * HC), BF),
            jax.ShapeDtypeStruct((4, wu.shape[0], width), BF),
            jax.ShapeDtypeStruct((4, 16, HC), F32),
            jax.ShapeDtypeStruct((4,) + pos.shape, jnp.int32),
            jax.ShapeDtypeStruct((4,) + place_of.shape, jnp.int32),
        ),
        in_specs=vmem(13),
        out_specs=tuple(vmem(7)),
        scratch_shapes=[
            pltpu.VMEM((4, wu.shape[0], 3 * HC), BF),
            pltpu.VMEM((16, HC), F32),
            dma(2, 2, 2), dma(2, 2, 2), dma(2, 3), dma(2, 3), dma(2, 9), dma(2, 9),
            dma(2, 3), dma(2, 3),
            dma(5, 3), dma(5, 3),
        ],
        compiler_params=params(0),
    )(hid, cot, w_qkv, wu, *vectors, pos, place_of)


def dot(left, right):
    return jnp.dot(left, right, preferred_element_type=F32)


def dot_nt(left, right):
    return lax.dot_general(left, right, (((1,), (1,)), ((), ())), preferred_element_type=F32)


def dot_tn(left, right):
    return lax.dot_general(left, right, (((0,), (0,)), ((), ())), preferred_element_type=F32)


def normalize(flat):
    center = flat - jnp.mean(flat, axis=-1, keepdims=True)
    r = lax.rsqrt(jnp.mean(center * center, axis=-1, keepdims=True) + 1e-05)
    return center * r, r


def vector(s_all, i):
    return jnp.concatenate([s_all[p, i : i + 1] for p in range(4)], axis=1)


def swap(v, flag):
    return jnp.where(flag > 0, pltpu.roll(v, 64, 1), v)


def low_of(order, s, c):
    first = order[s, 0, 2 * c]
    return jnp.minimum(first, 63 - first)


def flip_of(order, s, c):
    return jnp.where(order[s, 0, 2 * c] >= 32, 1, 0)


def turned(v, cosine, sine):
    first, second = v[0:8], v[8:16]
    return jnp.concatenate(
        [first * cosine - second * sine, second * cosine + first * sine, v[16:]], axis=0
    )


def prepare_kernel(
    order, h_all, c_all, wq, wu, s_all, places, freqs, w_out, w_down, b_up,
    qkvd, normed, zpart, pack, small, cs, t_k, t_q, s_q, t_rows, s_rows,
):
    z = lax.axis_index("shard")
    c, y, x, k = spots()
    count = h_all.shape[1]
    lane = lax.broadcasted_iota(jnp.int32, (1, 128), 1)
    left = lane < 64

    def positions(s, low):
        near = places[s, :, pl.ds(pl.multiple_of(lax.div(low, 2) * 128, 128), 128)]
        far = places[s, :, pl.ds(pl.multiple_of((31 - lax.div(low, 2)) * 128, 128), 128)]
        odd = lax.rem(low, 2)
        both = jnp.where(odd > 0, jnp.where(left, far, near), jnp.where(left, near, far))
        return swap(both.astype(F32), odd)

    def tokens(first, second):
        return jnp.where(left, 64 * first + lane, 64 * second - 64 + lane).astype(F32)

    for s in range(4):
        angle = swap(positions(s, low_of(order, s, c)), flip_of(order, s, c)) * freqs[...]
        turns = jnp.floor(angle * (0.5 / math.pi) + 0.5)
        angle = angle - turns * 6.28125
        angle = angle - turns * 1.93500518798828125e-3
        angle = angle - turns * 3.01991598195675e-7
        cs[s, 0:8] = jnp.cos(angle)
        cs[s, 8:16] = jnp.sin(angle)
    for j in range(16):
        at = (j // 2 % 4) * 8 + (j % 2) * 4 + j // 8
        first, second = low_of(order, y, at), low_of(order, y, at + 2)
        t_k[:, 128 * j : 128 * j + 128] = tokens(first, second)
        t_k[:, 2048 + 128 * j : 2176 + 128 * j] = tokens(63 - second, 63 - first)
    for n in range(16):
        low = low_of(order, y, 2 * n + k)
        row = tokens(low, 63 - low)
        t_rows[n : n + 1] = row
        s_rows[n : n + 1] = row - positions(y, low)
    for rows, to in ((t_rows, t_q), (s_rows, s_q)):
        turn = rows[...].T
        for n in range(4):
            cols = [turn[:, 4 * n + m : 4 * n + m + 1] for m in range(4)]
            to[0, n] = jnp.concatenate([col[0:64] for col in cols], axis=0)
            to[1, n] = jnp.concatenate([cols[m][64:128] for m in (1, 0, 3, 2)], axis=0)

    xhat, _ = normalize(h_all[...].reshape(4 * count, D).astype(F32))
    cot = c_all[...].reshape(4 * count, D)
    n1 = (xhat * vector(s_all, 0) + vector(s_all, 1)).astype(BF)
    normed[...] = n1
    bias = []
    for t in range(3):
        piece = jnp.zeros((1, HC), F32)
        for p in range(4):
            n = 4 * t + p
            piece = piece + jnp.where(z == p, s_all[n // 3, 6 + n % 3 : 7 + n % 3], 0.0)
        bias.append(piece)
    joined = dot(n1, wq[...].reshape(D, 3 * HC)) + jnp.concatenate(bias, axis=1)
    d_mixed = dot_nt(w_out[...], cot)
    for s in range(4):
        jt = joined[count * s : count * s + count].T
        cosine, sine = cs[s, 0:8], cs[s, 8:16]
        for h in range(NH):
            at = HD * h
            rows = [
                turned(jt[HC + at : HC + at + HD], cosine, sine),
                jt[2 * HC + at : 2 * HC + at + HD],
                turned(jt[at : at + HD], cosine, sine),
                d_mixed[at : at + HD, count * s : count * s + count],
            ]
            qkvd[s, h] = swap(jnp.concatenate(rows, axis=0), flip_of(order, s, c)).astype(BF)

    n2 = (xhat * vector(s_all, 2) + vector(s_all, 3)).astype(BF)
    up = wu[...].reshape(D, wu.shape[2])
    hidden = dot(n2, up) + b_up[...].astype(F32).reshape(1, b_up.shape[0])
    rise = 0.5 * (1.0 + lax.erf(hidden * (1.0 / math.sqrt(2.0))))
    slope = rise + hidden * jnp.exp(-0.5 * hidden * hidden) * (1.0 / math.sqrt(2.0 * math.pi))
    active = (hidden * rise).astype(BF)
    d_up = (dot_nt(cot, w_down[...]) * slope).astype(BF)
    g_down = dot_tn(active, cot).astype(BF)
    for half in range(2):
        for i in range(3):
            at = 384 * half + 128 * i
            tiles = g_down[:, at : at + 128].reshape(16, 3, 16, 128)
            pack[:, half, 12 + 3 * i : 15 + 3 * i] = tiles
    g_up = dot_tn(n2, d_up).astype(BF)
    pack[12:16, :, 0:12] = jnp.zeros((4, 2, 12, 16, 128), BF)
    for p in range(4):
        for j in range(6):
            tiles = g_up[HC * p : HC * p + HC, 128 * j : 128 * j + 128].reshape(2, 2, 3, 16, 128)
            pack[2 * j : 2 * j + 2, :, 3 * p : 3 * p + 3] = tiles
    branch = dot(active, w_down[...]).astype(BF)
    d_two = dot_nt(d_up, up)
    for s in range(4):
        zpart[s, 0] = branch[count * s : count * s + count]
        zpart[s, 1] = d_two[count * s : count * s + count].astype(BF)
    small[...] = jnp.zeros_like(small)
    small[2:3] = jnp.sum(d_two * xhat, axis=0, keepdims=True)
    small[3:4] = jnp.sum(d_two, axis=0, keepdims=True)
    small[4:5] = jnp.sum(cot.astype(F32), axis=0, keepdims=True)
    small[5:6] = jnp.sum(d_up.astype(F32), axis=0, keepdims=True)


def prepare(order, h_all, c_all, wq, wu, s_all, places, freqs, w_out, w_down, b_up):
    count = h_all.shape[1]
    return pl.pallas_call(
        prepare_kernel,
        out_shape=(
            jax.ShapeDtypeStruct((4, NH, 4 * HD, count), BF),
            jax.ShapeDtypeStruct((4 * count, D), BF),
            jax.ShapeDtypeStruct((4, 2, count, D), BF),
            jax.ShapeDtypeStruct((16, 2, 21, 16, 128), BF),
            jax.ShapeDtypeStruct((8, D), F32),
            jax.ShapeDtypeStruct((4, 16, count), F32),
            jax.ShapeDtypeStruct((1, 4096), F32),
            jax.ShapeDtypeStruct((2, 4, 256, 1), F32),
            jax.ShapeDtypeStruct((2, 4, 256, 1), F32),
        ),
        in_specs=[pl.BlockSpec(memory_space=pltpu.SMEM)] + vmem(10),
        out_specs=tuple(vmem(9)),
        scratch_shapes=[pltpu.VMEM((16, 128), F32), pltpu.VMEM((16, 128), F32)],
        compiler_params=pltpu.CompilerParams(vmem_limit_bytes=LIMIT),
    )(order, h_all, c_all, wq, wu, s_all, places, freqs, w_out, w_down, b_up)


def attend_kernel(
    qkvd, t_k, t_q, s_q, zpart, pack, out, z_all, full,
    kv, qd, kt, dkv, qdt, oqt, s_buf, p_buf, dpart, got, ready,
    w_got, w_one, w_far, w_two, w_beyond, w_three, w_last,
    s_k, r_k, s_d, r_d, s_f, r_f, s_n, r_n, s_o, r_o, s_z, r_z,
    w_sc, w_rc, w_sa, w_ra, w_sb, w_rb, w_sz, w_rz, w_gb, w_hb, w_ga, w_ha, w_gc, w_hc,
):
    z = lax.axis_index("shard")
    c, y, x, k = spots()
    sibling = {"ctx": c + 1 - 2 * k}
    z_peer = [{"shard": lax.rem(z + d, 4)} for d in range(4)]
    a, b, a_peer, b_peer = plane(x, y, k)
    steps = [(dy, dx) for dy in range(4) for dx in range(4) if dy or dx]
    steps.sort(key=lambda s: min(s[0], 4 - s[0]) + min(s[1], 4 - s[1]))
    far_spot, far_peer = {}, {}
    for dy, dx in steps:
        ys, xs = lax.rem(y + dy, 4), lax.rem(x + dx, 4)
        far_spot[dy, dx] = (ys, xs)
        far_peer[dy, dx] = {"ctx": place(ys, xs, k)}
    greet(list(far_peer.values()) + z_peer[1:] + [sibling])
    busy = x < 3
    slot = y * 4 + x
    tail = []

    there = {}
    for dy, dx in steps:
        ys, xs = far_spot[dy, dx]
        n = 4 * dy + dx
        h = lax.rem(xs, 3)
        there[dy, dx] = [
            remote(
                qkvd.at[ys, h, pl.ds(0, 128)], kv.at[k * 16 + slot], s_k.at[n], r_k.at[n],
                far_peer[dy, dx],
            ),
            remote(
                qkvd.at[ys, h, pl.ds(128, 128)], qd.at[slot], s_d.at[n], r_d.at[n],
                far_peer[dy, dx],
            ),
        ]
    for i in range(2):
        for dy, dx in steps:

            @pl.when(far_spot[dy, dx][1] < 3)
            def _():
                there[dy, dx][i].start()

    @pl.when(busy)
    def _():
        kv[k * 16 + slot] = qkvd[y, lax.rem(x, 3), 0:128]
        qd[slot] = qkvd[y, lax.rem(x, 3), 128:]

    w_near, w_across, w_over, w_turn, w_out_b, w_out_a = {}, {}, {}, {}, {}, {}

    def w_core():
        for d in (1, 3, 2, 0):
            ap = lax.rem(b + d, 4)
            w_near[d] = send(pack.at[1 - k, ap], w_got.at[ap], w_sc.at[d], w_rc.at[d], sibling)

    def w_sum_core():
        for d in (1, 3, 2, 0):
            ap = lax.rem(a + d, 4)
            w_near[d].wait_recv()
            w_one[ap] = (pack[k, ap].astype(F32) + w_got[ap].astype(F32)).astype(BF)
            if d:
                w_across[d] = send(
                    w_one.at[ap], w_far.at[d - 1], w_sa.at[d - 1], w_ra.at[d - 1], a_peer[d]
                )

    def w_sum_a():
        for d in (1, 3, 2):
            w_across[d].wait_recv()
        for d in (1, 3, 2, 0):
            bp = lax.rem(b + d, 4)
            total = w_one[a, bp].astype(F32)
            for n in range(3):
                total = total + w_far[n, bp].astype(F32)
            w_two[bp] = total.astype(BF)
            if d:
                w_over[d] = send(
                    w_two.at[bp], w_beyond.at[d - 1], w_sb.at[d - 1], w_rb.at[d - 1], b_peer[d]
                )

    def w_sum_b():
        for d in (1, 3, 2):
            w_over[d].wait_recv()
        total = w_two[b].astype(F32)
        for n in range(3):
            total = total + w_beyond[n].astype(F32)
        w_three[...] = total.astype(BF)
        for d in (1, 3, 2):
            zp = lax.rem(z + d, 4)
            w_turn[d] = send(
                w_three.at[pl.ds(3 * zp, 3)], w_last.at[pl.ds(3 * z, 3)],
                w_sz.at[d - 1], w_rz.at[d - 1], z_peer[d],
            )
        w_last[pl.ds(3 * z, 3)] = w_three[pl.ds(3 * z, 3)]
        w_last[12:] = w_three[12:]

    def w_back_b():
        for d in (1, 3, 2):
            w_turn[d].wait()
        full[k, a, b] = w_last[...]
        for d in (1, 3, 2):
            w_out_b[d] = send(
                w_last, full.at[k, a, b], w_gb.at[d - 1], w_hb.at[d - 1], b_peer[d]
            )

    def w_back_a():
        for d in (1, 3, 2):
            w_out_b[d].wait()
        for d in (1, 3, 2):
            w_out_a[d] = send(
                full.at[k, a], full.at[k, a], w_ga.at[d - 1], w_ha.at[d - 1], a_peer[d]
            )
        tail.append(send(full.at[k, a], full.at[k, a], w_gc.at[0], w_hc.at[0], sibling))

    def w_back_core():
        for d in (1, 3, 2):
            w_out_a[d].wait_recv()
            ap = lax.rem(a + 4 - d, 4)
            tail.append(send(full.at[k, ap], full.at[k, ap], w_gc.at[d], w_hc.at[d], sibling))

    left = lax.broadcasted_iota(jnp.int32, (128, 128), 1) < 64
    mine, others = pl.ds(k * 16, 16), pl.ds((1 - k) * 16, 16)
    forward = remote(kv.at[mine], kv.at[mine], s_f.at[0], r_f.at[0], sibling)

    def sort():
        def step(j, carry):
            one = kv[2 * j].astype(F32)
            two = pltpu.roll(kv[2 * j + 1].astype(F32), 64, 1)
            kt[:, pl.ds(pl.multiple_of(j * 128, 128), 128)] = jnp.where(left, one, two).astype(BF)
            kt[:, pl.ds(pl.multiple_of((16 + j) * 128, 128), 128)] = jnp.where(left, two, one).astype(BF)
            return carry

        lax.fori_loop(0, 16, step, 0)
        dkv[...] = jnp.zeros_like(dkv)

    def queries(n):
        for m in range(2):
            one = qd[4 * n + 2 * m].astype(F32)
            two = pltpu.roll(qd[4 * n + 2 * m + 1].astype(F32), 64, 1)
            cols = slice(128 * m, 128 * m + 128)
            qdt[0, :, cols] = jnp.where(left, one, two)
            qdt[1, :, cols] = jnp.where(left, two, one)

    def answers(n):
        for m in range(2):
            cols = slice(128 * m, 128 * m + 128)
            low, high = oqt[0, :, cols], oqt[1, :, cols]
            ready[1, 4 * n + 2 * m] = jnp.where(left, low, high).astype(BF)
            ready[1, 4 * n + 2 * m + 1] = pltpu.roll(jnp.where(left, high, low), 64, 1).astype(BF)

    def unsort():
        def step(j, carry):
            low = dkv[:, pl.ds(pl.multiple_of(j * 128, 128), 128)]
            high = dkv[:, pl.ds(pl.multiple_of((16 + j) * 128, 128), 128)]
            dpart[2 * j] = jnp.where(left, low, high).astype(BF)
            dpart[2 * j + 1] = pltpu.roll(jnp.where(left, high, low), 64, 1).astype(BF)
            return carry

        lax.fori_loop(0, 16, step, 0)

    keys, values = slice(0, HD), slice(HD, 2 * HD)

    def one_tile(tile, n):
        q_t = qdt[tile, keys, :] * 0.125
        d_t = qdt[tile, values, :]
        q_n, d_n = q_t.T.astype(BF), d_t.T.astype(BF)
        q_t, d_t = q_t.astype(BF), d_t.astype(BF)
        first_key, last_key = s_q[tile, n], t_q[tile, n]
        top = jnp.full((256, 128), -1e30, F32)
        total = jnp.zeros((256, 128), F32)
        inner = jnp.zeros((256, 128), F32)
        for i in range(tile + 1):
            at = slice(i * CHUNK, i * CHUNK + CHUNK)
            s = dot(q_n, kt[keys, at])
            key = t_k[:, at]
            s = jnp.where((key >= first_key) & (key <= last_key), s, -1e30)
            s_buf[:, at] = s
            dp = dot(d_n, kt[values, at])
            p_buf[:, at] = dp
            new = top
            for m in range(CHUNK // 128):
                new = jnp.maximum(new, s[:, 128 * m : 128 * m + 128])
            scale = jnp.exp(top - new)
            total, inner, top = total * scale, inner * scale, new
            for m in range(CHUNK // 128):
                e = jnp.exp(s[:, 128 * m : 128 * m + 128] - new)
                total = total + e
                inner = inner + e * dp[:, 128 * m : 128 * m + 128]
        most = jnp.max(top, axis=1, keepdims=True)
        scale = jnp.exp(top - most)
        over = 1.0 / jnp.sum(total * scale, axis=1, keepdims=True)
        inner = jnp.sum(inner * scale, axis=1, keepdims=True) * over
        out_t = jnp.zeros((HD, 256), F32)
        dq_t = jnp.zeros((HD, 256), F32)
        for i in range(tile + 1):
            at = slice(i * CHUNK, i * CHUNK + CHUNK)
            p = jnp.exp(s_buf[:, at] - most) * over
            pb = p.astype(BF)
            ds = (p * (p_buf[:, at] - inner)).astype(BF)
            out_t = out_t + dot_nt(kt[values, at], pb)
            dq_t = dq_t + dot_nt(kt[keys, at], ds)
            dkv[values, at] += dot(d_t, pb)
            dkv[keys, at] += dot(q_t, ds)
        oqt[tile, keys, :] = out_t
        oqt[tile, values, :] = dq_t * 0.125

    home = {}
    h = lax.rem(x, 3)
    for dy, dx in steps:
        ys, xs = far_spot[dy, dx]
        n = 4 * dy + dx
        home[dy, dx] = [
            remote(
                ready.at[i, 4 * ys + xs], out.at[y, h, pl.ds(128 * i, 128)],
                s_o.at[i, n], r_o.at[i, n], far_peer[dy, dx],
            )
            for i in range(2)
        ]

    w_core()
    for d in (1, 3, 2):
        zp = lax.rem(z + d, 4)
        tail.append(send(zpart.at[zp], z_all.at[z], s_z.at[d - 1], r_z.at[d - 1], z_peer[d]))
    z_all[z] = zpart[z]

    @pl.when(busy)
    def _():
        for dy, dx in steps:
            there[dy, dx][0].wait_recv()
        forward.start()
        for dy, dx in steps:
            there[dy, dx][1].wait_recv()
        forward.wait()
        sort()

    def nothing():
        pass

    points = (
        (w_sum_core, nothing), (nothing, w_sum_a), (w_sum_b, w_back_b), (w_back_a, nothing)
    )
    for n in range(4):

        @pl.when(busy)
        def _():
            queries(n)
            one_tile(0, n)

        points[n][0]()

        @pl.when(busy)
        def _():
            one_tile(1, n)
            answers(n)

        points[n][1]()

    swap_out = remote(dpart.at[others], got, s_n.at[0], r_n.at[0], sibling)

    @pl.when(busy)
    def _():
        unsort()
        swap_out.start()
        for dy, dx in steps:
            home[dy, dx][1].start()
        out[y, h, 128:] = ready[1, slot]
        swap_out.wait()
        for i in range(4):
            own = dpart[pl.ds(k * 16 + 4 * i, 4)].astype(F32)
            ready[0, 4 * i : 4 * i + 4] = (own + got[4 * i : 4 * i + 4].astype(F32)).astype(BF)
        for dy, dx in steps:
            home[dy, dx][0].start()
        out[y, h, 0:128] = ready[0, slot]

    w_back_core()
    for dy, dx in steps:
        @pl.when(lax.rem(x + 4 - dx, 4) < 3)
        def _():
            for i in range(2):
                home[dy, dx][i].wait_recv()

        @pl.when(far_spot[dy, dx][1] < 3)
        def _():
            for i in range(2):
                there[dy, dx][i].wait_send()

    @pl.when(busy)
    def _():
        for dy, dx in steps:
            for i in range(2):
                home[dy, dx][i].wait_send()

    for copy in tail:
        copy.wait()
    for group in (w_near, w_across, w_over, w_out_a):
        for copy in group.values():
            copy.wait_send()


def attend(qkvd, t_k, t_q, s_q, zpart, pack):
    square = (128, 128)
    tiles = pack.shape[3:]
    return pl.pallas_call(
        attend_kernel,
        out_shape=(
            jax.ShapeDtypeStruct(qkvd.shape, BF),
            jax.ShapeDtypeStruct(zpart.shape, BF),
            jax.ShapeDtypeStruct(pack.shape, BF),
        ),
        in_specs=vmem(6),
        out_specs=tuple(vmem(3)),
        scratch_shapes=[
            pltpu.VMEM((32,) + square, BF),
            pltpu.VMEM((16,) + square, BF),
            pltpu.VMEM((128, 4096), BF),
            pltpu.VMEM((128, 4096), F32),
            pltpu.VMEM((2, 128, 256), F32),
            pltpu.VMEM((2, 128, 256), F32),
            pltpu.VMEM((256, 4096), F32),
            pltpu.VMEM((256, 4096), F32),
            pltpu.VMEM((32,) + square, BF),
            pltpu.VMEM((16,) + square, BF),
            pltpu.VMEM((2, 16) + square, BF),
            pltpu.VMEM((4, 4) + tiles, BF),
            pltpu.VMEM((4, 4) + tiles, BF),
            pltpu.VMEM((3, 4) + tiles, BF),
            pltpu.VMEM((4,) + tiles, BF),
            pltpu.VMEM((3,) + tiles, BF),
            pltpu.VMEM(tiles, BF),
            pltpu.VMEM(tiles, BF),
            dma(16), dma(16), dma(16), dma(16), dma(1), dma(1), dma(1), dma(1),
            dma(2, 16), dma(2, 16), dma(3), dma(3),
            dma(4), dma(4), dma(3), dma(3), dma(3), dma(3), dma(3), dma(3),
            dma(3), dma(3), dma(3), dma(3), dma(4), dma(4),
        ],
        compiler_params=params(1),
    )(qkvd, t_k, t_q, s_q, zpart, pack)


def sum_kernel(
    pack, zpart, small, full, z_all, small_all,
    got, one, far_a, two, far_b, three, last, s1, s2, s3, s4,
    sz, rz, sc, rc, sa, ra, sb, rb, st, rt, gb, hb, ga, ha, gc, hc, sm, rm,
):
    z = lax.axis_index("shard")
    c, y, x, k = spots()
    sibling = {"ctx": c + 1 - 2 * k}
    z_peer = [{"shard": lax.rem(z + d, 4)} for d in range(4)]
    a, b, a_peer, b_peer = plane(x, y, k)
    greet(a_peer[1:] + b_peer[1:] + z_peer[1:] + [sibling])
    near = {}
    for d in (1, 3, 2, 0):
        ap = lax.rem(b + d, 4)
        near[d] = send(pack.at[1 - k, ap], got.at[ap], sc.at[d], rc.at[d], sibling)
    tail = [send(small, s1, sm.at[0], rm.at[0], sibling)]
    for d in (1, 3, 2):
        zp = lax.rem(z + d, 4)
        tail.append(send(zpart.at[zp], z_all.at[z], sz.at[d - 1], rz.at[d - 1], z_peer[d]))
    z_all[z] = zpart[z]
    across = {}
    for d in (1, 3, 2, 0):
        ap = lax.rem(a + d, 4)
        near[d].wait_recv()
        for n in range(4):
            both = pack[k, ap, n].astype(F32) + got[ap, n].astype(F32)
            one[ap, n] = both.astype(BF)
        if d:
            across[d] = send(one.at[ap], far_a.at[d - 1], sa.at[d - 1], ra.at[d - 1], a_peer[d])
    tail[0].wait()
    s2[0] = small[...] + s1[...]
    small_a = [send(s2.at[0], s2.at[d], sm.at[d], rm.at[d], a_peer[d]) for d in (1, 2, 3)]
    for d in (1, 3, 2):
        across[d].wait_recv()
    beyond = {}
    for d in (1, 3, 2, 0):
        bp = lax.rem(b + d, 4)
        total = one[a, bp].astype(F32)
        for n in range(3):
            total = total + far_a[n, bp].astype(F32)
        two[bp] = total.astype(BF)
        if d:
            beyond[d] = send(two.at[bp], far_b.at[d - 1], sb.at[d - 1], rb.at[d - 1], b_peer[d])
    for copy in small_a:
        copy.wait()
    s3[0] = (s2[0] + s2[1]) + (s2[2] + s2[3])
    small_b = [send(s3.at[0], s3.at[d], sm.at[3 + d], rm.at[3 + d], b_peer[d]) for d in (1, 2, 3)]
    for d in (1, 3, 2):
        beyond[d].wait_recv()
    total = two[b].astype(F32)
    for n in range(3):
        total = total + far_b[n].astype(F32)
    three[...] = total.astype(BF)
    turned = []
    for d in (1, 3, 2):
        zp = lax.rem(z + d, 4)
        turned.append(
            send(
                three.at[pl.ds(2 * zp, 2)], last.at[pl.ds(2 * z, 2)],
                st.at[d - 1], rt.at[d - 1], z_peer[d],
            )
        )
    last[pl.ds(2 * z, 2)] = three[pl.ds(2 * z, 2)]
    last[8:] = three[8:]
    for copy in small_b:
        copy.wait()
    s4[...] = (s3[0] + s3[1]) + (s3[2] + s3[3])
    for d in (1, 3, 2):
        tail.append(send(s4, small_all.at[z], sm.at[6 + d], rm.at[6 + d], z_peer[d]))
    small_all[z] = s4[...]
    for copy in turned:
        copy.wait()
    full[k, a, b] = last[...]
    out_b = {}
    for d in (1, 3, 2):
        out_b[d] = send(last, full.at[k, a, b], gb.at[d - 1], hb.at[d - 1], b_peer[d])
    for d in (1, 3, 2):
        out_b[d].wait()
    out_a = {}
    for d in (1, 3, 2):
        out_a[d] = send(full.at[k, a], full.at[k, a], ga.at[d - 1], ha.at[d - 1], a_peer[d])
    tail.append(send(full.at[k, a], full.at[k, a], gc.at[0], hc.at[0], sibling))
    for d in (1, 3, 2):
        out_a[d].wait_recv()
        ap = lax.rem(a + 4 - d, 4)
        tail.append(send(full.at[k, ap], full.at[k, ap], gc.at[d], hc.at[d], sibling))
    for copy in tail[1:]:
        copy.wait()
    for d in (1, 2, 3):
        out_a[d].wait_send()
        across[d].wait_send()
        beyond[d].wait_send()
    for d in range(4):
        near[d].wait_send()


def sums(pack, zpart, small):
    tiles = pack.shape[3:]
    return pl.pallas_call(
        sum_kernel,
        out_shape=(
            jax.ShapeDtypeStruct(pack.shape, BF),
            jax.ShapeDtypeStruct(zpart.shape, BF),
            jax.ShapeDtypeStruct((4,) + small.shape, F32),
        ),
        in_specs=vmem(3),
        out_specs=tuple(vmem(3)),
        scratch_shapes=[
            pltpu.VMEM((4, 4) + tiles, BF),
            pltpu.VMEM((4, 4) + tiles, BF),
            pltpu.VMEM((3, 4) + tiles, BF),
            pltpu.VMEM((4,) + tiles, BF),
            pltpu.VMEM((3,) + tiles, BF),
            pltpu.VMEM(tiles, BF),
            pltpu.VMEM(tiles, BF),
            pltpu.VMEM(small.shape, F32),
            pltpu.VMEM((4,) + small.shape, F32),
            pltpu.VMEM((4,) + small.shape, F32),
            pltpu.VMEM(small.shape, F32),
            dma(3), dma(3), dma(4), dma(4), dma(3), dma(3), dma(3), dma(3), dma(3), dma(3),
            dma(3), dma(3), dma(3), dma(3), dma(4), dma(4), dma(10), dma(10),
        ],
        compiler_params=params(3),
    )(pack, zpart, small)


def after_kernel(order, ret, h_all, c_all, normed, wq, w_out, cs, given, zpart, pack, small, dj, mt):
    count = h_all.shape[1]
    for s in range(4):
        cosine, sine = cs[s, 0:8], -cs[s, 8:16]
        flip = flip_of(order, s, lax.axis_index("ctx"))
        r = [swap(ret[s, h].astype(F32), flip) for h in range(NH)]
        rows = [turned(r[h][3 * HD :], cosine, sine) for h in range(NH)]
        rows += [turned(r[h][0:HD], cosine, sine) for h in range(NH)]
        rows += [r[h][HD : 2 * HD] for h in range(NH)]
        dj[count * s : count * s + count] = jnp.concatenate(rows, axis=0).T.astype(BF)
        for h in range(NH):
            mt[HD * h : HD * h + HD, count * s : count * s + count] = r[h][2 * HD : 3 * HD].astype(BF)
    cot = c_all[...].reshape(4 * count, D)
    xhat, _ = normalize(h_all[...].reshape(4 * count, D).astype(F32))
    d_one = dot_nt(dj[...], wq[...].reshape(D, 3 * HC))
    branch = dot(mt[...].astype(F32).T.astype(BF), w_out[...])
    for s in range(4):
        zpart[s, 0] = branch[count * s : count * s + count].astype(BF)
        zpart[s, 1] = d_one[count * s : count * s + count].astype(BF)
    small[...] = given[...]
    small[0:1] = jnp.sum(d_one * xhat, axis=0, keepdims=True)
    small[1:2] = jnp.sum(d_one, axis=0, keepdims=True)
    small[6:7, 0 : 3 * HC] = jnp.sum(dj[...].astype(F32), axis=0, keepdims=True)
    pack[24:32] = jnp.zeros((8,) + pack.shape[1:], BF)
    g = dot_tn(normed[...], dj[...])
    for p in range(4):
        mine = g[HC * p : HC * p + HC]
        for j in range(4):
            tiles = mine[:, 128 * j : 128 * j + 128].astype(BF).reshape(6, 2, 16, 128)
            pack[6 * j : 6 * j + 6, 2 * p : 2 * p + 2] = tiles
        rest = jnp.concatenate([mine[: HC // 2, 512:], mine[HC // 2 :, 512:]], axis=1)
        pack[24:27, 2 * p : 2 * p + 2] = rest.astype(BF).reshape(3, 2, 16, 128)
    g = dot(mt[...], cot)
    for j in range(6):
        tiles = g[:, 128 * j : 128 * j + 128].astype(BF).reshape(4, 3, 16, 128)
        pack[4 * j : 4 * j + 4, 8:11] = tiles


def after(order, ret, h_all, c_all, normed, wq, w_out, cs, given):
    count = h_all.shape[1]
    return pl.pallas_call(
        after_kernel,
        out_shape=(
            jax.ShapeDtypeStruct((4, 2, count, D), BF),
            jax.ShapeDtypeStruct((32, 11, 16, 128), BF),
            jax.ShapeDtypeStruct((8, D), F32),
        ),
        in_specs=[pl.BlockSpec(memory_space=pltpu.SMEM)] + vmem(8),
        out_specs=tuple(vmem(3)),
        scratch_shapes=[pltpu.VMEM((4 * count, 3 * HC), BF), pltpu.VMEM((HC, 4 * count), BF)],
        compiler_params=pltpu.CompilerParams(vmem_limit_bytes=LIMIT),
    )(order, ret, h_all, c_all, normed, wq, w_out, cs, given)


def finish_kernel(
    hid, cot, z_one, z_two, s_all, full, small_all, feed,
    out, grad, g_qkv, g_out, g_up, g_down, one_g, one_b, two_g, two_b, g_bqkv, g_bout, g_bup,
):
    z = lax.axis_index("shard")
    branch, d_one, d_two = 0.0, 0.0, 0.0
    for p in range(4):
        branch = branch + (z_one[p, 0].astype(F32) + z_two[p, 0].astype(F32))
        d_one = d_one + z_one[p, 1].astype(F32)
        d_two = d_two + z_two[p, 1].astype(F32)
    flat = hid[...].astype(F32)
    xhat, r = normalize(flat)
    out[...] = (flat + branch + vector(s_all, 4) + vector(s_all, 5)).astype(BF)
    g = d_one * vector(s_all, 0) + d_two * vector(s_all, 2)
    inner = jnp.mean(g * xhat, axis=-1, keepdims=True)
    grad[...] = cot[...].astype(F32) + r * (g - jnp.mean(g, axis=-1, keepdims=True) - xhat * inner)
    planes = []
    for p in range(4):
        cols = [full[6 * j : 6 * j + 6, 2 * p : 2 * p + 2].reshape(HC, 128) for j in range(4)]
        rest = full[24:27, 2 * p : 2 * p + 2].reshape(HC // 2, 128).astype(F32)
        rest = jnp.concatenate([rest[:, :64], rest[:, 64:]], axis=0)
        planes.append(jnp.concatenate([col.astype(F32) for col in cols] + [rest], axis=1))
    for t in range(3):
        g_qkv[:, D * t : D * t + D] = jnp.concatenate(
            [plane[:, HC * t : HC * t + HC] for plane in planes], axis=1
        )
    for j in range(6):
        tiles = full[4 * j : 4 * j + 4, 8:11].reshape(HC, 128)
        g_out[:, 128 * j : 128 * j + 128] = tiles.astype(F32)
    total = (small_all[0] + small_all[1]) + (small_all[2] + small_all[3])
    own = small_all[z]
    rows = jnp.concatenate([total[0:4], own[4:5]], axis=0)
    piece = jnp.zeros((5, HC), F32)
    for p in range(4):
        piece = piece + jnp.where(z == p, rows[:, HC * p : HC * p + HC], 0.0)
    for i, ref in enumerate((one_g, one_b, two_g, two_b, g_bout)):
        ref[...] = piece[i : i + 1].reshape(HC)
    pieces = []
    for i in range(3):
        piece = jnp.zeros((1, HC), F32)
        for p in range(4):
            n = 3 * p + i
            at = HC * (n // 4)
            piece = piece + jnp.where(z == p, small_all[n % 4, 6:7, at : at + HC], 0.0)
        pieces.append(piece)
    g_bqkv[...] = jnp.concatenate(pieces, axis=1).reshape(3 * HC)
    g_bup[...] = own[5:6].reshape(g_bup.shape)
    for half in range(2):
        for i in range(3):
            tiles = feed[:, half, 12 + 3 * i : 15 + 3 * i].reshape(D, 128)
            at = 384 * half + 128 * i
            g_down[:, at : at + 128] = tiles.astype(F32)
    for p in range(4):
        for j in range(6):
            tiles = feed[2 * j : 2 * j + 2, :, 3 * p : 3 * p + 3].reshape(HC, 128)
            g_up[:, D * p + 128 * j : D * p + 128 * j + 128] = tiles.astype(F32)


def finish(hid, cot, z_one, z_two, s_all, full, small_all, feed):
    return pl.pallas_call(
        finish_kernel,
        out_shape=(
            jax.ShapeDtypeStruct(hid.shape, BF),
            jax.ShapeDtypeStruct(hid.shape, F32),
            jax.ShapeDtypeStruct((HC, 3 * D), F32),
            jax.ShapeDtypeStruct((HC, D), F32),
            jax.ShapeDtypeStruct((HC, 4 * D), F32),
            jax.ShapeDtypeStruct((D, D), F32),
            jax.ShapeDtypeStruct((HC,), F32),
            jax.ShapeDtypeStruct((HC,), F32),
            jax.ShapeDtypeStruct((HC,), F32),
            jax.ShapeDtypeStruct((HC,), F32),
            jax.ShapeDtypeStruct((3 * HC,), F32),
            jax.ShapeDtypeStruct((HC,), F32),
            jax.ShapeDtypeStruct((D,), F32),
        ),
        in_specs=vmem(8),
        out_specs=tuple(vmem(13)),
        compiler_params=pltpu.CompilerParams(vmem_limit_bytes=LIMIT),
    )(hid, cot, z_one, z_two, s_all, full, small_all, feed)


def local(
    hidden, ln1_gain, ln1_bias, ln2_gain, ln2_bias, w_qkv, b_qkv, w_out, b_out, w_up, b_up,
    w_down, b_down, block_order, positions, cotangent,
):
    vectors = (ln1_gain, ln1_bias, ln2_gain, ln2_bias, b_out, b_down, b_qkv)
    h_all, c_all, wq, wu, s_all, p_all, o_all = spread(
        hidden, cotangent, w_qkv, w_up, vectors, positions, block_order
    )

    freqs = jnp.power(10000.0, -jnp.arange(0, ROT, 2, dtype=F32) / ROT).reshape(8, 1)
    qkvd, normed, zpart_two, feed_pack, small, cs, t_k, t_q, s_q = prepare(
        o_all, h_all, c_all, wq, wu, s_all, p_all, freqs, w_out, w_down, b_up
    )
    returned, z_two, feed = attend(
        qkvd, t_k, t_q, s_q, zpart_two, feed_pack.reshape(2, 4, 4, 21, 16, 128)
    )
    zpart_one, pack, small = after(o_all, returned, h_all, c_all, normed, wq, w_out, cs, small)
    full, z_one, small_all = sums(pack.reshape(2, 4, 4, 11, 16, 128), zpart_one, small)
    (
        output, grad_input, grad_qkv, grad_out, grad_up, grad_down, one_g, one_b, two_g, two_b,
        grad_bqkv, grad_bout, grad_bup,
    ) = finish(
        hidden, cotangent, z_one, z_two, s_all, full.reshape(32, 11, 16, 128), small_all,
        feed.reshape(16, 2, 21, 16, 128),
    )
    return (
        output, grad_input, one_g, one_b, two_g, two_b, grad_qkv, grad_bqkv, grad_out, grad_bout,
        grad_up, grad_bup, grad_down, grad_bout,
    )


def solution(mesh):
    tokens, vector, matrix = P(("shard", "ctx"), None), P("shard"), P("shard", None)
    return jax.shard_map(
        local,
        mesh=mesh,
        in_specs=(
            tokens, vector, vector, vector, vector, matrix, vector, matrix, vector, matrix, vector,
            matrix, vector, matrix, matrix, tokens,
        ),
        out_specs=(
            tokens, tokens, vector, vector, vector, vector, matrix, vector, matrix, vector, matrix,
            vector, matrix, vector,
        ),
        check_vma=False,
    )
```

```python
import functools
import math

import jax
import jax.numpy as jnp
import numpy as np
from jax import lax
from jax.experimental import pallas as pl
from jax.experimental.pallas import tpu as pltpu
from jax.sharding import PartitionSpec as P

HD = 64
ROT = 16
D = 768
NH = 3
HC = NH * HD
CHUNK = 2048
MESH = pl.DeviceIdType.MESH
BF = jnp.bfloat16
F32 = jnp.float32
LIMIT = 56 * 1024 * 1024


def vmem(count):
    return [pl.BlockSpec(memory_space=pltpu.VMEM)] * count


def spots():
    c = lax.axis_index("ctx")
    return c, lax.div(c, 8), lax.rem(lax.div(c, 2), 4), lax.rem(c, 2)


def place(y, x, k):
    return y * 8 + x * 2 + k


def plane(x, y, k):
    a = x + k * (y - x)
    b = y + k * (x - y)
    a_peer, b_peer = [], []
    for d in range(4):
        ax, by = lax.rem(a + d, 4), lax.rem(b + d, 4)
        a_peer.append({"ctx": place(b + k * (ax - b), ax + k * (b - ax), k)})
        b_peer.append({"ctx": place(by + k * (a - by), a + k * (by - a), k)})
    return a, b, a_peer, b_peer


def remote(src, dst, send_sem, recv_sem, where):
    return pltpu.make_async_remote_copy(
        src_ref=src,
        dst_ref=dst,
        send_sem=send_sem,
        recv_sem=recv_sem,
        device_id=where,
        device_id_type=MESH,
    )


def send(src, dst, send_sem, recv_sem, where):
    copy = remote(src, dst, send_sem, recv_sem, where)
    copy.start()
    return copy


def greet(peers):
    barrier = pltpu.get_barrier_semaphore()
    for peer in peers:
        pl.semaphore_signal(barrier, inc=1, device_id=peer, device_id_type=MESH)
    pl.semaphore_wait(barrier, len(peers))


def dma(*dims):
    return pltpu.SemaphoreType.DMA(dims)


def params(ident):
    return pltpu.CompilerParams(
        collective_id=ident, has_side_effects=True, vmem_limit_bytes=LIMIT
    )


def spread_kernel(
    hid, cot, w_qkv, wu, g1, b1, g2, b2, bo, bd, bq, pos, place_of,
    h_all, c_all, wq_all, wu_all, s_all, p_all, o_all,
    wq, small, so, ro, sp, rp, sx, rx, sf, rf, ss, rs,
):
    z = lax.axis_index("shard")
    c, y, x, k = spots()
    sibling = {"ctx": c + 1 - 2 * k}
    peers = [{"shard": lax.rem(z + d, 4)} for d in range(4)]
    greet(
        peers[1:] + [sibling] + [{"ctx": place(y, lax.rem(x + d, 4), k)} for d in (1, 2, 3)]
    )
    rows = wu.shape[0]
    quarter = rows // 4
    width = wu_all.shape[2]
    for p in range(4):
        wq[p] = jnp.concatenate(
            [w_qkv[:, D * t + HC * p : D * t + HC * p + HC] for t in range(3)], axis=1
        )
    small[...] = jnp.zeros_like(small)
    for i, ref in enumerate((g1, b1, g2, b2, bo, bd)):
        small[i : i + 1] = ref[...].astype(F32).reshape(1, HC)
    bias = bq[...].astype(F32).reshape(1, 3 * HC)
    for i in range(3):
        small[6 + i : 7 + i] = bias[:, HC * i : HC * i + HC]

    mine = pl.ds(pl.multiple_of(x * quarter, 16), quarter)
    x_peer = [{"ctx": place(y, lax.rem(x + d, 4), k)} for d in range(4)]
    weights, spread_x, spread_k, others = {}, {}, {}, []
    for d in (1, 3, 2):
        p = lax.rem(z + d, 4)
        source = lax.rem(z + 4 - d, 4)
        cols = pl.ds(pl.multiple_of(p * width, 128), width)
        weights[d] = (
            remote(wu.at[mine, cols], wu_all.at[z, mine], sp.at[0, d - 1], rp.at[0, d - 1], peers[d]),
            remote(wq.at[p, mine], wq_all.at[z, mine], sp.at[1, d - 1], rp.at[1, d - 1], peers[d]),
        )
        for i, full in enumerate((wu_all, wq_all)):
            part = full.at[source, mine]
            for e in (1, 3, 2):
                spread_x[i, d, e] = remote(
                    part, part, sx.at[i, 3 * d + e - 4], rx.at[i, 3 * d + e - 4], x_peer[e]
                )
            spread_k[i, d] = remote(
                full.at[source], full.at[source], sf.at[i, d - 1], rf.at[i, d - 1], sibling
            )
    for i in range(2):

        @pl.when(k == i)
        def _():
            for d in (1, 3, 2):
                weights[d][i].start()

    cut = hid.shape[0] // 2
    parts = [pl.ds(0, cut), pl.ds(cut, cut)]
    ring = {}
    for i, (src, dst) in enumerate(((hid, h_all), (cot, c_all))):
        for n in range(2):
            ring[i, 1, n] = send(
                src.at[parts[n]], dst.at[z, parts[n]], so.at[i, 0, n], ro.at[i, 0, n], peers[1]
            )
            m = 1 - n
            ring[i, 3, m] = send(
                src.at[parts[m]], dst.at[z, parts[m]], so.at[i, 1, m], ro.at[i, 1, m], peers[3]
            )
    for d in (1, 2, 3):
        for i, (src, dst) in enumerate(((small, s_all), (pos, p_all), (place_of, o_all))):
            others.append(send(src, dst.at[z], ss.at[i, d - 1], rs.at[i, d - 1], peers[d]))
    h_all[z] = hid[...]
    c_all[z] = cot[...]
    s_all[z] = small[...]
    p_all[z] = pos[...]
    o_all[z] = place_of[...]
    wq_all[z] = wq[z]
    wu_all[z] = wu[:, pl.ds(pl.multiple_of(z * width, 128), width)]
    before, after = lax.rem(z + 3, 4), lax.rem(z + 1, 4)
    for i in range(2):

        @pl.when(k == i)
        def _():
            for d in (1, 3, 2):
                weights[d][i].wait_recv()
                for e in (1, 3, 2):
                    spread_x[i, d, e].start()

    for i, full in enumerate((h_all, c_all)):
        ring[i, 1, 0].wait_recv()
        part = full.at[before, parts[0]]
        others.append(send(part, part, ss.at[3 + i, 0], rs.at[3 + i, 0], peers[1]))
        ring[i, 3, 1].wait_recv()
        part = full.at[after, parts[1]]
        others.append(send(part, part, ss.at[3 + i, 1], rs.at[3 + i, 1], peers[3]))
    for i in range(2):
        ring[i, 1, 1].wait_recv()
        ring[i, 3, 0].wait_recv()
    for i in range(2):

        @pl.when(k == i)
        def _():
            for d in (1, 3, 2):
                for e in (1, 3, 2):
                    spread_x[i, d, e].wait_recv()
                spread_k[i, d].start()
            for d in (1, 3, 2):
                spread_k[1 - i, d].wait_recv()
                spread_k[i, d].wait_send()
                weights[d][i].wait_send()
                for e in (1, 3, 2):
                    spread_x[i, d, e].wait_send()

    for copy in others:
        copy.wait()
    for copy in ring.values():
        copy.wait_send()


def spread(hid, cot, w_qkv, wu, vectors, pos, place_of):
    rows = hid.shape[0]
    width = wu.shape[1] // 4
    return pl.pallas_call(
        spread_kernel,
        out_shape=(
            jax.ShapeDtypeStruct((4, rows, D), BF),
            jax.ShapeDtypeStruct((4, rows, D), BF),
            jax.ShapeDtypeStruct((4, wu.shape[0], 3 * HC), BF),
            jax.ShapeDtypeStruct((4, wu.shape[0], width), BF),
            jax.ShapeDtypeStruct((4, 16, HC), F32),
            jax.ShapeDtypeStruct((4,) + pos.shape, jnp.int32),
            jax.ShapeDtypeStruct((4,) + place_of.shape, jnp.int32),
        ),
        in_specs=vmem(13),
        out_specs=tuple(vmem(7)),
        scratch_shapes=[
            pltpu.VMEM((4, wu.shape[0], 3 * HC), BF),
            pltpu.VMEM((16, HC), F32),
            dma(2, 2, 2), dma(2, 2, 2), dma(2, 3), dma(2, 3), dma(2, 9), dma(2, 9),
            dma(2, 3), dma(2, 3),
            dma(5, 3), dma(5, 3),
        ],
        compiler_params=params(0),
    )(hid, cot, w_qkv, wu, *vectors, pos, place_of)


def dot(left, right):
    return jnp.dot(left, right, preferred_element_type=F32)


def dot_nt(left, right):
    return lax.dot_general(left, right, (((1,), (1,)), ((), ())), preferred_element_type=F32)


def dot_tn(left, right):
    return lax.dot_general(left, right, (((0,), (0,)), ((), ())), preferred_element_type=F32)


def normalize(flat):
    center = flat - jnp.mean(flat, axis=-1, keepdims=True)
    r = lax.rsqrt(jnp.mean(center * center, axis=-1, keepdims=True) + 1e-05)
    return center * r, r


def vector(s_all, i):
    return jnp.concatenate([s_all[p, i : i + 1] for p in range(4)], axis=1)


def swap(v, flag):
    return jnp.where(flag > 0, pltpu.roll(v, 64, 1), v)


def low_of(order, s, c):
    first = order[s, 0, 2 * c]
    return jnp.minimum(first, 63 - first)


def flip_of(order, s, c):
    return jnp.where(order[s, 0, 2 * c] >= 32, 1, 0)


def turned(v, cosine, sine):
    first, second = v[0:8], v[8:16]
    return jnp.concatenate(
        [first * cosine - second * sine, second * cosine + first * sine, v[16:]], axis=0
    )


def prepare_kernel(
    order, h_all, c_all, wq, wu, s_all, places, freqs, w_out, w_down, b_up,
    qkvd, normed, zpart, pack, small, cs, t_k, t_q, s_q, t_rows, s_rows,
):
    z = lax.axis_index("shard")
    c, y, x, k = spots()
    count = h_all.shape[1]
    lane = lax.broadcasted_iota(jnp.int32, (1, 128), 1)
    left = lane < 64

    def positions(s, low):
        near = places[s, :, pl.ds(pl.multiple_of(lax.div(low, 2) * 128, 128), 128)]
        far = places[s, :, pl.ds(pl.multiple_of((31 - lax.div(low, 2)) * 128, 128), 128)]
        odd = lax.rem(low, 2)
        both = jnp.where(odd > 0, jnp.where(left, far, near), jnp.where(left, near, far))
        return swap(both.astype(F32), odd)

    def tokens(first, second):
        return jnp.where(left, 64 * first + lane, 64 * second - 64 + lane).astype(F32)

    for s in range(4):
        angle = swap(positions(s, low_of(order, s, c)), flip_of(order, s, c)) * freqs[...]
        turns = jnp.floor(angle * (0.5 / math.pi) + 0.5)
        angle = angle - turns * 6.28125
        angle = angle - turns * 1.93500518798828125e-3
        angle = angle - turns * 3.01991598195675e-7
        cs[s, 0:8] = jnp.cos(angle)
        cs[s, 8:16] = jnp.sin(angle)
    for j in range(16):
        at = (j // 2 % 4) * 8 + (j % 2) * 4 + j // 8
        first, second = low_of(order, y, at), low_of(order, y, at + 2)
        t_k[:, 128 * j : 128 * j + 128] = tokens(first, second)
        t_k[:, 2048 + 128 * j : 2176 + 128 * j] = tokens(63 - second, 63 - first)
    for n in range(16):
        low = low_of(order, y, 2 * n + k)
        row = tokens(low, 63 - low)
        t_rows[n : n + 1] = row
        s_rows[n : n + 1] = row - positions(y, low)
    for rows, to in ((t_rows, t_q), (s_rows, s_q)):
        turn = rows[...].T
        for n in range(4):
            cols = [turn[:, 4 * n + m : 4 * n + m + 1] for m in range(4)]
            to[0, n] = jnp.concatenate([col[0:64] for col in cols], axis=0)
            to[1, n] = jnp.concatenate([cols[m][64:128] for m in (1, 0, 3, 2)], axis=0)

    xhat, _ = normalize(h_all[...].reshape(4 * count, D).astype(F32))
    cot = c_all[...].reshape(4 * count, D)
    n1 = (xhat * vector(s_all, 0) + vector(s_all, 1)).astype(BF)
    normed[...] = n1
    bias = []
    for t in range(3):
        piece = jnp.zeros((1, HC), F32)
        for p in range(4):
            n = 4 * t + p
            piece = piece + jnp.where(z == p, s_all[n // 3, 6 + n % 3 : 7 + n % 3], 0.0)
        bias.append(piece)
    joined = dot(n1, wq[...].reshape(D, 3 * HC)) + jnp.concatenate(bias, axis=1)
    d_mixed = dot_nt(w_out[...], cot)
    for s in range(4):
        jt = joined[count * s : count * s + count].T
        cosine, sine = cs[s, 0:8], cs[s, 8:16]
        for h in range(NH):
            at = HD * h
            rows = [
                turned(jt[HC + at : HC + at + HD], cosine, sine),
                jt[2 * HC + at : 2 * HC + at + HD],
                turned(jt[at : at + HD], cosine, sine),
                d_mixed[at : at + HD, count * s : count * s + count],
            ]
            qkvd[s, h] = swap(jnp.concatenate(rows, axis=0), flip_of(order, s, c)).astype(BF)

    n2 = (xhat * vector(s_all, 2) + vector(s_all, 3)).astype(BF)
    up = wu[...].reshape(D, wu.shape[2])
    hidden = dot(n2, up) + b_up[...].astype(F32).reshape(1, b_up.shape[0])
    rise = 0.5 * (1.0 + lax.erf(hidden * (1.0 / math.sqrt(2.0))))
    slope = rise + hidden * jnp.exp(-0.5 * hidden * hidden) * (1.0 / math.sqrt(2.0 * math.pi))
    active = (hidden * rise).astype(BF)
    d_up = (dot_nt(cot, w_down[...]) * slope).astype(BF)
    g_down = dot_tn(active, cot).astype(BF)
    for half in range(2):
        for i in range(3):
            at = 384 * half + 128 * i
            tiles = g_down[:, at : at + 128].reshape(16, 3, 16, 128)
            pack[:, half, 12 + 3 * i : 15 + 3 * i] = tiles
    g_up = dot_tn(n2, d_up).astype(BF)
    pack[12:16, :, 0:12] = jnp.zeros((4, 2, 12, 16, 128), BF)
    for p in range(4):
        for j in range(6):
            tiles = g_up[HC * p : HC * p + HC, 128 * j : 128 * j + 128].reshape(2, 2, 3, 16, 128)
            pack[2 * j : 2 * j + 2, :, 3 * p : 3 * p + 3] = tiles
    branch = dot(active, w_down[...]).astype(BF)
    d_two = dot_nt(d_up, up)
    for s in range(4):
        zpart[s, 0] = branch[count * s : count * s + count]
        zpart[s, 1] = d_two[count * s : count * s + count].astype(BF)
    small[...] = jnp.zeros_like(small)
    small[2:3] = jnp.sum(d_two * xhat, axis=0, keepdims=True)
    small[3:4] = jnp.sum(d_two, axis=0, keepdims=True)
    small[4:5] = jnp.sum(cot.astype(F32), axis=0, keepdims=True)
    small[5:6] = jnp.sum(d_up.astype(F32), axis=0, keepdims=True)


def prepare(order, h_all, c_all, wq, wu, s_all, places, freqs, w_out, w_down, b_up):
    count = h_all.shape[1]
    return pl.pallas_call(
        prepare_kernel,
        out_shape=(
            jax.ShapeDtypeStruct((4, NH, 4 * HD, count), BF),
            jax.ShapeDtypeStruct((4 * count, D), BF),
            jax.ShapeDtypeStruct((4, 2, count, D), BF),
            jax.ShapeDtypeStruct((16, 2, 21, 16, 128), BF),
            jax.ShapeDtypeStruct((8, D), F32),
            jax.ShapeDtypeStruct((4, 16, count), F32),
            jax.ShapeDtypeStruct((1, 4096), F32),
            jax.ShapeDtypeStruct((2, 4, 256, 1), F32),
            jax.ShapeDtypeStruct((2, 4, 256, 1), F32),
        ),
        in_specs=[pl.BlockSpec(memory_space=pltpu.SMEM)] + vmem(10),
        out_specs=tuple(vmem(9)),
        scratch_shapes=[pltpu.VMEM((16, 128), F32), pltpu.VMEM((16, 128), F32)],
        compiler_params=pltpu.CompilerParams(vmem_limit_bytes=LIMIT),
    )(order, h_all, c_all, wq, wu, s_all, places, freqs, w_out, w_down, b_up)


def attend_kernel(
    qkvd, t_k, t_q, s_q, zpart, pack, out, z_all, full,
    kv, qd, kt, dkv, qdt, oqt, s_buf, p_buf, dpart, got, ready,
    w_got, w_one, w_far, w_two, w_beyond, w_three, w_last,
    s_k, r_k, s_d, r_d, s_f, r_f, s_n, r_n, s_o, r_o, s_z, r_z,
    w_sc, w_rc, w_sa, w_ra, w_sb, w_rb, w_sz, w_rz, w_gb, w_hb, w_ga, w_ha, w_gc, w_hc,
):
    z = lax.axis_index("shard")
    c, y, x, k = spots()
    sibling = {"ctx": c + 1 - 2 * k}
    z_peer = [{"shard": lax.rem(z + d, 4)} for d in range(4)]
    a, b, a_peer, b_peer = plane(x, y, k)
    steps = [(dy, dx) for dy in range(4) for dx in range(4) if dy or dx]
    steps.sort(key=lambda s: min(s[0], 4 - s[0]) + min(s[1], 4 - s[1]))
    far_spot, far_peer = {}, {}
    for dy, dx in steps:
        ys, xs = lax.rem(y + dy, 4), lax.rem(x + dx, 4)
        far_spot[dy, dx] = (ys, xs)
        far_peer[dy, dx] = {"ctx": place(ys, xs, k)}
    greet(list(far_peer.values()) + z_peer[1:] + [sibling])
    busy = x < 3
    slot = y * 4 + x
    tail = []

    there = {}
    for dy, dx in steps:
        ys, xs = far_spot[dy, dx]
        n = 4 * dy + dx
        h = lax.rem(xs, 3)
        there[dy, dx] = [
            remote(
                qkvd.at[ys, h, pl.ds(0, 128)], kv.at[k * 16 + slot], s_k.at[n], r_k.at[n],
                far_peer[dy, dx],
            ),
            remote(
                qkvd.at[ys, h, pl.ds(128, 128)], qd.at[slot], s_d.at[n], r_d.at[n],
                far_peer[dy, dx],
            ),
        ]
    for i in range(2):
        for dy, dx in steps:

            @pl.when(far_spot[dy, dx][1] < 3)
            def _():
                there[dy, dx][i].start()

    @pl.when(busy)
    def _():
        kv[k * 16 + slot] = qkvd[y, lax.rem(x, 3), 0:128]
        qd[slot] = qkvd[y, lax.rem(x, 3), 128:]

    w_near, w_across, w_over, w_turn, w_out_b, w_out_a = {}, {}, {}, {}, {}, {}

    def w_core():
        for d in (1, 3, 2, 0):
            ap = lax.rem(b + d, 4)
            w_near[d] = send(pack.at[1 - k, ap], w_got.at[ap], w_sc.at[d], w_rc.at[d], sibling)

    def w_sum_core():
        for d in (1, 3, 2, 0):
            ap = lax.rem(a + d, 4)
            w_near[d].wait_recv()
            w_one[ap] = (pack[k, ap].astype(F32) + w_got[ap].astype(F32)).astype(BF)
            if d:
                w_across[d] = send(
                    w_one.at[ap], w_far.at[d - 1], w_sa.at[d - 1], w_ra.at[d - 1], a_peer[d]
                )

    def w_sum_a():
        for d in (1, 3, 2):
            w_across[d].wait_recv()
        for d in (1, 3, 2, 0):
            bp = lax.rem(b + d, 4)
            total = w_one[a, bp].astype(F32)
            for n in range(3):
                total = total + w_far[n, bp].astype(F32)
            w_two[bp] = total.astype(BF)
            if d:
                w_over[d] = send(
                    w_two.at[bp], w_beyond.at[d - 1], w_sb.at[d - 1], w_rb.at[d - 1], b_peer[d]
                )

    def w_sum_b():
        for d in (1, 3, 2):
            w_over[d].wait_recv()
        total = w_two[b].astype(F32)
        for n in range(3):
            total = total + w_beyond[n].astype(F32)
        w_three[...] = total.astype(BF)
        for d in (1, 3, 2):
            zp = lax.rem(z + d, 4)
            w_turn[d] = send(
                w_three.at[pl.ds(3 * zp, 3)], w_last.at[pl.ds(3 * z, 3)],
                w_sz.at[d - 1], w_rz.at[d - 1], z_peer[d],
            )
        w_last[pl.ds(3 * z, 3)] = w_three[pl.ds(3 * z, 3)]
        w_last[12:] = w_three[12:]

    def w_back_b():
        for d in (1, 3, 2):
            w_turn[d].wait()
        full[k, a, b] = w_last[...]
        for d in (1, 3, 2):
            w_out_b[d] = send(
                w_last, full.at[k, a, b], w_gb.at[d - 1], w_hb.at[d - 1], b_peer[d]
            )

    def w_back_a():
        for d in (1, 3, 2):
            w_out_b[d].wait()
        for d in (1, 3, 2):
            w_out_a[d] = send(
                full.at[k, a], full.at[k, a], w_ga.at[d - 1], w_ha.at[d - 1], a_peer[d]
            )
        tail.append(send(full.at[k, a], full.at[k, a], w_gc.at[0], w_hc.at[0], sibling))

    def w_back_core():
        for d in (1, 3, 2):
            w_out_a[d].wait_recv()
            ap = lax.rem(a + 4 - d, 4)
            tail.append(send(full.at[k, ap], full.at[k, ap], w_gc.at[d], w_hc.at[d], sibling))

    left = lax.broadcasted_iota(jnp.int32, (128, 128), 1) < 64
    mine, others = pl.ds(k * 16, 16), pl.ds((1 - k) * 16, 16)
    forward = remote(kv.at[mine], kv.at[mine], s_f.at[0], r_f.at[0], sibling)

    def sort():
        def step(j, carry):
            one = kv[2 * j].astype(F32)
            two = pltpu.roll(kv[2 * j + 1].astype(F32), 64, 1)
            kt[:, pl.ds(pl.multiple_of(j * 128, 128), 128)] = jnp.where(left, one, two).astype(BF)
            kt[:, pl.ds(pl.multiple_of((16 + j) * 128, 128), 128)] = jnp.where(left, two, one).astype(BF)
            return carry

        lax.fori_loop(0, 16, step, 0)
        dkv[...] = jnp.zeros_like(dkv)

    def queries(n):
        for m in range(2):
            one = qd[4 * n + 2 * m].astype(F32)
            two = pltpu.roll(qd[4 * n + 2 * m + 1].astype(F32), 64, 1)
            cols = slice(128 * m, 128 * m + 128)
            qdt[0, :, cols] = jnp.where(left, one, two)
            qdt[1, :, cols] = jnp.where(left, two, one)

    def answers(n):
        for m in range(2):
            cols = slice(128 * m, 128 * m + 128)
            low, high = oqt[0, :, cols], oqt[1, :, cols]
            ready[1, 4 * n + 2 * m] = jnp.where(left, low, high).astype(BF)
            ready[1, 4 * n + 2 * m + 1] = pltpu.roll(jnp.where(left, high, low), 64, 1).astype(BF)

    def unsort():
        def step(j, carry):
            low = dkv[:, pl.ds(pl.multiple_of(j * 128, 128), 128)]
            high = dkv[:, pl.ds(pl.multiple_of((16 + j) * 128, 128), 128)]
            dpart[2 * j] = jnp.where(left, low, high).astype(BF)
            dpart[2 * j + 1] = pltpu.roll(jnp.where(left, high, low), 64, 1).astype(BF)
            return carry

        lax.fori_loop(0, 16, step, 0)

    keys, values = slice(0, HD), slice(HD, 2 * HD)

    def one_tile(tile, n):
        q_t = qdt[tile, keys, :] * 0.125
        d_t = qdt[tile, values, :]
        q_n, d_n = q_t.T.astype(BF), d_t.T.astype(BF)
        q_t, d_t = q_t.astype(BF), d_t.astype(BF)
        first_key, last_key = s_q[tile, n], t_q[tile, n]
        top = jnp.full((256, 128), -1e30, F32)
        total = jnp.zeros((256, 128), F32)
        inner = jnp.zeros((256, 128), F32)
        for i in range((tile + 1) * 2048 // CHUNK):
            at = slice(i * CHUNK, i * CHUNK + CHUNK)
            s = dot(q_n, kt[keys, at])
            key = t_k[:, at]
            s = jnp.where((key >= first_key) & (key <= last_key), s, -1e30)
            s_buf[:, at] = s
            dp = dot(d_n, kt[values, at])
            p_buf[:, at] = dp
            new = top
            for m in range(CHUNK // 128):
                new = jnp.maximum(new, s[:, 128 * m : 128 * m + 128])
            scale = jnp.exp(top - new)
            total, inner, top = total * scale, inner * scale, new
            for m in range(CHUNK // 128):
                e = jnp.exp(s[:, 128 * m : 128 * m + 128] - new)
                total = total + e
                inner = inner + e * dp[:, 128 * m : 128 * m + 128]
        most = jnp.max(top, axis=1, keepdims=True)
        scale = jnp.exp(top - most)
        over = 1.0 / jnp.sum(total * scale, axis=1, keepdims=True)
        inner = jnp.sum(inner * scale, axis=1, keepdims=True) * over
        out_t = jnp.zeros((HD, 256), F32)
        dq_t = jnp.zeros((HD, 256), F32)
        for i in range((tile + 1) * 2048 // CHUNK):
            at = slice(i * CHUNK, i * CHUNK + CHUNK)
            p = jnp.exp(s_buf[:, at] - most) * over
            pb = p.astype(BF)
            ds = (p * (p_buf[:, at] - inner)).astype(BF)
            out_t = out_t + dot_nt(kt[values, at], pb)
            dq_t = dq_t + dot_nt(kt[keys, at], ds)
            dkv[values, at] += dot(d_t, pb)
            dkv[keys, at] += dot(q_t, ds)
        oqt[tile, keys, :] = out_t
        oqt[tile, values, :] = dq_t * 0.125

    home = {}
    h = lax.rem(x, 3)
    for dy, dx in steps:
        ys, xs = far_spot[dy, dx]
        n = 4 * dy + dx
        home[dy, dx] = [
            remote(
                ready.at[i, 4 * ys + xs], out.at[y, h, pl.ds(128 * i, 128)],
                s_o.at[i, n], r_o.at[i, n], far_peer[dy, dx],
            )
            for i in range(2)
        ]

    w_core()
    for d in (1, 3, 2):
        zp = lax.rem(z + d, 4)
        tail.append(send(zpart.at[zp], z_all.at[z], s_z.at[d - 1], r_z.at[d - 1], z_peer[d]))
    z_all[z] = zpart[z]

    @pl.when(busy)
    def _():
        for dy, dx in steps:
            there[dy, dx][0].wait_recv()
        forward.start()

    w_sum_core()

    @pl.when(busy)
    def _():
        for dy, dx in steps:
            there[dy, dx][1].wait_recv()
        forward.wait()
        sort()

    def nothing():
        pass

    points = (
        (nothing, w_sum_a), (nothing, w_sum_b), (w_back_b, w_back_a), (nothing, nothing)
    )
    for n in range(4):

        @pl.when(busy)
        def _():
            queries(n)
            one_tile(0, n)

        points[n][0]()

        @pl.when(busy)
        def _():
            one_tile(1, n)
            answers(n)

        points[n][1]()

    swap_out = remote(dpart.at[others], got, s_n.at[0], r_n.at[0], sibling)

    @pl.when(busy)
    def _():
        unsort()
        swap_out.start()
        for dy, dx in steps:
            home[dy, dx][1].start()
        out[y, h, 128:] = ready[1, slot]
        swap_out.wait()
        for i in range(4):
            own = dpart[pl.ds(k * 16 + 4 * i, 4)].astype(F32)
            ready[0, 4 * i : 4 * i + 4] = (own + got[4 * i : 4 * i + 4].astype(F32)).astype(BF)
        for dy, dx in steps:
            home[dy, dx][0].start()
        out[y, h, 0:128] = ready[0, slot]

    w_back_core()
    for dy, dx in steps:
        @pl.when(lax.rem(x + 4 - dx, 4) < 3)
        def _():
            for i in range(2):
                home[dy, dx][i].wait_recv()

        @pl.when(far_spot[dy, dx][1] < 3)
        def _():
            for i in range(2):
                there[dy, dx][i].wait_send()

    @pl.when(busy)
    def _():
        for dy, dx in steps:
            for i in range(2):
                home[dy, dx][i].wait_send()

    for copy in tail:
        copy.wait()
    for group in (w_near, w_across, w_over, w_out_a):
        for copy in group.values():
            copy.wait_send()


def attend(qkvd, t_k, t_q, s_q, zpart, pack):
    square = (128, 128)
    tiles = pack.shape[3:]
    return pl.pallas_call(
        attend_kernel,
        out_shape=(
            jax.ShapeDtypeStruct(qkvd.shape, BF),
            jax.ShapeDtypeStruct(zpart.shape, BF),
            jax.ShapeDtypeStruct(pack.shape, BF),
        ),
        in_specs=vmem(6),
        out_specs=tuple(vmem(3)),
        scratch_shapes=[
            pltpu.VMEM((32,) + square, BF),
            pltpu.VMEM((16,) + square, BF),
            pltpu.VMEM((128, 4096), BF),
            pltpu.VMEM((128, 4096), F32),
            pltpu.VMEM((2, 128, 256), F32),
            pltpu.VMEM((2, 128, 256), F32),
            pltpu.VMEM((256, 4096), F32),
            pltpu.VMEM((256, 4096), F32),
            pltpu.VMEM((32,) + square, BF),
            pltpu.VMEM((16,) + square, BF),
            pltpu.VMEM((2, 16) + square, BF),
            pltpu.VMEM((4, 4) + tiles, BF),
            pltpu.VMEM((4, 4) + tiles, BF),
            pltpu.VMEM((3, 4) + tiles, BF),
            pltpu.VMEM((4,) + tiles, BF),
            pltpu.VMEM((3,) + tiles, BF),
            pltpu.VMEM(tiles, BF),
            pltpu.VMEM(tiles, BF),
            dma(16), dma(16), dma(16), dma(16), dma(1), dma(1), dma(1), dma(1),
            dma(2, 16), dma(2, 16), dma(3), dma(3),
            dma(4), dma(4), dma(3), dma(3), dma(3), dma(3), dma(3), dma(3),
            dma(3), dma(3), dma(3), dma(3), dma(4), dma(4),
        ],
        compiler_params=params(1),
    )(qkvd, t_k, t_q, s_q, zpart, pack)


def sum_kernel(
    pack, zpart, small, full, z_all, small_all,
    got, one, far_a, two, far_b, three, last, s1, s2, s3, s4,
    sz, rz, sc, rc, sa, ra, sb, rb, st, rt, gb, hb, ga, ha, gc, hc, sm, rm,
):
    z = lax.axis_index("shard")
    c, y, x, k = spots()
    sibling = {"ctx": c + 1 - 2 * k}
    z_peer = [{"shard": lax.rem(z + d, 4)} for d in range(4)]
    a, b, a_peer, b_peer = plane(x, y, k)
    greet(a_peer[1:] + b_peer[1:] + z_peer[1:] + [sibling])
    near = {}
    for d in (1, 3, 2, 0):
        ap = lax.rem(b + d, 4)
        near[d] = send(pack.at[1 - k, ap], got.at[ap], sc.at[d], rc.at[d], sibling)
    tail = [send(small, s1, sm.at[0], rm.at[0], sibling)]
    for d in (1, 3, 2):
        zp = lax.rem(z + d, 4)
        tail.append(send(zpart.at[zp], z_all.at[z], sz.at[d - 1], rz.at[d - 1], z_peer[d]))
    z_all[z] = zpart[z]
    across = {}
    for d in (1, 3, 2, 0):
        ap = lax.rem(a + d, 4)
        near[d].wait_recv()
        for n in range(4):
            both = pack[k, ap, n].astype(F32) + got[ap, n].astype(F32)
            one[ap, n] = both.astype(BF)
        if d:
            across[d] = send(one.at[ap], far_a.at[d - 1], sa.at[d - 1], ra.at[d - 1], a_peer[d])
    tail[0].wait()
    s2[0] = small[...] + s1[...]
    small_a = [send(s2.at[0], s2.at[d], sm.at[d], rm.at[d], a_peer[d]) for d in (1, 2, 3)]
    for d in (1, 3, 2):
        across[d].wait_recv()
    beyond = {}
    for d in (1, 3, 2, 0):
        bp = lax.rem(b + d, 4)
        total = one[a, bp].astype(F32)
        for n in range(3):
            total = total + far_a[n, bp].astype(F32)
        two[bp] = total.astype(BF)
        if d:
            beyond[d] = send(two.at[bp], far_b.at[d - 1], sb.at[d - 1], rb.at[d - 1], b_peer[d])
    for copy in small_a:
        copy.wait()
    s3[0] = (s2[0] + s2[1]) + (s2[2] + s2[3])
    small_b = [send(s3.at[0], s3.at[d], sm.at[3 + d], rm.at[3 + d], b_peer[d]) for d in (1, 2, 3)]
    for d in (1, 3, 2):
        beyond[d].wait_recv()
    total = two[b].astype(F32)
    for n in range(3):
        total = total + far_b[n].astype(F32)
    three[...] = total.astype(BF)
    turned = []
    for d in (1, 3, 2):
        zp = lax.rem(z + d, 4)
        turned.append(
            send(
                three.at[pl.ds(2 * zp, 2)], last.at[pl.ds(2 * z, 2)],
                st.at[d - 1], rt.at[d - 1], z_peer[d],
            )
        )
    last[pl.ds(2 * z, 2)] = three[pl.ds(2 * z, 2)]
    last[8:] = three[8:]
    for copy in small_b:
        copy.wait()
    s4[...] = (s3[0] + s3[1]) + (s3[2] + s3[3])
    for d in (1, 3, 2):
        tail.append(send(s4, small_all.at[z], sm.at[6 + d], rm.at[6 + d], z_peer[d]))
    small_all[z] = s4[...]
    for copy in turned:
        copy.wait()
    full[k, a, b] = last[...]
    out_b = {}
    for d in (1, 3, 2):
        out_b[d] = send(last, full.at[k, a, b], gb.at[d - 1], hb.at[d - 1], b_peer[d])
    for d in (1, 3, 2):
        out_b[d].wait()
    out_a = {}
    for d in (1, 3, 2):
        out_a[d] = send(full.at[k, a], full.at[k, a], ga.at[d - 1], ha.at[d - 1], a_peer[d])
    tail.append(send(full.at[k, a], full.at[k, a], gc.at[0], hc.at[0], sibling))
    for d in (1, 3, 2):
        out_a[d].wait_recv()
        ap = lax.rem(a + 4 - d, 4)
        tail.append(send(full.at[k, ap], full.at[k, ap], gc.at[d], hc.at[d], sibling))
    for copy in tail[1:]:
        copy.wait()
    for d in (1, 2, 3):
        out_a[d].wait_send()
        across[d].wait_send()
        beyond[d].wait_send()
    for d in range(4):
        near[d].wait_send()


def sums(pack, zpart, small):
    tiles = pack.shape[3:]
    return pl.pallas_call(
        sum_kernel,
        out_shape=(
            jax.ShapeDtypeStruct(pack.shape, BF),
            jax.ShapeDtypeStruct(zpart.shape, BF),
            jax.ShapeDtypeStruct((4,) + small.shape, F32),
        ),
        in_specs=vmem(3),
        out_specs=tuple(vmem(3)),
        scratch_shapes=[
            pltpu.VMEM((4, 4) + tiles, BF),
            pltpu.VMEM((4, 4) + tiles, BF),
            pltpu.VMEM((3, 4) + tiles, BF),
            pltpu.VMEM((4,) + tiles, BF),
            pltpu.VMEM((3,) + tiles, BF),
            pltpu.VMEM(tiles, BF),
            pltpu.VMEM(tiles, BF),
            pltpu.VMEM(small.shape, F32),
            pltpu.VMEM((4,) + small.shape, F32),
            pltpu.VMEM((4,) + small.shape, F32),
            pltpu.VMEM(small.shape, F32),
            dma(3), dma(3), dma(4), dma(4), dma(3), dma(3), dma(3), dma(3), dma(3), dma(3),
            dma(3), dma(3), dma(3), dma(3), dma(4), dma(4), dma(10), dma(10),
        ],
        compiler_params=params(3),
    )(pack, zpart, small)


def after_kernel(order, ret, h_all, c_all, normed, wq, w_out, cs, given, zpart, pack, small, dj, mt):
    count = h_all.shape[1]
    for s in range(4):
        cosine, sine = cs[s, 0:8], -cs[s, 8:16]
        flip = flip_of(order, s, lax.axis_index("ctx"))
        r = [swap(ret[s, h].astype(F32), flip) for h in range(NH)]
        rows = [turned(r[h][3 * HD :], cosine, sine) for h in range(NH)]
        rows += [turned(r[h][0:HD], cosine, sine) for h in range(NH)]
        rows += [r[h][HD : 2 * HD] for h in range(NH)]
        dj[count * s : count * s + count] = jnp.concatenate(rows, axis=0).T.astype(BF)
        for h in range(NH):
            mt[HD * h : HD * h + HD, count * s : count * s + count] = r[h][2 * HD : 3 * HD].astype(BF)
    cot = c_all[...].reshape(4 * count, D)
    xhat, _ = normalize(h_all[...].reshape(4 * count, D).astype(F32))
    d_one = dot_nt(dj[...], wq[...].reshape(D, 3 * HC))
    branch = dot(mt[...].astype(F32).T.astype(BF), w_out[...])
    for s in range(4):
        zpart[s, 0] = branch[count * s : count * s + count].astype(BF)
        zpart[s, 1] = d_one[count * s : count * s + count].astype(BF)
    small[...] = given[...]
    small[0:1] = jnp.sum(d_one * xhat, axis=0, keepdims=True)
    small[1:2] = jnp.sum(d_one, axis=0, keepdims=True)
    small[6:7, 0 : 3 * HC] = jnp.sum(dj[...].astype(F32), axis=0, keepdims=True)
    pack[24:32] = jnp.zeros((8,) + pack.shape[1:], BF)
    g = dot_tn(normed[...], dj[...])
    for p in range(4):
        mine = g[HC * p : HC * p + HC]
        for j in range(4):
            tiles = mine[:, 128 * j : 128 * j + 128].astype(BF).reshape(6, 2, 16, 128)
            pack[6 * j : 6 * j + 6, 2 * p : 2 * p + 2] = tiles
        rest = jnp.concatenate([mine[: HC // 2, 512:], mine[HC // 2 :, 512:]], axis=1)
        pack[24:27, 2 * p : 2 * p + 2] = rest.astype(BF).reshape(3, 2, 16, 128)
    g = dot(mt[...], cot)
    for j in range(6):
        tiles = g[:, 128 * j : 128 * j + 128].astype(BF).reshape(4, 3, 16, 128)
        pack[4 * j : 4 * j + 4, 8:11] = tiles


def after(order, ret, h_all, c_all, normed, wq, w_out, cs, given):
    count = h_all.shape[1]
    return pl.pallas_call(
        after_kernel,
        out_shape=(
            jax.ShapeDtypeStruct((4, 2, count, D), BF),
            jax.ShapeDtypeStruct((32, 11, 16, 128), BF),
            jax.ShapeDtypeStruct((8, D), F32),
        ),
        in_specs=[pl.BlockSpec(memory_space=pltpu.SMEM)] + vmem(8),
        out_specs=tuple(vmem(3)),
        scratch_shapes=[pltpu.VMEM((4 * count, 3 * HC), BF), pltpu.VMEM((HC, 4 * count), BF)],
        compiler_params=pltpu.CompilerParams(vmem_limit_bytes=LIMIT),
    )(order, ret, h_all, c_all, normed, wq, w_out, cs, given)


def finish_kernel(
    hid, cot, z_one, z_two, s_all, full, small_all, feed,
    out, grad, g_qkv, g_out, g_up, g_down, one_g, one_b, two_g, two_b, g_bqkv, g_bout, g_bup,
):
    z = lax.axis_index("shard")
    branch, d_one, d_two = 0.0, 0.0, 0.0
    for p in range(4):
        branch = branch + (z_one[p, 0].astype(F32) + z_two[p, 0].astype(F32))
        d_one = d_one + z_one[p, 1].astype(F32)
        d_two = d_two + z_two[p, 1].astype(F32)
    flat = hid[...].astype(F32)
    xhat, r = normalize(flat)
    out[...] = (flat + branch + vector(s_all, 4) + vector(s_all, 5)).astype(BF)
    g = d_one * vector(s_all, 0) + d_two * vector(s_all, 2)
    inner = jnp.mean(g * xhat, axis=-1, keepdims=True)
    grad[...] = cot[...].astype(F32) + r * (g - jnp.mean(g, axis=-1, keepdims=True) - xhat * inner)
    planes = []
    for p in range(4):
        cols = [full[6 * j : 6 * j + 6, 2 * p : 2 * p + 2].reshape(HC, 128) for j in range(4)]
        rest = full[24:27, 2 * p : 2 * p + 2].reshape(HC // 2, 128).astype(F32)
        rest = jnp.concatenate([rest[:, :64], rest[:, 64:]], axis=0)
        planes.append(jnp.concatenate([col.astype(F32) for col in cols] + [rest], axis=1))
    for t in range(3):
        g_qkv[:, D * t : D * t + D] = jnp.concatenate(
            [plane[:, HC * t : HC * t + HC] for plane in planes], axis=1
        )
    for j in range(6):
        tiles = full[4 * j : 4 * j + 4, 8:11].reshape(HC, 128)
        g_out[:, 128 * j : 128 * j + 128] = tiles.astype(F32)
    total = (small_all[0] + small_all[1]) + (small_all[2] + small_all[3])
    own = small_all[z]
    rows = jnp.concatenate([total[0:4], own[4:5]], axis=0)
    piece = jnp.zeros((5, HC), F32)
    for p in range(4):
        piece = piece + jnp.where(z == p, rows[:, HC * p : HC * p + HC], 0.0)
    for i, ref in enumerate((one_g, one_b, two_g, two_b, g_bout)):
        ref[...] = piece[i : i + 1].reshape(HC)
    pieces = []
    for i in range(3):
        piece = jnp.zeros((1, HC), F32)
        for p in range(4):
            n = 3 * p + i
            at = HC * (n // 4)
            piece = piece + jnp.where(z == p, small_all[n % 4, 6:7, at : at + HC], 0.0)
        pieces.append(piece)
    g_bqkv[...] = jnp.concatenate(pieces, axis=1).reshape(3 * HC)
    g_bup[...] = own[5:6].reshape(g_bup.shape)
    for half in range(2):
        for i in range(3):
            tiles = feed[:, half, 12 + 3 * i : 15 + 3 * i].reshape(D, 128)
            at = 384 * half + 128 * i
            g_down[:, at : at + 128] = tiles.astype(F32)
    for p in range(4):
        for j in range(6):
            tiles = feed[2 * j : 2 * j + 2, :, 3 * p : 3 * p + 3].reshape(HC, 128)
            g_up[:, D * p + 128 * j : D * p + 128 * j + 128] = tiles.astype(F32)


def finish(hid, cot, z_one, z_two, s_all, full, small_all, feed):
    return pl.pallas_call(
        finish_kernel,
        out_shape=(
            jax.ShapeDtypeStruct(hid.shape, BF),
            jax.ShapeDtypeStruct(hid.shape, F32),
            jax.ShapeDtypeStruct((HC, 3 * D), F32),
            jax.ShapeDtypeStruct((HC, D), F32),
            jax.ShapeDtypeStruct((HC, 4 * D), F32),
            jax.ShapeDtypeStruct((D, D), F32),
            jax.ShapeDtypeStruct((HC,), F32),
            jax.ShapeDtypeStruct((HC,), F32),
            jax.ShapeDtypeStruct((HC,), F32),
            jax.ShapeDtypeStruct((HC,), F32),
            jax.ShapeDtypeStruct((3 * HC,), F32),
            jax.ShapeDtypeStruct((HC,), F32),
            jax.ShapeDtypeStruct((D,), F32),
        ),
        in_specs=vmem(8),
        out_specs=tuple(vmem(13)),
        compiler_params=pltpu.CompilerParams(vmem_limit_bytes=LIMIT),
    )(hid, cot, z_one, z_two, s_all, full, small_all, feed)


def local(
    hidden, ln1_gain, ln1_bias, ln2_gain, ln2_bias, w_qkv, b_qkv, w_out, b_out, w_up, b_up,
    w_down, b_down, block_order, positions, cotangent,
):
    vectors = (ln1_gain, ln1_bias, ln2_gain, ln2_bias, b_out, b_down, b_qkv)
    h_all, c_all, wq, wu, s_all, p_all, o_all = spread(
        hidden, cotangent, w_qkv, w_up, vectors, positions, block_order
    )

    freqs = jnp.power(10000.0, -jnp.arange(0, ROT, 2, dtype=F32) / ROT).reshape(8, 1)
    qkvd, normed, zpart_two, feed_pack, small, cs, t_k, t_q, s_q = prepare(
        o_all, h_all, c_all, wq, wu, s_all, p_all, freqs, w_out, w_down, b_up
    )
    returned, z_two, feed = attend(
        qkvd, t_k, t_q, s_q, zpart_two, feed_pack.reshape(2, 4, 4, 21, 16, 128)
    )
    zpart_one, pack, small = after(o_all, returned, h_all, c_all, normed, wq, w_out, cs, small)
    full, z_one, small_all = sums(pack.reshape(2, 4, 4, 11, 16, 128), zpart_one, small)
    (
        output, grad_input, grad_qkv, grad_out, grad_up, grad_down, one_g, one_b, two_g, two_b,
        grad_bqkv, grad_bout, grad_bup,
    ) = finish(
        hidden, cotangent, z_one, z_two, s_all, full.reshape(32, 11, 16, 128), small_all,
        feed.reshape(16, 2, 21, 16, 128),
    )
    return (
        output, grad_input, one_g, one_b, two_g, two_b, grad_qkv, grad_bqkv, grad_out, grad_bout,
        grad_up, grad_bup, grad_down, grad_bout,
    )


def solution(mesh):
    tokens, vector, matrix = P(("shard", "ctx"), None), P("shard"), P("shard", None)
    return jax.shard_map(
        local,
        mesh=mesh,
        in_specs=(
            tokens, vector, vector, vector, vector, matrix, vector, matrix, vector, matrix, vector,
            matrix, vector, matrix, matrix, tokens,
        ),
        out_specs=(
            tokens, tokens, vector, vector, vector, vector, matrix, vector, matrix, vector, matrix,
            vector, matrix, vector,
        ),
        check_vma=False,
    )
```
